32 devices in a mesh: pipe: 4 (over z), expert: 8 (over y, x, core).
Axes of the slice: x: 2, y: 2, z: 4, core: 2. Of those that a mesh axis runs over, the one named last changes fastest.
Arguments:
- up_state: bfloat16 [4, 128, 3584], P('pipe', 'expert'), may hold values from -6 to 6
- down_state: bfloat16 [4, 128, 3584], P('pipe', 'expert'), may hold values from -6 to 6
- entering_up: bfloat16 [128, 3584], P('expert'), may hold values from -6 to 6
- entering_down: bfloat16 [128, 3584], P('expert'), may hold values from -6 to 6
- up_route: int32 [2, 4, 128, 1], P(None, 'pipe', 'expert'), may hold values from 0 to 7; in each aligned block of 16 rows (0 to 15, 16 to 31, ..., all dimensions but the last counted through in order) at most 2 rows name the same one
- down_route: int32 [2, 4, 128, 1], P(None, 'pipe', 'expert'), may hold values from 0 to 7; in each aligned block of 16 rows (0 to 15, 16 to 31, ..., all dimensions but the last counted through in order) at most 2 rows name the same one
- norm_gain: float32 [4, 3584], P('pipe'), may hold values from 0.5 to 1.5
- router: bfloat16 [4, 3584, 8], P('pipe'), may hold values from -0.09375 to 0.09375
- w_gate: bfloat16 [4, 3584, 8192], P('pipe', None, 'expert'), may hold values from -0.09375 to 0.09375
- w_up: bfloat16 [4, 3584, 8192], P('pipe', None, 'expert'), may hold values from -0.09375 to 0.09375
- w_down: bfloat16 [4, 8192, 3584], P('pipe', 'expert'), may hold values from -0.1875 to 0.1875
Outputs:
- up_out: bfloat16 [4, 128, 3584], P('pipe', 'expert')
- down_out: bfloat16 [4, 128, 3584], P('pipe', 'expert')
The draws below stay inside these ranges and needn't reach their ends.
Inputs may be any that keep to these rules, and one draw needn't show every extreme that they name: `up_route`: each row names one expert. Within each aligned block of 16 rows (the rows of one device) every expert is named by exactly 2 rows. `down_route`: as for up_route.
All inputs are finite; a program needn't handle non-finite values.
Results may differ from the reference program's by a relative error of at most 0.0057.
Values may be sent and summed in bfloat16 or wider, within the bound.
No kernel may reach another device: no remote copies, remote signals or barrier semaphores. Data moves between devices by JAX's collectives and lax.ppermute only.
A program may use at most 64 MiB of HBM per device.

```python
import math
import jax
import jax.numpy as jnp
import numpy as np
from jax import lax

D = 3584
FFE = 1024
TOP = 1
TICKS = 2
ROWS = 16
GROUP = 1
EXPERTS = 8
CAP = 2
HID = 1024
SECTIONS = 4
RT = 128
N_EXPERT = 8


def level_of(key, extent, cuts, smallest, high):
    factor_of, own = 1.0, jax.random.fold_in(key, 6)
    for dim, shards_of in cuts:
        steps = jnp.exp(jax.random.uniform(jax.random.fold_in(own, dim), (shards_of,), jnp.float32, smallest / len(cuts), high / len(cuts)))
        factor_of = factor_of * jnp.repeat(steps, extent[dim] // shards_of).reshape([-1 if axis == dim else 1 for axis in range(len(extent))])
    return factor_of


def routed_block(stream_key, own, number, rows, count, top, reach, lean):
    order = jax.random.permutation(stream_key, count)
    crowded, ordinary = load_shares(count, rows * top, reach, lean, True), load_shares(count, rows * top, reach, lean, False)
    places = jnp.arange(count)

    def named(lengths, rotation):
        used = int((lengths > 0).sum())
        fixed = max(1, used // 4)
        shifted = fixed + (places - fixed + rotation * (used - fixed)) % max(1, count - fixed)
        return jnp.zeros((count,), jnp.int32).at[order[jnp.where(places < fixed, places, shifted)]].set(jnp.asarray(lengths, jnp.int32))

    lengths = jnp.where(number % 4 == 0, named(crowded, number // 4), named(ordinary, number - number // 4 - 1))
    mixed = jax.random.permutation(jax.random.fold_in(own, 3), count)
    source_of, sink = mixed[0:count // 2 * 2:2], mixed[1:count // 2 * 2:2]
    room = jnp.minimum(lengths[source_of] - 1, reach - lengths[sink]) // 2
    room = jnp.where((source_of == order[0]) | (sink == order[0]) | (lengths[sink] == 0), 0, jnp.maximum(room, 0))
    shifted = jax.random.randint(jax.random.fold_in(own, 4), (count // 2,), 0, 1 << 20) % (room + 1)
    lengths = lengths.at[source_of].add(-shifted).at[sink].add(shifted)
    members = jnp.searchsorted(jnp.cumsum(lengths), jnp.arange(rows * top), side="right").astype(jnp.int32)
    table = members.reshape(top, rows).T
    table = table[jax.random.permutation(jax.random.fold_in(own, 1), rows)]
    rotation = jax.random.randint(jax.random.fold_in(own, 2), (rows, 1), 0, top)
    return jnp.take_along_axis(table, (jnp.arange(top)[None, :] + rotation) % top, axis=1)


def load_shares(amount, total, bound, skew, full):
    loads = [(1 << 20) // math.isqrt(rank ** skew) + 1 for rank in range(1, amount + 1)]
    largest = bound if full else min(bound, max(-(-total // amount), total * loads[0] // sum(loads)))
    least = 1 if total - largest >= amount - 1 else 0
    holding, spare = [largest] + [least] * (amount - 1), total - largest - least * (amount - 1)
    while spare > 0:
        movable = [i for i in range(1, amount) if holding[i] < largest] or [i for i in range(1, amount) if holding[i] < bound]
        mass, remaining = sum([loads[i] for i in movable]), spare
        for i in movable:
            addition = min(bound - holding[i], max(1, remaining * loads[i] // mass), spare)
            holding[i] = holding[i] + addition
            spare = spare - addition
    return np.array(holding)


def gaussian(key, extent, scale, limit, shards=(), held_as=jnp.bfloat16):
    factor_of = level_of(key, extent, shards, -0.22, 0.18) if shards else 1.0
    drawn = jax.random.normal(key, extent, jnp.float32) * scale * factor_of
    return jnp.minimum(jnp.maximum(drawn, -limit), limit).astype(held_as)


def setup_inputs(seed: int = 0) -> dict:
    key_list = jax.random.split(jax.random.key(seed), 12)
    up_state = gaussian(key_list[0], (SECTIONS, RT, D), 1.0, 6.0, ((0, 4), (1, 8)))
    down_state = gaussian(key_list[1], (SECTIONS, RT, D), 1.0, 6.0, ((0, 4), (1, 8)))
    entering_up = gaussian(key_list[2], (RT, D), 1.0, 6.0, ((0, 8),))
    entering_down = gaussian(key_list[3], (RT, D), 1.0, 6.0, ((0, 8),))
    up_route_keys = jax.random.split(jax.random.fold_in(key_list[4], 1), TICKS * SECTIONS * RT // ROWS)
    up_route_turns = jax.random.permutation(jax.random.fold_in(key_list[4], 3), TICKS * SECTIONS * RT // ROWS)
    up_route = jax.vmap(lambda own, number: routed_block(jax.random.fold_in(key_list[4], 2), own, number, ROWS, EXPERTS, TOP, CAP, 0))(up_route_keys, up_route_turns).reshape((TICKS, SECTIONS, RT, TOP))
    down_route_keys = jax.random.split(jax.random.fold_in(key_list[5], 1), TICKS * SECTIONS * RT // ROWS)
    down_route_turns = jax.random.permutation(jax.random.fold_in(key_list[5], 3), TICKS * SECTIONS * RT // ROWS)
    down_route = jax.vmap(lambda own, number: routed_block(jax.random.fold_in(key_list[5], 2), own, number, ROWS, EXPERTS, TOP, CAP, 0))(down_route_keys, down_route_turns).reshape((TICKS, SECTIONS, RT, TOP))
    norm_gain = jnp.clip(1.0 + 0.1 * jax.random.normal(key_list[6], (SECTIONS, D), jnp.float32), 0.5, 1.5)
    router = gaussian(key_list[7], (SECTIONS, D, EXPERTS), D ** -0.5, 0.09375, ((0, 4),))
    w_gate = gaussian(key_list[8], (SECTIONS, D, EXPERTS * FFE), D ** -0.5, 0.09375, ((0, 4), (2, 8)))
    w_up = gaussian(key_list[9], (SECTIONS, D, EXPERTS * FFE), D ** -0.5, 0.09375, ((0, 4), (2, 8)))
    w_down = gaussian(key_list[10], (SECTIONS, EXPERTS * FFE, D), FFE ** -0.5, 0.1875, ((0, 4), (1, 8)))
    return {"up_state": up_state, "down_state": down_state, "entering_up": entering_up, "entering_down": entering_down, "up_route": up_route, "down_route": down_route, "norm_gain": norm_gain, "router": router, "w_gate": w_gate, "w_up": w_up, "w_down": w_down}


norm_eps = 1e-06

def slot_table(routing):
    blocks = routing.reshape(N_EXPERT, ROWS * TOP)
    onehot = (blocks[:, :, None] == jnp.arange(EXPERTS, dtype=jnp.int32)[None, None, :]).astype(jnp.int32)
    before = jnp.cumsum(onehot, axis=1) - onehot
    slot_ids = lax.optimization_barrier(jnp.sum(before * onehot, axis=2))
    owner_base = jnp.arange(N_EXPERT, dtype=jnp.int32)[:, None] * CAP
    return (slot_ids + owner_base).reshape(RT, TOP).astype(jnp.int32)

def section(token_rows, routing, gain_row, router_cols, gate_cols, up_cols, down_rows):
    widened = token_rows.astype(jnp.float32)
    inverse = lax.rsqrt(lax.optimization_barrier(jnp.mean(widened * widened, axis=1, keepdims=True)) + norm_eps)
    normed = (widened * inverse * gain_row.astype(jnp.float32)).astype(jnp.bfloat16)
    logits = jnp.dot(normed, router_cols, preferred_element_type=jnp.float32)
    affinity = jax.nn.sigmoid(logits)
    weights = jnp.take_along_axis(affinity, routing, axis=1)
    position = slot_table(routing)
    buffer = jnp.zeros((EXPERTS, N_EXPERT * CAP, D), jnp.bfloat16)
    buffer = buffer.at[routing, position].set(jnp.broadcast_to(normed[:, None, :], (RT, TOP, D)))

    def one_expert(expert_id):
        inputs = buffer[expert_id]
        gate_part = lax.dynamic_slice_in_dim(gate_cols, expert_id * FFE, FFE, 1)
        up_part = lax.dynamic_slice_in_dim(up_cols, expert_id * FFE, FFE, 1)
        down_part = lax.dynamic_slice_in_dim(down_rows, expert_id * FFE, FFE, 0)
        gate_pre = jnp.dot(inputs, gate_part, preferred_element_type=jnp.float32)
        up_pre = jnp.dot(inputs, up_part, preferred_element_type=jnp.float32)
        hidden = (jax.nn.silu(gate_pre) * up_pre).astype(jnp.bfloat16)
        summed = jnp.zeros((N_EXPERT * CAP, D), jnp.float32)
        for shard_id in range(GROUP):
            partial_value = jnp.dot(hidden[:, shard_id * HID:(shard_id + 1) * HID], down_part[shard_id * HID:(shard_id + 1) * HID], preferred_element_type=jnp.float32).astype(jnp.bfloat16)
            summed = summed + lax.optimization_barrier(partial_value).astype(jnp.float32)
        return summed
    outputs = lax.map(one_expert, jnp.arange(EXPERTS, dtype=jnp.int32))
    gathered = outputs[routing, position]
    mixed_rows = widened + lax.optimization_barrier(jnp.sum(weights[:, :, None] * gathered, axis=1))
    return mixed_rows.astype(jnp.bfloat16)

def reference(up_state, down_state, entering_up, entering_down, up_route, down_route, norm_gain, router, w_gate, w_up, w_down):

    def apply_section(packed):
        return section(*packed)

    def apply_all(states, routings):
        return lax.map(apply_section, (states, routings, norm_gain, router, w_gate, w_up, w_down))
    up_now = up_state
    down_now = down_state
    up_done = up_state
    down_done = down_state
    for tick_id in range(TICKS):
        up_done = apply_all(up_now, up_route[tick_id])
        down_done = apply_all(down_now, down_route[tick_id])
        if tick_id + 1 < TICKS:
            up_now = jnp.concatenate([entering_up[None], up_done[:-1]], axis=0)
            down_now = jnp.concatenate([down_done[1:], entering_down[None]], axis=0)
    return (up_done, down_done)
```

```python
import functools

import jax
import jax.numpy as jnp
from jax import lax
from jax.experimental import pallas as pl
from jax.experimental.pallas import tpu as pltpu
from jax.sharding import PartitionSpec as P

TOP = 1
TICKS = 2
EXPERTS = 8
LANES = 128
SUBLANES = 16


norm_eps = 1e-06


def shifted(value, axis, by):
    length = lax.axis_size(axis)
    pairs = [(i, i + by) for i in range(length) if 0 <= i + by < length]
    return lax.ppermute(value, axis, pairs)


def normalize(token_rows, gain_row):
    widened = token_rows.astype(jnp.float32)
    inverse = lax.rsqrt(jnp.mean(widened * widened, axis=1, keepdims=True) + norm_eps)
    return (widened * inverse * gain_row).astype(jnp.bfloat16)


def routing_tables(normed, routing, router_cols, expert_count, slot_cap):
    logits = jnp.dot(normed, router_cols, preferred_element_type=jnp.float32)
    affinity = jax.nn.sigmoid(logits)
    weights = jnp.take_along_axis(affinity, routing, axis=1)
    flat_ids = routing.reshape(-1)
    onehot = (flat_ids[:, None] == jnp.arange(expert_count, dtype=jnp.int32)[None, :]).astype(
        jnp.int32
    )
    before = jnp.cumsum(onehot, axis=0) - onehot
    slot_ids = jnp.sum(before * onehot, axis=1).reshape(routing.shape)
    expert_hit = (
        routing[:, :, None] == jnp.arange(expert_count, dtype=jnp.int32)[None, None, :]
    ).astype(jnp.float32)
    slot_hit = (
        slot_ids[:, :, None] == jnp.arange(slot_cap, dtype=jnp.int32)[None, None, :]
    ).astype(jnp.float32)
    scatter_map = jnp.einsum("rke,rkc->ecr", expert_hit, slot_hit).astype(jnp.bfloat16)
    flat_slot = routing * slot_cap + slot_ids
    return (scatter_map, weights, flat_slot)


def run_experts(received, gate_cols, up_cols, down_rows):
    sources, slot_count, features = received.shape
    flat_rows = received.reshape(sources * slot_count, features)
    gate_pre = jnp.dot(flat_rows, gate_cols, preferred_element_type=jnp.float32)
    up_pre = jnp.dot(flat_rows, up_cols, preferred_element_type=jnp.float32)
    hidden = (jax.nn.silu(gate_pre) * up_pre).astype(jnp.bfloat16)
    partial_value = jnp.dot(hidden, down_rows, preferred_element_type=jnp.float32).astype(
        jnp.bfloat16
    )
    partial_value = partial_value.reshape(sources, slot_count, features)
    return lax.all_to_all(partial_value, "expert", split_axis=0, concat_axis=0, tiled=True)


def mix_rows(token_rows, weights, flat_slot, outputs):
    picked = outputs[flat_slot]
    return token_rows.astype(jnp.float32) + jnp.sum(weights[:, :, None] * picked, axis=1)


def grouped_shards(
    up_state,
    down_state,
    entering_up,
    entering_down,
    up_route,
    down_route,
    norm_gain,
    router,
    w_gate,
    w_up,
    w_down,
):
    gate_cols = w_gate[0]
    up_cols = w_up[0]
    down_rows = w_down[0]
    gain_row = norm_gain[0]
    router_cols = router[0]
    group_size = max(1, lax.axis_size("expert") // EXPERTS)
    expert_count = lax.axis_size("expert") // group_size
    segment_id = lax.axis_index("pipe")
    last_segment = lax.axis_size("pipe") - 1
    up_now = up_state[0]
    down_now = down_state[0]
    features = up_now.shape[1]
    slot_cap = up_now.shape[0] * TOP // expert_count
    up_done = up_now
    down_done = down_now
    for tick_id in range(TICKS):
        up_normed = normalize(up_now, gain_row)
        down_normed = normalize(down_now, gain_row)
        up_scatter, up_weights, up_slot = routing_tables(
            up_normed, up_route[tick_id, 0], router_cols, expert_count, slot_cap
        )
        down_scatter, down_weights, down_slot = routing_tables(
            down_normed, down_route[tick_id, 0], router_cols, expert_count, slot_cap
        )
        up_send = jnp.einsum(
            "ecr,rd->ecd", up_scatter, up_normed, preferred_element_type=jnp.float32
        ).astype(jnp.bfloat16)
        down_send = jnp.einsum(
            "ecr,rd->ecd", down_scatter, down_normed, preferred_element_type=jnp.float32
        ).astype(jnp.bfloat16)
        outbound = jnp.concatenate([up_send, down_send], axis=1)
        outgoing = jnp.broadcast_to(
            outbound[:, None], (expert_count, group_size, 2 * slot_cap, features)
        ).reshape(expert_count * group_size, 2 * slot_cap, features)
        returned = run_experts(
            lax.all_to_all(outgoing, "expert", split_axis=0, concat_axis=0, tiled=True),
            gate_cols,
            up_cols,
            down_rows,
        )
        summed = jnp.sum(
            returned.reshape(expert_count, group_size, 2 * slot_cap, features).astype(jnp.float32),
            axis=1,
        )
        up_outputs = summed[:, :slot_cap].reshape(expert_count * slot_cap, features)
        down_outputs = summed[:, slot_cap:].reshape(expert_count * slot_cap, features)
        up_done = mix_rows(up_now, up_weights, up_slot, up_outputs).astype(jnp.bfloat16)
        down_done = mix_rows(down_now, down_weights, down_slot, down_outputs).astype(jnp.bfloat16)
        if tick_id + 1 < TICKS:
            up_moved = shifted(up_done, "pipe", 1)
            down_moved = shifted(down_done, "pipe", -1)
            up_now = jnp.where(segment_id == 0, entering_up, up_moved)
            down_now = jnp.where(segment_id == last_segment, entering_down, down_moved)
    return (up_done[None], down_done[None])


def iota(shape, axis):
    return lax.broadcasted_iota(jnp.int32, shape, axis)


def slot_map(up_ids, down_ids, parts, slot_cap):
    rows = up_ids.shape[1]
    span = 2 * rows * parts
    diagonal = iota((rows, rows), 0) == iota((rows, rows), 1)
    up_ids = jnp.sum(jnp.where(diagonal, up_ids, 0), axis=1, keepdims=True)
    down_ids = jnp.sum(jnp.where(diagonal, down_ids, 0), axis=1, keepdims=True)
    lane = iota((rows, span), 1)
    row = iota((rows, span), 0)
    own = lane % rows
    way = lane // rows % 2
    ids = jnp.where(way == 0, up_ids, down_ids)
    chosen = jnp.sum(jnp.where(row == own, ids, 0), axis=0, keepdims=True)
    rank = jnp.sum(jnp.where((ids == chosen) & (row < own), 1, 0), axis=0, keepdims=True)
    lane = iota((1, span), 1)
    piece = lane // (2 * rows)
    way = lane // rows % 2
    target = chosen * SUBLANES + piece * (2 * slot_cap) + way * slot_cap + rank
    return jnp.where(iota((span, span), 0) == target, 1.0, 0.0)


def block_map(parts, slot_cap, span):
    wide = 2 * slot_cap
    rows = span // parts
    lane = iota((span, span), 1)
    block, within = lane // SUBLANES, lane % SUBLANES
    target = within // wide * rows + block * wide + within % wide
    return jnp.where(iota((span, span), 0) == target, 1.0, 0.0)


def moved(onehot, rows):
    return jnp.dot(
        onehot.astype(jnp.bfloat16), rows, preferred_element_type=jnp.float32
    ).astype(jnp.bfloat16)


def pack_rows(onehot, up_rows, down_rows, parts):
    width = up_rows.shape[1] // parts
    pieces = []
    for q in range(parts):
        pieces += [up_rows[:, q * width : (q + 1) * width], down_rows[:, q * width : (q + 1) * width]]
    return moved(onehot, jnp.concatenate(pieces, axis=0))


def started(sources, targets, sems, first=0):
    copies = [
        pltpu.make_async_copy(source, target, sems.at[first + i])
        for i, (source, target) in enumerate(zip(sources, targets))
    ]
    for copy in copies:
        copy.start()
    return copies


def row_chunks(source, target, count):
    step = target.shape[0] // count
    ranges = [pl.ds(i * step, step) for i in range(count)]
    return [source.at[r] for r in ranges], [target.at[r] for r in ranges]


def prepare_kernel(
    parts,
    slot_cap,
    ticks,
    early,
    up,
    down,
    up_ids,
    down_ids,
    enter_up,
    enter_down,
    gain,
    router,
    w_down,
    out_ref,
    maps_ref,
    backs_ref,
    enter_up_v,
    enter_down_v,
    gain_v,
    router_v,
    early_v,
    up_v,
    down_v,
    up_i,
    down_i,
    cols_v,
    sems,
):
    sources = (up_ids, down_ids, up.at[0], down.at[0], router.at[0], gain, enter_up, enter_down)
    targets = (up_i, down_i, up_v, down_v, cols_v, gain_v, enter_up_v, enter_down_v)
    copies = started(sources, targets, sems)
    rows = early_v.shape[0] // early
    ranges = [pl.ds(i * rows, rows) for i in range(early)]
    late = started(
        [w_down.at[0, r] for r in ranges], [early_v.at[r] for r in ranges], sems, len(copies)
    )
    copies[0].wait()
    copies[1].wait()
    onehots = [slot_map(up_i[t, 0], down_i[t, 0], parts, slot_cap) for t in range(ticks)]
    copies[2].wait()
    copies[3].wait()
    out_ref[...] = pack_rows(onehots[0], up_v[...], down_v[...], parts)
    for t in range(ticks):
        maps_ref[t] = onehots[t].astype(jnp.bfloat16)
        backs_ref[t] = onehots[t].T.astype(jnp.bfloat16)
    copies[4].wait()
    cols = cols_v[...].astype(jnp.float32)
    mine = iota(cols.shape, 0) == lax.axis_index("expert")
    router_v[...] = jnp.sum(jnp.where(mine, cols, 0.0), axis=0, keepdims=True)
    for copy in copies[5:] + late:
        copy.wait()


def resend_kernel(parts, pipe, tick_id, even_ref, odd_ref, enter_up_ref, enter_down_ref, maps_ref, out_ref):
    place = lax.axis_index("pipe")
    is_even = place % 2 == 0
    even, odd = even_ref[...], odd_ref[...]
    up_rows = jnp.where(is_even, odd, even)
    down_rows = jnp.where(is_even, even, odd)
    up_rows = jnp.where(place == 0, enter_up_ref[...], up_rows)
    down_rows = jnp.where(place == pipe - 1, enter_down_ref[...], down_rows)
    out_ref[...] = pack_rows(maps_ref[tick_id], up_rows, down_rows, parts)


def unpack_kernel(tick_id, by_parity, in_ref, backs_ref, first_ref, second_ref):
    rows = first_ref.shape[0]
    width = in_ref.shape[1]
    back = moved(backs_ref[tick_id], in_ref[...])
    swap = lax.axis_index("pipe") % 2 == 1 if by_parity else None
    for q in range(first_ref.shape[1] // width):
        up_piece = back[2 * q * rows : (2 * q + 1) * rows]
        down_piece = back[(2 * q + 1) * rows : (2 * q + 2) * rows]
        if by_parity:
            up_piece, down_piece = (
                jnp.where(swap, down_piece, up_piece),
                jnp.where(swap, up_piece, down_piece),
            )
        first_ref[:, q * width : (q + 1) * width] = up_piece
        second_ref[:, q * width : (q + 1) * width] = down_piece


def expert_rows(parts, slot_cap, in_ref, gain_ref, router_ref, out_ref, x_ref, inner, outer):
    span, width = in_ref.shape
    rows = span // parts
    onehot = block_map(parts, slot_cap, span)
    spread = moved(onehot, in_ref[...])
    for q in range(parts):
        x_ref[:, q * width : (q + 1) * width] = spread[q * rows : (q + 1) * rows]
    widened = x_ref[...].astype(jnp.float32)
    inverse = lax.rsqrt(jnp.mean(widened * widened, axis=1, keepdims=True) + norm_eps)
    normed = (widened * inverse * gain_ref[...]).astype(jnp.bfloat16)
    logit = jnp.sum(normed.astype(jnp.float32) * router_ref[...], axis=1, keepdims=True)
    weight = jax.nn.sigmoid(logit)
    gate_pre = up_pre = part = 0.0
    start = 0
    for gate, up, copies in inner:
        for copy in copies:
            copy.wait()
        piece = normed[:, start : start + gate.shape[0]]
        gate_pre += jnp.dot(piece, gate[...], preferred_element_type=jnp.float32)
        up_pre += jnp.dot(piece, up[...], preferred_element_type=jnp.float32)
        start += gate.shape[0]
    hidden = (jax.nn.silu(gate_pre) * up_pre).astype(jnp.bfloat16)
    start = 0
    for down, copies in outer:
        for copy in copies:
            copy.wait()
        piece = hidden[:, start : start + down.shape[0]]
        part += jnp.dot(piece, down[...], preferred_element_type=jnp.float32)
        start += down.shape[0]
    part = part.astype(jnp.bfloat16).astype(jnp.float32)
    done = (x_ref[...].astype(jnp.float32) + weight * part).astype(jnp.bfloat16)
    pieces = [done[:, q * width : (q + 1) * width] for q in range(parts)]
    out_ref[...] = moved(onehot.T, jnp.concatenate(pieces, axis=0))


def first_kernel(
    parts,
    slot_cap,
    chunks,
    in_ref,
    gain_ref,
    router_ref,
    early_ref,
    gate,
    up,
    down,
    out_ref,
    gate_v,
    up_v,
    late_v,
    x_ref,
    sems,
):
    step = gate_v.shape[0] // chunks
    inner = []
    for i in range(chunks):
        r = pl.ds(i * step, step)
        copies = started((gate.at[0, r], up.at[0, r]), (gate_v.at[r], up_v.at[r]), sems, 2 * i)
        inner.append((gate_v.at[r], up_v.at[r], copies))
    early = early_ref.shape[0]
    step = late_v.shape[0] // 2
    ranges = [(pl.ds(i * step, step), pl.ds(early + i * step, step)) for i in range(2)]
    copies = started(
        [down.at[0, s] for _, s in ranges], [late_v.at[r] for r, _ in ranges], sems, 2 * chunks
    )
    outer = [(early_ref, [])] + [(late_v.at[r], [c]) for (r, _), c in zip(ranges, copies)]
    expert_rows(parts, slot_cap, in_ref, gain_ref, router_ref, out_ref, x_ref, inner, outer)


def later_kernel(
    parts, slot_cap, in_ref, gain_ref, router_ref, early_ref, gate_ref, up_ref, late_ref, out_ref, x_ref
):
    inner = [(gate_ref, up_ref, [])]
    outer = [(early_ref, []), (late_ref, [])]
    expert_rows(parts, slot_cap, in_ref, gain_ref, router_ref, out_ref, x_ref, inner, outer)


VMEM_SPEC = pl.BlockSpec(memory_space=pltpu.VMEM)
HBM_SPEC = pl.BlockSpec(memory_space=pltpu.HBM)


def local_call(kernel, out_shapes, near, far=(), scratch=(), limit=8 << 20):
    far = [pltpu.with_memory_space_constraint(x, pltpu.HBM) for x in far]
    return pl.pallas_call(
        kernel,
        out_shape=out_shapes,
        in_specs=[VMEM_SPEC] * len(near) + [HBM_SPEC] * len(far),
        out_specs=jax.tree.map(lambda _: VMEM_SPEC, out_shapes),
        scratch_shapes=list(scratch),
        compiler_params=pltpu.CompilerParams(vmem_limit_bytes=limit),
    )(*near, *far)


def exchanged(blocks):
    return lax.all_to_all(blocks, "expert", split_axis=0, concat_axis=0, tiled=True)


EARLY_COPIES = 4
CHUNKS = 7


def single_shards(
    up_state,
    down_state,
    entering_up,
    entering_down,
    up_route,
    down_route,
    norm_gain,
    router,
    w_gate,
    w_up,
    w_down,
):
    pipe = lax.axis_size("pipe")
    experts = lax.axis_size("expert")
    rows, features = up_state.shape[1:]
    hidden = w_gate.shape[2]
    slot_cap = rows * TOP // experts
    parts = SUBLANES // (2 * slot_cap)
    span = experts * SUBLANES
    early = hidden // 2
    blocks = pltpu.VMEM((span, features // parts), jnp.bfloat16)
    batch = pltpu.VMEM((rows, features), jnp.bfloat16)
    ids_v = pltpu.VMEM((TICKS, 1, 1, rows), jnp.int32)
    row_v = pltpu.VMEM((1, features), jnp.float32)
    x_v = pltpu.VMEM((span // parts, features), jnp.bfloat16)
    maps_v = pltpu.VMEM((TICKS, span, span), jnp.bfloat16)
    inner_v = pltpu.VMEM((features, hidden), jnp.bfloat16)
    sent, maps, backs, enter_up, enter_down, gain, column, early_down = local_call(
        functools.partial(prepare_kernel, parts, slot_cap, TICKS, EARLY_COPIES),
        (blocks, maps_v, maps_v, batch, batch, row_v, row_v, pltpu.VMEM((early, features), jnp.bfloat16)),
        (),
        (
            up_state,
            down_state,
            up_route.transpose(0, 1, 3, 2),
            down_route.transpose(0, 1, 3, 2),
            entering_up,
            entering_down,
            norm_gain,
            router.transpose(0, 2, 1),
            w_down,
        ),
        [
            batch,
            batch,
            ids_v,
            ids_v,
            pltpu.VMEM(router.shape[:0:-1], router.dtype),
            pltpu.SemaphoreType.DMA((8 + EARLY_COPIES,)),
        ],
    )
    done, gate, up, late_down = local_call(
        functools.partial(first_kernel, parts, slot_cap, CHUNKS),
        (blocks, inner_v, inner_v, pltpu.VMEM((hidden - early, features), jnp.bfloat16)),
        (exchanged(sent), gain, column, early_down),
        (w_gate, w_up, w_down),
        [x_v, pltpu.SemaphoreType.DMA((2 * CHUNKS + 2,))],
    )
    even_pairs = [(i, i ^ 1) for i in range(pipe) if i ^ 1 < pipe]
    odd_pairs = [(i, ((i + 1) ^ 1) - 1) for i in range(pipe) if 0 <= ((i + 1) ^ 1) - 1 < pipe]
    for tick_id in range(1, TICKS):
        kernel = functools.partial(unpack_kernel, tick_id - 1, True)
        first, second = local_call(kernel, (batch, batch), (exchanged(done), backs))
        first = lax.ppermute(first, "pipe", even_pairs)
        second = lax.ppermute(second, "pipe", odd_pairs)
        kernel = functools.partial(resend_kernel, parts, pipe, tick_id)
        sent = local_call(kernel, blocks, (first, second, enter_up, enter_down, maps))
        kernel = functools.partial(later_kernel, parts, slot_cap)
        args = (exchanged(sent), gain, column, early_down, gate, up, late_down)
        done = local_call(kernel, blocks, args, (), [x_v])
    batch = jax.ShapeDtypeStruct((rows, features), jnp.bfloat16)
    kernel = functools.partial(unpack_kernel, TICKS - 1, False)
    first, second = local_call(kernel, (batch, batch), (exchanged(done), backs))
    return (first[None], second[None])


def shards(*args):
    rows, features = args[0].shape[1:]
    experts = lax.axis_size("expert")
    slot_cap = rows * TOP // EXPERTS
    fits = experts == EXPERTS and rows % SUBLANES == 0 and SUBLANES % (2 * slot_cap) == 0
    fits = fits and features % (SUBLANES // (2 * slot_cap) * LANES) == 0
    return single_shards(*args) if fits else grouped_shards(*args)


def solution(mesh):
    return jax.shard_map(
        shards,
        mesh=mesh,
        in_specs=(
            P("pipe", "expert", None),
            P("pipe", "expert", None),
            P("expert", None),
            P("expert", None),
            P(None, "pipe", "expert", None),
            P(None, "pipe", "expert", None),
            P("pipe", None),
            P("pipe", None, None),
            P("pipe", None, "expert"),
            P("pipe", None, "expert"),
            P("pipe", "expert", None),
        ),
        out_specs=(P("pipe", "expert", None), P("pipe", "expert", None)),
        check_vma=False,
    )
```

```python
import functools

import jax
import jax.numpy as jnp
from jax import lax
from jax.experimental import pallas as pl
from jax.experimental.pallas import tpu as pltpu
from jax.sharding import PartitionSpec as P

TOP = 1
TICKS = 2
EXPERTS = 8
LANES = 128
SUBLANES = 16


norm_eps = 1e-06


def shifted(value, axis, by):
    length = lax.axis_size(axis)
    pairs = [(i, i + by) for i in range(length) if 0 <= i + by < length]
    return lax.ppermute(value, axis, pairs)


def normalize(token_rows, gain_row):
    widened = token_rows.astype(jnp.float32)
    inverse = lax.rsqrt(jnp.mean(widened * widened, axis=1, keepdims=True) + norm_eps)
    return (widened * inverse * gain_row).astype(jnp.bfloat16)


def routing_tables(normed, routing, router_cols, expert_count, slot_cap):
    logits = jnp.dot(normed, router_cols, preferred_element_type=jnp.float32)
    affinity = jax.nn.sigmoid(logits)
    weights = jnp.take_along_axis(affinity, routing, axis=1)
    flat_ids = routing.reshape(-1)
    onehot = (flat_ids[:, None] == jnp.arange(expert_count, dtype=jnp.int32)[None, :]).astype(
        jnp.int32
    )
    before = jnp.cumsum(onehot, axis=0) - onehot
    slot_ids = jnp.sum(before * onehot, axis=1).reshape(routing.shape)
    expert_hit = (
        routing[:, :, None] == jnp.arange(expert_count, dtype=jnp.int32)[None, None, :]
    ).astype(jnp.float32)
    slot_hit = (
        slot_ids[:, :, None] == jnp.arange(slot_cap, dtype=jnp.int32)[None, None, :]
    ).astype(jnp.float32)
    scatter_map = jnp.einsum("rke,rkc->ecr", expert_hit, slot_hit).astype(jnp.bfloat16)
    flat_slot = routing * slot_cap + slot_ids
    return (scatter_map, weights, flat_slot)


def run_experts(received, gate_cols, up_cols, down_rows):
    sources, slot_count, features = received.shape
    flat_rows = received.reshape(sources * slot_count, features)
    gate_pre = jnp.dot(flat_rows, gate_cols, preferred_element_type=jnp.float32)
    up_pre = jnp.dot(flat_rows, up_cols, preferred_element_type=jnp.float32)
    hidden = (jax.nn.silu(gate_pre) * up_pre).astype(jnp.bfloat16)
    partial_value = jnp.dot(hidden, down_rows, preferred_element_type=jnp.float32).astype(
        jnp.bfloat16
    )
    partial_value = partial_value.reshape(sources, slot_count, features)
    return lax.all_to_all(partial_value, "expert", split_axis=0, concat_axis=0, tiled=True)


def mix_rows(token_rows, weights, flat_slot, outputs):
    picked = outputs[flat_slot]
    return token_rows.astype(jnp.float32) + jnp.sum(weights[:, :, None] * picked, axis=1)


def grouped_shards(
    up_state,
    down_state,
    entering_up,
    entering_down,
    up_route,
    down_route,
    norm_gain,
    router,
    w_gate,
    w_up,
    w_down,
):
    gate_cols = w_gate[0]
    up_cols = w_up[0]
    down_rows = w_down[0]
    gain_row = norm_gain[0]
    router_cols = router[0]
    group_size = max(1, lax.axis_size("expert") // EXPERTS)
    expert_count = lax.axis_size("expert") // group_size
    segment_id = lax.axis_index("pipe")
    last_segment = lax.axis_size("pipe") - 1
    up_now = up_state[0]
    down_now = down_state[0]
    features = up_now.shape[1]
    slot_cap = up_now.shape[0] * TOP // expert_count
    up_done = up_now
    down_done = down_now
    for tick_id in range(TICKS):
        up_normed = normalize(up_now, gain_row)
        down_normed = normalize(down_now, gain_row)
        up_scatter, up_weights, up_slot = routing_tables(
            up_normed, up_route[tick_id, 0], router_cols, expert_count, slot_cap
        )
        down_scatter, down_weights, down_slot = routing_tables(
            down_normed, down_route[tick_id, 0], router_cols, expert_count, slot_cap
        )
        up_send = jnp.einsum(
            "ecr,rd->ecd", up_scatter, up_normed, preferred_element_type=jnp.float32
        ).astype(jnp.bfloat16)
        down_send = jnp.einsum(
            "ecr,rd->ecd", down_scatter, down_normed, preferred_element_type=jnp.float32
        ).astype(jnp.bfloat16)
        outbound = jnp.concatenate([up_send, down_send], axis=1)
        outgoing = jnp.broadcast_to(
            outbound[:, None], (expert_count, group_size, 2 * slot_cap, features)
        ).reshape(expert_count * group_size, 2 * slot_cap, features)
        returned = run_experts(
            lax.all_to_all(outgoing, "expert", split_axis=0, concat_axis=0, tiled=True),
            gate_cols,
            up_cols,
            down_rows,
        )
        summed = jnp.sum(
            returned.reshape(expert_count, group_size, 2 * slot_cap, features).astype(jnp.float32),
            axis=1,
        )
        up_outputs = summed[:, :slot_cap].reshape(expert_count * slot_cap, features)
        down_outputs = summed[:, slot_cap:].reshape(expert_count * slot_cap, features)
        up_done = mix_rows(up_now, up_weights, up_slot, up_outputs).astype(jnp.bfloat16)
        down_done = mix_rows(down_now, down_weights, down_slot, down_outputs).astype(jnp.bfloat16)
        if tick_id + 1 < TICKS:
            up_moved = shifted(up_done, "pipe", 1)
            down_moved = shifted(down_done, "pipe", -1)
            up_now = jnp.where(segment_id == 0, entering_up, up_moved)
            down_now = jnp.where(segment_id == last_segment, entering_down, down_moved)
    return (up_done[None], down_done[None])


def iota(shape, axis):
    return lax.broadcasted_iota(jnp.int32, shape, axis)


def place():
    index = lax.axis_index("expert")
    return index // 2, index % 2


def one_hot(rows, target):
    return jnp.where(iota((rows, target.shape[1]), 0) == target, 1.0, 0.0)


def row_maps(up_ids, down_ids, parts, slot_cap, span):
    rows = up_ids.shape[1]
    width = 2 * rows * parts
    diagonal = iota((rows, rows), 0) == iota((rows, rows), 1)
    up_ids = jnp.sum(jnp.where(diagonal, up_ids, 0), axis=1, keepdims=True)
    down_ids = jnp.sum(jnp.where(diagonal, down_ids, 0), axis=1, keepdims=True)
    lane = iota((rows, width), 1)
    row = iota((rows, width), 0)
    own = lane % rows
    ids = jnp.where(lane // rows % 2 == 0, up_ids, down_ids)
    chosen = jnp.sum(jnp.where(row == own, ids, 0), axis=0, keepdims=True)
    rank = jnp.sum(jnp.where((ids == chosen) & (row < own), 1, 0), axis=0, keepdims=True)
    lane = iota((1, width), 1)
    within = lane // (2 * rows) * (2 * slot_cap) + lane // rows % 2 * slot_cap + rank
    chip, core = place()
    across = (chosen // 2) ^ chip ^ (span // (2 * SUBLANES) - 1)
    to_core = chosen % 2
    sent = (across * 2 + to_core) * SUBLANES + within
    array = across + jnp.where(to_core == core, 0, span // (2 * SUBLANES))
    received = (array * 2 + core) * SUBLANES + within
    return one_hot(span, sent), one_hot(2 * span, received)


def expert_maps(parts, slot_cap, span):
    wide = 2 * slot_cap
    rows = span // parts
    chips = span // (2 * SUBLANES)
    _, core = place()
    lane = iota((1, 2 * span), 1)
    array, to_core, within = lane // (2 * SUBLANES), lane // SUBLANES % 2, lane % SUBLANES
    row = within // wide * rows + array * wide + within % wide
    received = one_hot(span, jnp.where(to_core == core, row, -1))
    lane = iota((1, span), 1)
    array, to_core, within = lane // (2 * SUBLANES), lane // SUBLANES % 2, lane % SUBLANES
    array = array + jnp.where(to_core == core, 0, chips)
    return received, one_hot(span, within // wide * rows + array * wide + within % wide)


def moved(onehot, rows):
    return jnp.dot(
        onehot.astype(jnp.bfloat16), rows, preferred_element_type=jnp.float32
    ).astype(jnp.bfloat16)


def stacked(refs):
    return jnp.concatenate([ref[...] for ref in refs], axis=0)


def put(value, refs):
    rows = refs[0].shape[0]
    for i, ref in enumerate(refs):
        ref[...] = value[i * rows : (i + 1) * rows]


def pack_rows(onehot, up_rows, down_rows, parts):
    width = up_rows.shape[1] // parts
    pieces = []
    for q in range(parts):
        pieces += [up_rows[:, q * width : (q + 1) * width], down_rows[:, q * width : (q + 1) * width]]
    return moved(onehot, jnp.concatenate(pieces, axis=0))


def started(sources, targets, sems, first=0):
    copies = [
        pltpu.make_async_copy(source, target, sems.at[first + i])
        for i, (source, target) in enumerate(zip(sources, targets))
    ]
    for copy in copies:
        copy.start()
    return copies


def cut(rows, count):
    step = rows // count
    return [pl.ds(i * step, step) for i in range(count)]


def prepare_kernel(
    parts,
    slot_cap,
    ticks,
    early,
    up,
    down,
    up_ids,
    down_ids,
    enter_up,
    enter_down,
    gain,
    router,
    w_up,
    out_refs,
    maps_ref,
    backs_ref,
    enter_up_v,
    enter_down_v,
    gain_v,
    router_v,
    early_v,
    up_v,
    down_v,
    up_i,
    down_i,
    cols_v,
    sems,
):
    sources = (up_ids, down_ids, up.at[0], down.at[0], router.at[0], gain, enter_up, enter_down)
    targets = (up_i, down_i, up_v, down_v, cols_v, gain_v, enter_up_v, enter_down_v)
    copies = started(sources, targets, sems)
    ranges = cut(early_v.shape[0], early)
    late = started(
        [w_up.at[0, r] for r in ranges], [early_v.at[r] for r in ranges], sems, len(copies)
    )
    copies[0].wait()
    copies[1].wait()
    span = maps_ref.shape[1]
    maps = [row_maps(up_i[t, 0], down_i[t, 0], parts, slot_cap, span) for t in range(ticks)]
    copies[2].wait()
    copies[3].wait()
    put(pack_rows(maps[0][0], up_v[...], down_v[...], parts), out_refs)
    for t in range(ticks):
        maps_ref[t] = maps[t][0].astype(jnp.bfloat16)
        backs_ref[t] = maps[t][1].T.astype(jnp.bfloat16)
    copies[4].wait()
    cols = cols_v[...].astype(jnp.float32)
    mine = iota(cols.shape, 0) == lax.axis_index("expert")
    router_v[...] = jnp.sum(jnp.where(mine, cols, 0.0), axis=0, keepdims=True)
    for copy in copies[5:] + late:
        copy.wait()


def resend_kernel(parts, pipe, tick_id, even_ref, odd_ref, enter_up_ref, enter_down_ref, maps_ref, out_refs):
    section = lax.axis_index("pipe")
    is_even = section % 2 == 0
    even, odd = even_ref[...], odd_ref[...]
    up_rows = jnp.where(is_even, odd, even)
    down_rows = jnp.where(is_even, even, odd)
    up_rows = jnp.where(section == 0, enter_up_ref[...], up_rows)
    down_rows = jnp.where(section == pipe - 1, enter_down_ref[...], down_rows)
    put(pack_rows(maps_ref[tick_id], up_rows, down_rows, parts), out_refs)


def unpack_kernel(tick_id, by_parity, in_refs, backs_ref, first_ref, second_ref):
    rows = first_ref.shape[0]
    width = in_refs[0].shape[1]
    back = moved(backs_ref[tick_id], stacked(in_refs))
    swap = lax.axis_index("pipe") % 2 == 1 if by_parity else None
    for q in range(first_ref.shape[1] // width):
        up_piece = back[2 * q * rows : (2 * q + 1) * rows]
        down_piece = back[(2 * q + 1) * rows : (2 * q + 2) * rows]
        if by_parity:
            up_piece, down_piece = (
                jnp.where(swap, down_piece, up_piece),
                jnp.where(swap, up_piece, down_piece),
            )
        first_ref[:, q * width : (q + 1) * width] = up_piece
        second_ref[:, q * width : (q + 1) * width] = down_piece


def expert_rows(parts, slot_cap, in_refs, gain_ref, router_ref, out_refs, x_ref, gates, ups, downs):
    span = sum(ref.shape[0] for ref in out_refs)
    width = in_refs[0].shape[1]
    rows = span // parts
    received, sent = expert_maps(parts, slot_cap, span)
    spread = moved(received, stacked(in_refs))
    for q in range(parts):
        x_ref[:, q * width : (q + 1) * width] = spread[q * rows : (q + 1) * rows]
    widened = x_ref[...].astype(jnp.float32)
    inverse = lax.rsqrt(jnp.mean(widened * widened, axis=1, keepdims=True) + norm_eps)
    normed = (widened * inverse * gain_ref[...]).astype(jnp.bfloat16)
    logit = jnp.sum(normed.astype(jnp.float32) * router_ref[...], axis=1, keepdims=True)
    weight = jax.nn.sigmoid(logit)

    def product(left, pieces):
        total, start = 0.0, 0
        for ref, copies in pieces:
            for copy in copies:
                copy.wait()
            part = left[:, start : start + ref.shape[0]]
            total += jnp.dot(part, ref[...], preferred_element_type=jnp.float32)
            start += ref.shape[0]
        return total

    gate_pre = product(normed, gates)
    hidden = (jax.nn.silu(gate_pre) * product(normed, ups)).astype(jnp.bfloat16)
    part = product(hidden, downs).astype(jnp.bfloat16).astype(jnp.float32)
    done = (x_ref[...].astype(jnp.float32) + weight * part).astype(jnp.bfloat16)
    pieces = [done[:, q * width : (q + 1) * width] for q in range(parts)]
    put(moved(sent.T, jnp.concatenate(pieces, axis=0)), out_refs)


def load_kernel(after_ref, source, target, sems):
    del after_ref
    ranges = cut(target.shape[0], sems.shape[0])
    for copy in started([source.at[0, r] for r in ranges], [target.at[r] for r in ranges], sems):
        copy.wait()


def first_kernel(
    parts,
    slot_cap,
    in_refs,
    gain_ref,
    router_ref,
    gate_ref,
    early_ref,
    down_ref,
    up,
    out_refs,
    late_v,
    x_ref,
    sems,
):
    early = early_ref.shape[0]
    step = late_v.shape[0] // sems.shape[0]
    ranges = cut(late_v.shape[0], sems.shape[0])
    sources = [up.at[0, pl.ds(early + i * step, step)] for i in range(len(ranges))]
    copies = started(sources, [late_v.at[r] for r in ranges], sems)
    ups = [(early_ref, [])] + [(late_v.at[r], [c]) for r, c in zip(ranges, copies)]
    expert_rows(
        parts, slot_cap, in_refs, gain_ref, router_ref, out_refs, x_ref, [(gate_ref, [])], ups, [(down_ref, [])]
    )


def later_kernel(
    parts, slot_cap, in_refs, gain_ref, router_ref, gate_ref, early_ref, down_ref, late_ref, out_refs, x_ref
):
    ups = [(early_ref, []), (late_ref, [])]
    expert_rows(
        parts, slot_cap, in_refs, gain_ref, router_ref, out_refs, x_ref, [(gate_ref, [])], ups, [(down_ref, [])]
    )


VMEM_SPEC = pl.BlockSpec(memory_space=pltpu.VMEM)
HBM_SPEC = pl.BlockSpec(memory_space=pltpu.HBM)


def local_call(kernel, out_shapes, near, far=(), scratch=(), limit=8 << 20, cost=None):
    far = [pltpu.with_memory_space_constraint(x, pltpu.HBM) for x in far]
    close, near_tree = jax.tree.flatten(tuple(near))
    outs, out_tree = jax.tree.flatten(out_shapes)

    def body(*refs):
        refs = iter(refs)
        take = lambda count: [next(refs) for _ in range(count)]
        args = [*near_tree.unflatten(take(len(close))), *take(len(far))]
        results = out_tree.unflatten(take(len(outs)))
        kernel(*args, *(results if isinstance(results, tuple) else (results,)), *refs)

    results = pl.pallas_call(
        body,
        out_shape=outs,
        in_specs=[VMEM_SPEC] * len(close) + [HBM_SPEC] * len(far),
        out_specs=[VMEM_SPEC] * len(outs),
        scratch_shapes=list(scratch),
        compiler_params=pltpu.CompilerParams(vmem_limit_bytes=limit),
        cost_estimate=cost,
    )(*close, *far)
    return out_tree.unflatten(results)


def exchanged(arrays, beside=None):
    last = len(arrays) - 1
    devices = range(2 * len(arrays))
    arrived = [
        lax.ppermute(arrays[j], "expert", [(i, i ^ (2 * (last - j))) for i in devices])
        for j in range(last)
    ]
    if beside is not None:
        arrived, beside = lax.optimization_barrier((arrived, beside))
    arrived.append(arrays[last])
    passed = [lax.ppermute(x, "expert", [(i, i ^ 1) for i in devices]) for x in arrived]
    return tuple(arrived + passed), beside


def section_pairs(parity, pipe, experts):
    pairs = []
    for section in range(pipe):
        other = ((section + parity) ^ 1) - parity
        for i in range(experts):
            target = (other, i) if 0 <= other < pipe else (section, i ^ 1)
            pairs.append((section * experts + i, target[0] * experts + target[1]))
    return pairs


EARLY_COPIES = 4
LATE_COPIES = 4
LOAD_COPIES = 4


def single_shards(
    up_state,
    down_state,
    entering_up,
    entering_down,
    up_route,
    down_route,
    norm_gain,
    router,
    w_gate,
    w_up,
    w_down,
):
    pipe = lax.axis_size("pipe")
    experts = lax.axis_size("expert")
    rows, features = up_state.shape[1:]
    hidden = w_gate.shape[2]
    slot_cap = rows * TOP // experts
    parts = SUBLANES // (2 * slot_cap)
    span = experts * SUBLANES
    early = features // 2
    blocks = (pltpu.VMEM((2 * SUBLANES, features // parts), jnp.bfloat16),) * (experts // 2)
    batch = pltpu.VMEM((rows, features), jnp.bfloat16)
    ids_v = pltpu.VMEM((TICKS, 1, 1, rows), jnp.int32)
    row_v = pltpu.VMEM((1, features), jnp.float32)
    x_v = pltpu.VMEM((span // parts, features), jnp.bfloat16)
    sent, maps, backs, enter_up, enter_down, gain, column, early_up = local_call(
        functools.partial(prepare_kernel, parts, slot_cap, TICKS, EARLY_COPIES),
        (
            blocks,
            pltpu.VMEM((TICKS, span, span), jnp.bfloat16),
            pltpu.VMEM((TICKS, span, 2 * span), jnp.bfloat16),
            batch,
            batch,
            row_v,
            row_v,
            pltpu.VMEM((early, hidden), jnp.bfloat16),
        ),
        (),
        (
            up_state,
            down_state,
            up_route.transpose(0, 1, 3, 2),
            down_route.transpose(0, 1, 3, 2),
            entering_up,
            entering_down,
            norm_gain,
            router.transpose(0, 2, 1),
            w_up,
        ),
        [
            batch,
            batch,
            ids_v,
            ids_v,
            pltpu.VMEM(router.shape[:0:-1], router.dtype),
            pltpu.SemaphoreType.DMA((8 + EARLY_COPIES,)),
        ],
    )
    gate = local_call(
        load_kernel,
        pltpu.VMEM((features, hidden), jnp.bfloat16),
        (sent[0],),
        (w_gate,),
        [pltpu.SemaphoreType.DMA((LOAD_COPIES,))],
        cost=pl.CostEstimate(flops=0, transcendentals=0, bytes_accessed=4 * features * hidden),
    )
    received, gate = exchanged(sent, gate)
    done, late_up = local_call(
        functools.partial(first_kernel, parts, slot_cap),
        (blocks, pltpu.VMEM((features - early, hidden), jnp.bfloat16)),
        (received, gain, column, gate, early_up, w_down[0]),
        (w_up,),
        [x_v, pltpu.SemaphoreType.DMA((LATE_COPIES,))],
    )
    for tick_id in range(1, TICKS):
        kernel = functools.partial(unpack_kernel, tick_id - 1, True)
        first, second = local_call(kernel, (batch, batch), (exchanged(done)[0], backs))
        first = lax.ppermute(first, ("pipe", "expert"), section_pairs(0, pipe, experts))
        second = lax.ppermute(second, ("pipe", "expert"), section_pairs(1, pipe, experts))
        kernel = functools.partial(resend_kernel, parts, pipe, tick_id)
        (sent,) = local_call(kernel, (blocks,), (first, second, enter_up, enter_down, maps))
        kernel = functools.partial(later_kernel, parts, slot_cap)
        args = (exchanged(sent)[0], gain, column, gate, early_up, w_down[0], late_up)
        (done,) = local_call(kernel, (blocks,), args, (), [x_v])
    batch = jax.ShapeDtypeStruct((rows, features), jnp.bfloat16)
    kernel = functools.partial(unpack_kernel, TICKS - 1, False)
    first, second = local_call(kernel, (batch, batch), (exchanged(done)[0], backs))
    return (first[None], second[None])


def shards(*args):
    rows, features = args[0].shape[1:]
    experts = lax.axis_size("expert")
    slot_cap = rows * TOP // EXPERTS
    fits = experts == EXPERTS and rows % SUBLANES == 0 and SUBLANES % (2 * slot_cap) == 0
    fits = fits and features % (SUBLANES // (2 * slot_cap) * LANES) == 0
    return single_shards(*args) if fits else grouped_shards(*args)


def solution(mesh):
    return jax.shard_map(
        shards,
        mesh=mesh,
        in_specs=(
            P("pipe", "expert", None),
            P("pipe", "expert", None),
            P("expert", None),
            P("expert", None),
            P(None, "pipe", "expert", None),
            P(None, "pipe", "expert", None),
            P("pipe", None),
            P("pipe", None, None),
            P("pipe", None, "expert"),
            P("pipe", None, "expert"),
            P("pipe", "expert", None),
        ),
        out_specs=(P("pipe", "expert", None), P("pipe", "expert", None)),
        check_vma=False,
    )
```

```python
import functools

import jax
import jax.numpy as jnp
from jax import lax
from jax.experimental import pallas as pl
from jax.experimental.pallas import tpu as pltpu
from jax.sharding import PartitionSpec as P

TOP = 1
TICKS = 2
EXPERTS = 8
LANES = 128
SUBLANES = 16


norm_eps = 1e-06


def shifted(value, axis, by):
    length = lax.axis_size(axis)
    pairs = [(i, i + by) for i in range(length) if 0 <= i + by < length]
    return lax.ppermute(value, axis, pairs)


def normalize(token_rows, gain_row):
    widened = token_rows.astype(jnp.float32)
    inverse = lax.rsqrt(jnp.mean(widened * widened, axis=1, keepdims=True) + norm_eps)
    return (widened * inverse * gain_row).astype(jnp.bfloat16)


def routing_tables(normed, routing, router_cols, expert_count, slot_cap):
    logits = jnp.dot(normed, router_cols, preferred_element_type=jnp.float32)
    affinity = jax.nn.sigmoid(logits)
    weights = jnp.take_along_axis(affinity, routing, axis=1)
    flat_ids = routing.reshape(-1)
    onehot = (flat_ids[:, None] == jnp.arange(expert_count, dtype=jnp.int32)[None, :]).astype(
        jnp.int32
    )
    before = jnp.cumsum(onehot, axis=0) - onehot
    slot_ids = jnp.sum(before * onehot, axis=1).reshape(routing.shape)
    expert_hit = (
        routing[:, :, None] == jnp.arange(expert_count, dtype=jnp.int32)[None, None, :]
    ).astype(jnp.float32)
    slot_hit = (
        slot_ids[:, :, None] == jnp.arange(slot_cap, dtype=jnp.int32)[None, None, :]
    ).astype(jnp.float32)
    scatter_map = jnp.einsum("rke,rkc->ecr", expert_hit, slot_hit).astype(jnp.bfloat16)
    flat_slot = routing * slot_cap + slot_ids
    return (scatter_map, weights, flat_slot)


def run_experts(received, gate_cols, up_cols, down_rows):
    sources, slot_count, features = received.shape
    flat_rows = received.reshape(sources * slot_count, features)
    gate_pre = jnp.dot(flat_rows, gate_cols, preferred_element_type=jnp.float32)
    up_pre = jnp.dot(flat_rows, up_cols, preferred_element_type=jnp.float32)
    hidden = (jax.nn.silu(gate_pre) * up_pre).astype(jnp.bfloat16)
    partial_value = jnp.dot(hidden, down_rows, preferred_element_type=jnp.float32).astype(
        jnp.bfloat16
    )
    partial_value = partial_value.reshape(sources, slot_count, features)
    return lax.all_to_all(partial_value, "expert", split_axis=0, concat_axis=0, tiled=True)


def mix_rows(token_rows, weights, flat_slot, outputs):
    picked = outputs[flat_slot]
    return token_rows.astype(jnp.float32) + jnp.sum(weights[:, :, None] * picked, axis=1)


def grouped_shards(
    up_state,
    down_state,
    entering_up,
    entering_down,
    up_route,
    down_route,
    norm_gain,
    router,
    w_gate,
    w_up,
    w_down,
):
    gate_cols = w_gate[0]
    up_cols = w_up[0]
    down_rows = w_down[0]
    gain_row = norm_gain[0]
    router_cols = router[0]
    group_size = max(1, lax.axis_size("expert") // EXPERTS)
    expert_count = lax.axis_size("expert") // group_size
    segment_id = lax.axis_index("pipe")
    last_segment = lax.axis_size("pipe") - 1
    up_now = up_state[0]
    down_now = down_state[0]
    features = up_now.shape[1]
    slot_cap = up_now.shape[0] * TOP // expert_count
    up_done = up_now
    down_done = down_now
    for tick_id in range(TICKS):
        up_normed = normalize(up_now, gain_row)
        down_normed = normalize(down_now, gain_row)
        up_scatter, up_weights, up_slot = routing_tables(
            up_normed, up_route[tick_id, 0], router_cols, expert_count, slot_cap
        )
        down_scatter, down_weights, down_slot = routing_tables(
            down_normed, down_route[tick_id, 0], router_cols, expert_count, slot_cap
        )
        up_send = jnp.einsum(
            "ecr,rd->ecd", up_scatter, up_normed, preferred_element_type=jnp.float32
        ).astype(jnp.bfloat16)
        down_send = jnp.einsum(
            "ecr,rd->ecd", down_scatter, down_normed, preferred_element_type=jnp.float32
        ).astype(jnp.bfloat16)
        outbound = jnp.concatenate([up_send, down_send], axis=1)
        outgoing = jnp.broadcast_to(
            outbound[:, None], (expert_count, group_size, 2 * slot_cap, features)
        ).reshape(expert_count * group_size, 2 * slot_cap, features)
        returned = run_experts(
            lax.all_to_all(outgoing, "expert", split_axis=0, concat_axis=0, tiled=True),
            gate_cols,
            up_cols,
            down_rows,
        )
        summed = jnp.sum(
            returned.reshape(expert_count, group_size, 2 * slot_cap, features).astype(jnp.float32),
            axis=1,
        )
        up_outputs = summed[:, :slot_cap].reshape(expert_count * slot_cap, features)
        down_outputs = summed[:, slot_cap:].reshape(expert_count * slot_cap, features)
        up_done = mix_rows(up_now, up_weights, up_slot, up_outputs).astype(jnp.bfloat16)
        down_done = mix_rows(down_now, down_weights, down_slot, down_outputs).astype(jnp.bfloat16)
        if tick_id + 1 < TICKS:
            up_moved = shifted(up_done, "pipe", 1)
            down_moved = shifted(down_done, "pipe", -1)
            up_now = jnp.where(segment_id == 0, entering_up, up_moved)
            down_now = jnp.where(segment_id == last_segment, entering_down, down_moved)
    return (up_done[None], down_done[None])


def iota(shape, axis):
    return lax.broadcasted_iota(jnp.int32, shape, axis)


def chip_and_core():
    index = lax.axis_index("expert")
    return index // 2, index % 2


def one_hot(rows, target):
    return jnp.where(iota((rows, target.shape[1]), 0) == target, 1.0, 0.0)


def upright(ids):
    rows = ids.shape[1]
    diagonal = iota((rows, rows), 0) == iota((rows, rows), 1)
    return jnp.sum(jnp.where(diagonal, ids, 0), axis=1, keepdims=True)


def slots(first_ids, second_ids, parts):
    rows = first_ids.shape[1]
    width = 2 * rows * parts
    lane = iota((rows, width), 1)
    row = iota((rows, width), 0)
    own = lane % rows
    ids = jnp.where(lane // rows % 2 == 0, upright(first_ids), upright(second_ids))
    chosen = jnp.sum(jnp.where(row == own, ids, 0), axis=0, keepdims=True)
    rank = jnp.sum(jnp.where((ids == chosen) & (row < own), 1, 0), axis=0, keepdims=True)
    lane = iota((1, width), 1)
    return chosen, rank, lane // (2 * rows), lane // rows % 2


def sending_map(first_ids, second_ids, parts, slot_cap, span):
    chosen, rank, piece, group = slots(first_ids, second_ids, parts)
    chip, _ = chip_and_core()
    array = (chosen // 2) ^ chip ^ (span // (2 * SUBLANES) - 1)
    within = piece * (2 * slot_cap) + group * slot_cap + rank
    return one_hot(span, (array * 2 + chosen % 2) * SUBLANES + within)


def returning_map(up_ids, down_ids, parts, slot_cap, span):
    chosen, rank, piece, group = slots(up_ids, down_ids, parts)
    chip, core = chip_and_core()
    chips = span // (2 * SUBLANES)
    array = (chosen // 2) ^ chip ^ (chips - 1)
    array = array + jnp.where(chosen % 2 == core, 0, chips)
    sender = (lax.axis_index("pipe") + 1 + group) % 2
    within = piece * (2 * slot_cap) + sender * slot_cap + rank
    return one_hot(2 * span, (array * 2 + core) * SUBLANES + within)


def arriving_map(parts, slot_cap, span):
    wide = 2 * slot_cap
    _, core = chip_and_core()
    lane = iota((1, 2 * span), 1)
    array, to_core, within = lane // (2 * SUBLANES), lane // SUBLANES % 2, lane % SUBLANES
    row = within // wide * (span // parts) + array * wide + within % wide
    return one_hot(span, jnp.where(to_core == core, row, -1))


def relaying_map(parts, slot_cap, span):
    wide = 2 * slot_cap
    chips = span // (2 * SUBLANES)
    _, core = chip_and_core()
    lane = iota((1, span), 1)
    half = lane // (span // 2)
    array, within = lane % (span // 2) // SUBLANES, lane % SUBLANES
    piece, row = within // wide, within % wide
    array = array + jnp.where(row // slot_cap == core, 0, chips)
    way = (half + core + lax.axis_index("pipe")) % 2
    row = way * slot_cap + row % slot_cap
    return one_hot(span, piece * (span // parts) + array * wide + row)


def closing_map(parts, slot_cap, span):
    wide = 2 * slot_cap
    chips = span // (2 * SUBLANES)
    _, core = chip_and_core()
    lane = iota((1, span), 1)
    array, to_core, within = lane // (2 * SUBLANES), lane // SUBLANES % 2, lane % SUBLANES
    piece, row = within // wide, within % wide
    array = array + jnp.where(row // slot_cap == core, 0, chips)
    row = to_core * slot_cap + row % slot_cap
    return one_hot(span, piece * (span // parts) + array * wide + row)


def moved(onehot, rows):
    return jnp.dot(
        onehot.astype(jnp.bfloat16), rows, preferred_element_type=jnp.float32
    ).astype(jnp.bfloat16)


def stacked(refs):
    return jnp.concatenate([ref[...] for ref in refs], axis=0)


def put(value, refs):
    rows = refs[0].shape[0]
    for i, ref in enumerate(refs):
        ref[...] = value[i * rows : (i + 1) * rows]


def pack_rows(onehot, up_rows, down_rows, parts):
    width = up_rows.shape[1] // parts
    pieces = []
    for q in range(parts):
        pieces += [up_rows[:, q * width : (q + 1) * width], down_rows[:, q * width : (q + 1) * width]]
    return moved(onehot, jnp.concatenate(pieces, axis=0))


def started(sources, targets, sems, first=0):
    copies = [
        pltpu.make_async_copy(source, target, sems.at[first + i])
        for i, (source, target) in enumerate(zip(sources, targets))
    ]
    for copy in copies:
        copy.start()
    return copies


def cut(rows, count):
    step = rows // count
    return [pl.ds(i * step, step) for i in range(count)]


def prepare_kernel(
    parts,
    slot_cap,
    up,
    down,
    up_ids,
    down_ids,
    enter_up,
    enter_down,
    gain,
    router,
    w_gate,
    w_up,
    w_down,
    out_refs,
    aside_ref,
    back_ref,
    gain_v,
    router_v,
    up_v,
    down_v,
    enter_up_v,
    enter_down_v,
    up_i,
    down_i,
    cols_v,
    sems,
):
    sources = (up_ids, down_ids, up.at[0], down.at[0], router.at[0], gain, enter_up, enter_down)
    targets = (up_i, down_i, up_v, down_v, cols_v, gain_v, enter_up_v, enter_down_v)
    copies = started(sources, targets, sems)
    copies[0].wait()
    copies[1].wait()
    span = back_ref.shape[0]
    rows, features = up_v.shape
    width = features // parts
    sending = sending_map(up_i[0, 0], down_i[0, 0], parts, slot_cap, span)
    numbers = (iota((span, LANES), 0) % rows).astype(jnp.float32).astype(jnp.bfloat16)
    copies[2].wait()
    copies[3].wait()
    packed = pack_rows(sending, up_v[...], down_v[...], parts)
    put(packed, [ref.at[:, :width] for ref in out_refs])
    put(moved(sending, numbers), [ref.at[:, width:] for ref in out_refs])
    last = up_i.shape[0] - 1
    back_ref[...] = returning_map(up_i[last, 0], down_i[last, 0], parts, slot_cap, span).T.astype(jnp.bfloat16)
    ids = jnp.where(iota((rows, LANES), 0) == iota((rows, LANES), 1), 1, 0)
    up_line = jnp.sum(ids * upright(up_i[last, 0]), axis=0, keepdims=True)
    down_line = jnp.sum(ids * upright(down_i[last, 0]), axis=0, keepdims=True)
    row = iota((rows, LANES), 0)
    lines = jnp.where(row == 0, up_line, jnp.where(row == 1, down_line, 0))
    aside_ref[rows:] = jnp.zeros((rows, features), jnp.bfloat16)
    aside_ref[rows:, :LANES] = lines.astype(jnp.float32).astype(jnp.bfloat16)
    copies[4].wait()
    cols = cols_v[...].astype(jnp.float32)
    mine = iota(cols.shape, 0) == lax.axis_index("expert")
    router_v[...] = jnp.sum(jnp.where(mine, cols, 0.0), axis=0, keepdims=True)
    for copy in copies[5:]:
        copy.wait()
    aside_ref[:rows] = jnp.where(lax.axis_index("pipe") == 0, enter_up_v[...], enter_down_v[...])


def merge_kernel(kept_ref, passed_ref, out_refs):
    for j, ref in enumerate(out_refs):
        ref[:SUBLANES] = kept_ref[j * SUBLANES : (j + 1) * SUBLANES]
        ref[SUBLANES:] = passed_ref[j * SUBLANES : (j + 1) * SUBLANES]


def turn_kernel(parts, slot_cap, pipe, in_refs, aside_ref, other_ref, out_refs):
    section = lax.axis_index("pipe")
    _, core = chip_and_core()
    wide = 2 * slot_cap
    rows = aside_ref.shape[0] // 2
    width = out_refs[0].shape[1]
    span = sum(ref.shape[0] for ref in out_refs)
    own, other = aside_ref[...], other_ref[...]
    first = jnp.where(core == 0, own, other)
    second = jnp.where(core == 0, other, own)
    line = (section + core + 1) % 2
    picked = iota((rows, LANES), 0) == line

    def ids(aside):
        lines = jnp.where(picked, aside[rows:, :LANES].astype(jnp.float32), 0.0)
        return jnp.sum(lines, axis=0, keepdims=True)[:, :rows].astype(jnp.int32)

    sending = sending_map(ids(first), ids(second), parts, slot_cap, span)
    received = stacked(in_refs)
    numbers = received[:, width:].astype(jnp.float32).astype(jnp.int32)[:, :span]
    sublane = iota((span, span), 0)
    within = sublane % SUBLANES
    place = within // wide * (2 * rows) + within % wide // slot_cap * rows
    sorting = jnp.where(iota((span, span), 1) == place + numbers[:, :1], 1.0, 0.0).T
    sorted_rows = moved(sorting, received[:, :width])
    entering = []
    for q in range(parts):
        entering += [x[:rows, q * width : (q + 1) * width] for x in (first, second)]
    partner = ((section + core) ^ 1) - core
    enters = (partner < 0) | (partner >= pipe)
    sorted_rows = jnp.where(enters, jnp.concatenate(entering, axis=0), sorted_rows)
    put(moved(sending, sorted_rows), out_refs)


def unpack_kernel(in_refs, back_ref, up_ref, down_ref):
    rows = up_ref.shape[0]
    width = in_refs[0].shape[1]
    back = moved(back_ref[...], stacked(in_refs))
    for q in range(up_ref.shape[1] // width):
        up_ref[:, q * width : (q + 1) * width] = back[2 * q * rows : (2 * q + 1) * rows]
        down_ref[:, q * width : (q + 1) * width] = back[(2 * q + 1) * rows : (2 * q + 2) * rows]


def expert_rows(parts, slot_cap, in_refs, gain_ref, router_ref, x_ref, gates, ups, downs):
    span = in_refs[0].shape[0] * len(in_refs) // 2
    rows = span // parts
    width = x_ref.shape[1] // parts
    spread = moved(arriving_map(parts, slot_cap, span), stacked(in_refs))
    for q in range(parts):
        x_ref[:, q * width : (q + 1) * width] = spread[q * rows : (q + 1) * rows, :width]
    widened = x_ref[...].astype(jnp.float32)
    inverse = lax.rsqrt(jnp.mean(widened * widened, axis=1, keepdims=True) + norm_eps)
    normed = (widened * inverse * gain_ref[...]).astype(jnp.bfloat16)
    logit = jnp.sum(normed.astype(jnp.float32) * router_ref[...], axis=1, keepdims=True)
    weight = jax.nn.sigmoid(logit)

    def product(left, pieces):
        total, start = 0.0, 0
        for ref, copies in pieces:
            for copy in copies:
                copy.wait()
            part = left[:, start : start + ref.shape[0]]
            total += jnp.dot(part, ref[...], preferred_element_type=jnp.float32)
            start += ref.shape[0]
        return total

    gate_pre = product(normed, gates)
    hidden = (jax.nn.silu(gate_pre) * product(normed, ups)).astype(jnp.bfloat16)
    part = product(hidden, downs).astype(jnp.bfloat16).astype(jnp.float32)
    done = (x_ref[...].astype(jnp.float32) + weight * part).astype(jnp.bfloat16)
    done = jnp.concatenate([done[:, q * width : (q + 1) * width] for q in range(parts)], axis=0)
    return done, spread[:, width:]


def first_kernel(
    parts, slot_cap, in_refs, gain_ref, router_ref, gate_ref, up_ref, down_ref, kept_ref, passed_ref, x_ref
):
    done, numbers = expert_rows(
        parts, slot_cap, in_refs, gain_ref, router_ref, x_ref, [(gate_ref, [])], [(up_ref, [])], [(down_ref, [])]
    )
    onehot = relaying_map(parts, slot_cap, done.shape[0]).T
    put(moved(onehot, jnp.concatenate([done, numbers], axis=1)), (kept_ref, passed_ref))


def later_kernel(parts, slot_cap, in_refs, gain_ref, router_ref, gate_ref, up_ref, down_ref, out_refs, x_ref):
    done, _ = expert_rows(
        parts, slot_cap, in_refs, gain_ref, router_ref, x_ref, [(gate_ref, [])], [(up_ref, [])], [(down_ref, [])]
    )
    put(moved(closing_map(parts, slot_cap, done.shape[0]).T, done), out_refs)


VMEM_SPEC = pl.BlockSpec(memory_space=pltpu.VMEM)
HBM_SPEC = pl.BlockSpec(memory_space=pltpu.HBM)


def local_call(kernel, out_shapes, near, far=(), scratch=(), limit=8 << 20, cost=None):
    far = [pltpu.with_memory_space_constraint(x, pltpu.HBM) for x in far]
    close, near_tree = jax.tree.flatten(tuple(near))
    outs, out_tree = jax.tree.flatten(out_shapes)

    def body(*refs):
        refs = iter(refs)
        take = lambda count: [next(refs) for _ in range(count)]
        args = [*near_tree.unflatten(take(len(close))), *take(len(far))]
        results = out_tree.unflatten(take(len(outs)))
        kernel(*args, *(results if isinstance(results, tuple) else (results,)), *refs)

    results = pl.pallas_call(
        body,
        out_shape=outs,
        in_specs=[VMEM_SPEC] * len(close) + [HBM_SPEC] * len(far),
        out_specs=[VMEM_SPEC] * len(outs),
        scratch_shapes=list(scratch),
        compiler_params=pltpu.CompilerParams(vmem_limit_bytes=limit),
        cost_estimate=cost,
    )(*close, *far)
    return out_tree.unflatten(results)


def exchanged(arrays, beside=None):
    last = len(arrays) - 1
    devices = range(2 * len(arrays))
    arrived = [
        lax.ppermute(arrays[j], "expert", [(i, i ^ (2 * (last - j))) for i in devices])
        for j in range(last)
    ]
    if beside is not None:
        arrived, beside = lax.optimization_barrier((arrived, beside))
    arrived.append(arrays[last])
    passed = [lax.ppermute(x, "expert", [(i, i ^ 1) for i in devices]) for x in arrived]
    return tuple(arrived + passed), beside


def relay_pairs(k, pipe, experts):
    pairs = []
    for section in range(pipe):
        for i in range(experts):
            other = ((section + i % 2) ^ 1) - i % 2
            target = (other, i ^ (2 * k)) if 0 <= other < pipe else (section, i ^ (2 * (k or 1)))
            pairs.append((section * experts + i, target[0] * experts + target[1]))
    return pairs


EARLY_COPIES = 4
LATE_COPIES = 4
LOAD_COPIES = 4


def single_shards(
    up_state,
    down_state,
    entering_up,
    entering_down,
    up_route,
    down_route,
    norm_gain,
    router,
    w_gate,
    w_up,
    w_down,
):
    pipe = lax.axis_size("pipe")
    experts = lax.axis_size("expert")
    rows, features = up_state.shape[1:]
    hidden = w_gate.shape[2]
    slot_cap = rows * TOP // experts
    parts = SUBLANES // (2 * slot_cap)
    span = experts * SUBLANES
    chips = experts // 2
    width = features // parts
    early = features // 2
    numbered = (pltpu.VMEM((2 * SUBLANES, width + LANES), jnp.bfloat16),) * chips
    blocks = (pltpu.VMEM((2 * SUBLANES, width), jnp.bfloat16),) * chips
    half = pltpu.VMEM((span // 2, width + LANES), jnp.bfloat16)
    batch = pltpu.VMEM((rows, features), jnp.bfloat16)
    ids_v = pltpu.VMEM((TICKS, 1, 1, rows), jnp.int32)
    row_v = pltpu.VMEM((1, features), jnp.float32)
    x_v = pltpu.VMEM((span // parts, features), jnp.bfloat16)
    sibling = [(i, i ^ 1) for i in range(experts)]
    sent, aside, back, gain, column = local_call(
        functools.partial(prepare_kernel, parts, slot_cap),
        (
            numbered,
            pltpu.VMEM((2 * rows, features), jnp.bfloat16),
            pltpu.VMEM((span, 2 * span), jnp.bfloat16),
            row_v,
            row_v,
        ),
        (),
        (
            up_state,
            down_state,
            up_route.transpose(0, 1, 3, 2),
            down_route.transpose(0, 1, 3, 2),
            entering_up,
            entering_down,
            norm_gain,
            router.transpose(0, 2, 1),
            w_gate,
            w_up,
            w_down,
        ),
        [
            batch,
            batch,
            batch,
            batch,
            ids_v,
            ids_v,
            pltpu.VMEM(router.shape[:0:-1], router.dtype),
            pltpu.SemaphoreType.DMA((8,)),
        ],
    )
    received, _ = exchanged(sent)
    gate, up, down = w_gate[0], w_up[0], w_down[0]
    kept, passed = local_call(
        functools.partial(first_kernel, parts, slot_cap),
        (half, half),
        (received, gain, column, gate, up, down),
        (),
        [x_v],
    )
    other = lax.ppermute(aside, "expert", sibling)
    passed = lax.ppermute(passed, "expert", sibling)
    (merged,) = local_call(merge_kernel, (numbered,), (kept, passed))
    relayed = tuple(
        lax.ppermute(x, ("pipe", "expert"), relay_pairs(chips - 1 - j, pipe, experts))
        for j, x in enumerate(merged)
    )
    kernel = functools.partial(turn_kernel, parts, slot_cap, pipe)
    relayed = relayed[chips // 2 :] + relayed[: chips // 2]
    (sent,) = local_call(kernel, (blocks,), (relayed, aside, other))
    received, _ = exchanged(sent)
    kernel = functools.partial(later_kernel, parts, slot_cap)
    args = (received, gain, column, gate, up, down)
    (done,) = local_call(kernel, (blocks,), args, (), [x_v])
    batch = jax.ShapeDtypeStruct((rows, features), jnp.bfloat16)
    received, _ = exchanged(done)
    up_done, down_done = local_call(unpack_kernel, (batch, batch), (received, back))
    return (up_done[None], down_done[None])


def shards(*args):
    rows, features = args[0].shape[1:]
    experts = lax.axis_size("expert")
    slot_cap = rows * TOP // EXPERTS
    fits = experts == EXPERTS and rows % SUBLANES == 0 and SUBLANES % (2 * slot_cap) == 0
    fits = fits and TICKS == 2 and lax.axis_size("pipe") > 1
    fits = fits and features % (SUBLANES // (2 * slot_cap) * LANES) == 0
    return single_shards(*args) if fits else grouped_shards(*args)


def solution(mesh):
    return jax.shard_map(
        shards,
        mesh=mesh,
        in_specs=(
            P("pipe", "expert", None),
            P("pipe", "expert", None),
            P("expert", None),
            P("expert", None),
            P(None, "pipe", "expert", None),
            P(None, "pipe", "expert", None),
            P("pipe", None),
            P("pipe", None, None),
            P("pipe", None, "expert"),
            P("pipe", None, "expert"),
            P("pipe", "expert", None),
        ),
        out_specs=(P("pipe", "expert", None), P("pipe", "expert", None)),
        check_vma=False,
    )
```

```python
import functools

import jax
import jax.numpy as jnp
from jax import lax
from jax.experimental import pallas as pl
from jax.experimental.pallas import tpu as pltpu
from jax.sharding import PartitionSpec as P

TOP = 1
TICKS = 2
EXPERTS = 8
LANES = 128
SUBLANES = 16


norm_eps = 1e-06


def shifted(value, axis, by):
    length = lax.axis_size(axis)
    pairs = [(i, i + by) for i in range(length) if 0 <= i + by < length]
    return lax.ppermute(value, axis, pairs)


def normalize(token_rows, gain_row):
    widened = token_rows.astype(jnp.float32)
    inverse = lax.rsqrt(jnp.mean(widened * widened, axis=1, keepdims=True) + norm_eps)
    return (widened * inverse * gain_row).astype(jnp.bfloat16)


def routing_tables(normed, routing, router_cols, expert_count, slot_cap):
    logits = jnp.dot(normed, router_cols, preferred_element_type=jnp.float32)
    affinity = jax.nn.sigmoid(logits)
    weights = jnp.take_along_axis(affinity, routing, axis=1)
    flat_ids = routing.reshape(-1)
    onehot = (flat_ids[:, None] == jnp.arange(expert_count, dtype=jnp.int32)[None, :]).astype(
        jnp.int32
    )
    before = jnp.cumsum(onehot, axis=0) - onehot
    slot_ids = jnp.sum(before * onehot, axis=1).reshape(routing.shape)
    expert_hit = (
        routing[:, :, None] == jnp.arange(expert_count, dtype=jnp.int32)[None, None, :]
    ).astype(jnp.float32)
    slot_hit = (
        slot_ids[:, :, None] == jnp.arange(slot_cap, dtype=jnp.int32)[None, None, :]
    ).astype(jnp.float32)
    scatter_map = jnp.einsum("rke,rkc->ecr", expert_hit, slot_hit).astype(jnp.bfloat16)
    flat_slot = routing * slot_cap + slot_ids
    return (scatter_map, weights, flat_slot)


def run_experts(received, gate_cols, up_cols, down_rows):
    sources, slot_count, features = received.shape
    flat_rows = received.reshape(sources * slot_count, features)
    gate_pre = jnp.dot(flat_rows, gate_cols, preferred_element_type=jnp.float32)
    up_pre = jnp.dot(flat_rows, up_cols, preferred_element_type=jnp.float32)
    hidden = (jax.nn.silu(gate_pre) * up_pre).astype(jnp.bfloat16)
    partial_value = jnp.dot(hidden, down_rows, preferred_element_type=jnp.float32).astype(
        jnp.bfloat16
    )
    partial_value = partial_value.reshape(sources, slot_count, features)
    return lax.all_to_all(partial_value, "expert", split_axis=0, concat_axis=0, tiled=True)


def mix_rows(token_rows, weights, flat_slot, outputs):
    picked = outputs[flat_slot]
    return token_rows.astype(jnp.float32) + jnp.sum(weights[:, :, None] * picked, axis=1)


def grouped_shards(
    up_state,
    down_state,
    entering_up,
    entering_down,
    up_route,
    down_route,
    norm_gain,
    router,
    w_gate,
    w_up,
    w_down,
):
    gate_cols = w_gate[0]
    up_cols = w_up[0]
    down_rows = w_down[0]
    gain_row = norm_gain[0]
    router_cols = router[0]
    group_size = max(1, lax.axis_size("expert") // EXPERTS)
    expert_count = lax.axis_size("expert") // group_size
    segment_id = lax.axis_index("pipe")
    last_segment = lax.axis_size("pipe") - 1
    up_now = up_state[0]
    down_now = down_state[0]
    features = up_now.shape[1]
    slot_cap = up_now.shape[0] * TOP // expert_count
    up_done = up_now
    down_done = down_now
    for tick_id in range(TICKS):
        up_normed = normalize(up_now, gain_row)
        down_normed = normalize(down_now, gain_row)
        up_scatter, up_weights, up_slot = routing_tables(
            up_normed, up_route[tick_id, 0], router_cols, expert_count, slot_cap
        )
        down_scatter, down_weights, down_slot = routing_tables(
            down_normed, down_route[tick_id, 0], router_cols, expert_count, slot_cap
        )
        up_send = jnp.einsum(
            "ecr,rd->ecd", up_scatter, up_normed, preferred_element_type=jnp.float32
        ).astype(jnp.bfloat16)
        down_send = jnp.einsum(
            "ecr,rd->ecd", down_scatter, down_normed, preferred_element_type=jnp.float32
        ).astype(jnp.bfloat16)
        outbound = jnp.concatenate([up_send, down_send], axis=1)
        outgoing = jnp.broadcast_to(
            outbound[:, None], (expert_count, group_size, 2 * slot_cap, features)
        ).reshape(expert_count * group_size, 2 * slot_cap, features)
        returned = run_experts(
            lax.all_to_all(outgoing, "expert", split_axis=0, concat_axis=0, tiled=True),
            gate_cols,
            up_cols,
            down_rows,
        )
        summed = jnp.sum(
            returned.reshape(expert_count, group_size, 2 * slot_cap, features).astype(jnp.float32),
            axis=1,
        )
        up_outputs = summed[:, :slot_cap].reshape(expert_count * slot_cap, features)
        down_outputs = summed[:, slot_cap:].reshape(expert_count * slot_cap, features)
        up_done = mix_rows(up_now, up_weights, up_slot, up_outputs).astype(jnp.bfloat16)
        down_done = mix_rows(down_now, down_weights, down_slot, down_outputs).astype(jnp.bfloat16)
        if tick_id + 1 < TICKS:
            up_moved = shifted(up_done, "pipe", 1)
            down_moved = shifted(down_done, "pipe", -1)
            up_now = jnp.where(segment_id == 0, entering_up, up_moved)
            down_now = jnp.where(segment_id == last_segment, entering_down, down_moved)
    return (up_done[None], down_done[None])


def iota(shape, axis):
    return lax.broadcasted_iota(jnp.int32, shape, axis)


def chip_and_core():
    index = lax.axis_index("expert")
    return index // 2, index % 2


def one_hot(rows, target):
    return jnp.where(iota((rows, target.shape[1]), 0) == target, 1.0, 0.0)


def upright(ids):
    rows = ids.shape[1]
    diagonal = iota((rows, rows), 0) == iota((rows, rows), 1)
    return jnp.sum(jnp.where(diagonal, ids, 0), axis=1, keepdims=True)


def slots(first_ids, second_ids, parts):
    rows = first_ids.shape[1]
    width = 2 * rows * parts
    lane = iota((rows, width), 1)
    row = iota((rows, width), 0)
    own = lane % rows
    ids = jnp.where(lane // rows % 2 == 0, upright(first_ids), upright(second_ids))
    chosen = jnp.sum(jnp.where(row == own, ids, 0), axis=0, keepdims=True)
    rank = jnp.sum(jnp.where((ids == chosen) & (row < own), 1, 0), axis=0, keepdims=True)
    lane = iota((1, width), 1)
    return chosen, rank, lane // (2 * rows), lane // rows % 2


def sending_map(first_ids, second_ids, parts, slot_cap, span):
    chosen, rank, piece, group = slots(first_ids, second_ids, parts)
    chip, _ = chip_and_core()
    array = (chosen // 2) ^ chip ^ (span // (2 * SUBLANES) - 1)
    within = piece * (2 * slot_cap) + group * slot_cap + rank
    return one_hot(span, (array * 2 + chosen % 2) * SUBLANES + within)


def returning_map(up_ids, down_ids, parts, slot_cap, span):
    chosen, rank, piece, group = slots(up_ids, down_ids, parts)
    chip, core = chip_and_core()
    chips = span // (2 * SUBLANES)
    array = (chosen // 2) ^ chip ^ (chips - 1)
    array = array + jnp.where(chosen % 2 == core, 0, chips)
    sender = (lax.axis_index("pipe") + 1 + group) % 2
    within = piece * (2 * slot_cap) + sender * slot_cap + rank
    return one_hot(2 * span, (array * 2 + core) * SUBLANES + within)


def arriving_map(parts, slot_cap, span):
    wide = 2 * slot_cap
    _, core = chip_and_core()
    lane = iota((1, 2 * span), 1)
    array, to_core, within = lane // (2 * SUBLANES), lane // SUBLANES % 2, lane % SUBLANES
    row = within // wide * (span // parts) + array * wide + within % wide
    return one_hot(span, jnp.where(to_core == core, row, -1))


def relaying_map(parts, slot_cap, span):
    wide = 2 * slot_cap
    chips = span // (2 * SUBLANES)
    _, core = chip_and_core()
    lane = iota((1, span), 1)
    half = lane // (span // 2)
    array, within = lane % (span // 2) // SUBLANES, lane % SUBLANES
    piece, row = within // wide, within % wide
    array = array + jnp.where(row // slot_cap == core, 0, chips)
    way = (half + core + lax.axis_index("pipe")) % 2
    row = way * slot_cap + row % slot_cap
    return one_hot(span, piece * (span // parts) + array * wide + row)


def closing_map(parts, slot_cap, span):
    wide = 2 * slot_cap
    chips = span // (2 * SUBLANES)
    _, core = chip_and_core()
    lane = iota((1, span), 1)
    array, to_core, within = lane // (2 * SUBLANES), lane // SUBLANES % 2, lane % SUBLANES
    piece, row = within // wide, within % wide
    array = array + jnp.where(row // slot_cap == core, 0, chips)
    row = to_core * slot_cap + row % slot_cap
    return one_hot(span, piece * (span // parts) + array * wide + row)


def moved(onehot, rows):
    return jnp.dot(
        onehot.astype(jnp.bfloat16), rows, preferred_element_type=jnp.float32
    ).astype(jnp.bfloat16)


def stacked(refs):
    return jnp.concatenate([ref[...] for ref in refs], axis=0)


def put(value, refs):
    rows = refs[0].shape[0]
    for i, ref in enumerate(refs):
        ref[...] = value[i * rows : (i + 1) * rows]


def pack_rows(onehot, up_rows, down_rows, parts):
    width = up_rows.shape[1] // parts
    pieces = []
    for q in range(parts):
        pieces += [up_rows[:, q * width : (q + 1) * width], down_rows[:, q * width : (q + 1) * width]]
    return moved(onehot, jnp.concatenate(pieces, axis=0))


def started(sources, targets, sems, first=0):
    copies = [
        pltpu.make_async_copy(source, target, sems.at[first + i])
        for i, (source, target) in enumerate(zip(sources, targets))
    ]
    for copy in copies:
        copy.start()
    return copies


def send_kernel(
    parts,
    slot_cap,
    up,
    down,
    up_ids,
    down_ids,
    enter_up,
    enter_down,
    w_gate,
    w_up,
    w_down,
    out_refs,
    up_v,
    down_v,
    up_i,
    down_i,
    enter_up_v,
    enter_down_v,
    sems,
):
    del w_gate, w_up, w_down
    sources = (up_ids, down_ids, up.at[0], down.at[0], enter_up, enter_down)
    copies = started(sources, (up_i, down_i, up_v, down_v, enter_up_v, enter_down_v), sems)
    copies[0].wait()
    copies[1].wait()
    blocks = [ref.at[: 2 * SUBLANES] for ref in out_refs]
    span = 2 * SUBLANES * len(blocks)
    rows, features = up_v.shape
    width = features // parts
    sending = sending_map(up_i[0, 0], down_i[0, 0], parts, slot_cap, span)
    last = up_i.shape[0] - 1
    square = jnp.where(iota((rows, LANES), 0) == iota((rows, LANES), 1), 1, 0)
    up_line = jnp.sum(square * upright(up_i[last, 0]), axis=0, keepdims=True)
    down_line = jnp.sum(square * upright(down_i[last, 0]), axis=0, keepdims=True)
    row = iota((rows, LANES), 0)
    lines = jnp.where(row == 0, up_line, jnp.where(row == 1, down_line, 0))
    aside = out_refs[-1].at[2 * SUBLANES :]
    aside[parts * rows :, :LANES] = lines.astype(jnp.float32).astype(jnp.bfloat16)
    numbers = (iota((span, LANES), 0) % rows).astype(jnp.float32).astype(jnp.bfloat16)
    put(moved(sending, numbers), [ref.at[:, width:] for ref in blocks])
    copies[2].wait()
    copies[3].wait()
    packed = pack_rows(sending, up_v[...], down_v[...], parts)
    put(packed, [ref.at[:, :width] for ref in blocks])
    copies[4].wait()
    copies[5].wait()
    for q in range(parts):
        cols = slice(q * width, (q + 1) * width)
        entering = jnp.where(lax.axis_index("pipe") == 0, enter_up_v[:, cols], enter_down_v[:, cols])
        aside[q * rows : (q + 1) * rows, :width] = entering


def plan_kernel(
    parts,
    slot_cap,
    after_ref,
    up_ids,
    down_ids,
    gain,
    router,
    back_ref,
    arriving_ref,
    relaying_ref,
    closing_ref,
    gain_v,
    router_v,
    up_i,
    down_i,
    cols_v,
    sems,
):
    del after_ref
    last = up_ids.shape[0] - 1
    sources = (up_ids.at[last, 0], down_ids.at[last, 0], router.at[0], gain)
    copies = started(sources, (up_i, down_i, cols_v, gain_v), sems)
    span = back_ref.shape[0]
    arriving_ref[...] = arriving_map(parts, slot_cap, span).astype(jnp.bfloat16)
    relaying_ref[...] = relaying_map(parts, slot_cap, span).T.astype(jnp.bfloat16)
    closing_ref[...] = closing_map(parts, slot_cap, span).T.astype(jnp.bfloat16)
    copies[0].wait()
    copies[1].wait()
    back_ref[...] = returning_map(up_i[...], down_i[...], parts, slot_cap, span).T.astype(jnp.bfloat16)
    copies[2].wait()
    cols = cols_v[...].astype(jnp.float32)
    mine = iota(cols.shape, 0) == lax.axis_index("expert")
    router_v[...] = jnp.sum(jnp.where(mine, cols, 0.0), axis=0, keepdims=True)
    copies[3].wait()


def merge_kernel(kept_ref, passed_ref, out_refs):
    for j, ref in enumerate(out_refs):
        ref[:SUBLANES] = kept_ref[j * SUBLANES : (j + 1) * SUBLANES]
        ref[SUBLANES:] = passed_ref[j * SUBLANES : (j + 1) * SUBLANES]


def turn_plan_kernel(parts, slot_cap, own_ref, other_ref, sending_ref, entering_ref):
    section = lax.axis_index("pipe")
    _, core = chip_and_core()
    span, width = entering_ref.shape
    rows = span // (2 * parts)
    own, other = own_ref[2 * SUBLANES :], other_ref[2 * SUBLANES :]
    first = jnp.where(core == 0, own, other)
    second = jnp.where(core == 0, other, own)
    picked = iota((rows, LANES), 0) == (section + core + 1) % 2

    def ids(aside):
        lines = jnp.where(picked, aside[parts * rows :, :LANES].astype(jnp.float32), 0.0)
        return jnp.sum(lines, axis=0, keepdims=True)[:, :rows].astype(jnp.int32)

    sending = sending_map(ids(first), ids(second), parts, slot_cap, span)
    sending_ref[...] = sending.astype(jnp.bfloat16)
    pieces = []
    for q in range(parts):
        pieces += [x[q * rows : (q + 1) * rows, :width] for x in (first, second)]
    entering_ref[...] = moved(sending, jnp.concatenate(pieces, axis=0))


def turn_kernel(parts, slot_cap, pipe, in_refs, sending_ref, entering_ref, out_refs):
    section = lax.axis_index("pipe")
    _, core = chip_and_core()
    wide = 2 * slot_cap
    span, width = entering_ref.shape
    rows = span // (2 * parts)
    received = stacked(in_refs)
    numbers = received[:, width:].astype(jnp.float32).astype(jnp.int32)[:, :span]
    sublane = iota((span, span), 0)
    within = sublane % SUBLANES
    place = within // wide * (2 * rows) + within % wide // slot_cap * rows
    sorting = jnp.where(iota((span, span), 1) == place + numbers, 1.0, 0.0).astype(jnp.bfloat16)
    across = (((1,), (1,)), ((), ()))
    sending = lax.dot_general(sending_ref[...], sorting, across, preferred_element_type=jnp.float32)
    partner = ((section + core) ^ 1) - core
    enters = (partner < 0) | (partner >= pipe)
    put(jnp.where(enters, entering_ref[...], moved(sending, received[:, :width])), out_refs)


def unpack_kernel(in_refs, back_ref, up_ref, down_ref):
    rows = up_ref.shape[0]
    width = in_refs[0].shape[1]
    back = moved(back_ref[...], stacked(in_refs))
    for q in range(up_ref.shape[1] // width):
        up_ref[:, q * width : (q + 1) * width] = back[2 * q * rows : (2 * q + 1) * rows]
        down_ref[:, q * width : (q + 1) * width] = back[(2 * q + 1) * rows : (2 * q + 2) * rows]


MXU_ROWS = 128


def product(left, weight):
    rows = left.shape[0]
    spare = jnp.zeros((max(0, MXU_ROWS - rows), left.shape[1]), left.dtype)
    left = jnp.concatenate([left, spare], axis=0)
    return jnp.dot(left, weight, preferred_element_type=jnp.float32)[:rows]


def expert_rows(parts, in_refs, arriving_ref, gain_ref, router_ref, gate_ref, up_ref, down_ref, x_ref):
    rows = x_ref.shape[0]
    width = x_ref.shape[1] // parts
    spread = moved(arriving_ref[...], stacked([ref.at[: 2 * SUBLANES] for ref in in_refs]))
    for q in range(parts):
        x_ref[:, q * width : (q + 1) * width] = spread[q * rows : (q + 1) * rows, :width]
    widened = x_ref[...].astype(jnp.float32)
    inverse = lax.rsqrt(jnp.mean(widened * widened, axis=1, keepdims=True) + norm_eps)
    normed = (widened * inverse * gain_ref[...]).astype(jnp.bfloat16)
    logit = jnp.sum(normed.astype(jnp.float32) * router_ref[...], axis=1, keepdims=True)
    weight = jax.nn.sigmoid(logit)
    gate_pre = product(normed, gate_ref[...])
    hidden = (jax.nn.silu(gate_pre) * product(normed, up_ref[...])).astype(jnp.bfloat16)
    part = product(hidden, down_ref[...]).astype(jnp.bfloat16).astype(jnp.float32)
    done = (x_ref[...].astype(jnp.float32) + weight * part).astype(jnp.bfloat16)
    done = jnp.concatenate([done[:, q * width : (q + 1) * width] for q in range(parts)], axis=0)
    return done, spread[:, width:]


def first_kernel(parts, in_refs, leaving_ref, *refs):
    *ins, kept_ref, passed_ref, x_ref = refs
    done, numbers = expert_rows(parts, in_refs, *ins, x_ref)
    put(moved(leaving_ref[...], jnp.concatenate([done, numbers], axis=1)), (kept_ref, passed_ref))


def later_kernel(parts, in_refs, leaving_ref, *refs):
    *ins, out_refs, x_ref = refs
    done, _ = expert_rows(parts, in_refs, *ins, x_ref)
    put(moved(leaving_ref[...], done), out_refs)


VMEM_SPEC = pl.BlockSpec(memory_space=pltpu.VMEM)
HBM_SPEC = pl.BlockSpec(memory_space=pltpu.HBM)


def local_call(kernel, out_shapes, near, far=(), scratch=()):
    far = [pltpu.with_memory_space_constraint(x, pltpu.HBM) for x in far]
    close, near_tree = jax.tree.flatten(tuple(near))
    outs, out_tree = jax.tree.flatten(out_shapes)

    def body(*refs):
        refs = iter(refs)
        take = lambda count: [next(refs) for _ in range(count)]
        args = [*near_tree.unflatten(take(len(close))), *take(len(far))]
        results = out_tree.unflatten(take(len(outs)))
        kernel(*args, *(results if isinstance(results, tuple) else (results,)), *refs)

    results = pl.pallas_call(
        body,
        out_shape=outs,
        in_specs=[VMEM_SPEC] * len(close) + [HBM_SPEC] * len(far),
        out_specs=[VMEM_SPEC] * len(outs),
        scratch_shapes=list(scratch),
        compiler_params=pltpu.CompilerParams(vmem_limit_bytes=8 << 20),
    )(*close, *far)
    return out_tree.unflatten(results)


def exchanged(arrays):
    last = len(arrays) - 1
    devices = range(2 * len(arrays))
    arrived = [
        lax.ppermute(arrays[j], "expert", [(i, i ^ (2 * (last - j))) for i in devices])
        for j in range(last)
    ]
    arrived.append(arrays[last])
    passed = [lax.ppermute(x, "expert", [(i, i ^ 1) for i in devices]) for x in arrived]
    return tuple(arrived + passed)


def relay_pairs(k, pipe, experts):
    pairs = []
    for section in range(pipe):
        for i in range(experts):
            other = ((section + i % 2) ^ 1) - i % 2
            target = (other, i ^ (2 * k)) if 0 <= other < pipe else (section, i ^ (2 * (k or 1)))
            pairs.append((section * experts + i, target[0] * experts + target[1]))
    return pairs


def single_shards(
    up_state,
    down_state,
    entering_up,
    entering_down,
    up_route,
    down_route,
    norm_gain,
    router,
    w_gate,
    w_up,
    w_down,
):
    pipe = lax.axis_size("pipe")
    experts = lax.axis_size("expert")
    rows, features = up_state.shape[1:]
    slot_cap = rows * TOP // experts
    parts = SUBLANES // (2 * slot_cap)
    span = experts * SUBLANES
    chips = experts // 2
    width = features // parts
    numbered = (pltpu.VMEM((2 * SUBLANES, width + LANES), jnp.bfloat16),) * chips
    blocks = (pltpu.VMEM((2 * SUBLANES, width), jnp.bfloat16),) * chips
    half = pltpu.VMEM((span // 2, width + LANES), jnp.bfloat16)
    batch = pltpu.VMEM((rows, features), jnp.bfloat16)
    ids_v = pltpu.VMEM((1, rows), jnp.int32)
    all_ids_v = pltpu.VMEM((TICKS, 1, 1, rows), jnp.int32)
    row_v = pltpu.VMEM((1, features), jnp.float32)
    x_v = pltpu.VMEM((span // parts, features), jnp.bfloat16)
    map_v = pltpu.VMEM((span, span), jnp.bfloat16)
    wide_map_v = pltpu.VMEM((span, 2 * span), jnp.bfloat16)
    sibling = [(i, i ^ 1) for i in range(experts)]
    ids = (up_route.transpose(0, 1, 3, 2), down_route.transpose(0, 1, 3, 2))
    kept_back = pltpu.VMEM((2 * SUBLANES + (parts + 1) * rows, width + LANES), jnp.bfloat16)
    (sent,) = local_call(
        functools.partial(send_kernel, parts, slot_cap),
        (numbered[1:] + (kept_back,),),
        (),
        (up_state, down_state, *ids, entering_up, entering_down, w_gate, w_up, w_down),
        [batch, batch, all_ids_v, all_ids_v, batch, batch, pltpu.SemaphoreType.DMA((6,))],
    )
    back, arriving, relaying, closing, gain, column = local_call(
        functools.partial(plan_kernel, parts, slot_cap),
        (wide_map_v, wide_map_v, map_v, map_v, row_v, row_v),
        (sent[-1],),
        (*ids, norm_gain, router.transpose(0, 2, 1)),
        [ids_v, ids_v, pltpu.VMEM(router.shape[:0:-1], router.dtype), pltpu.SemaphoreType.DMA((4,))],
    )
    layer = (arriving, gain, column, w_gate[0], w_up[0], w_down[0])
    received = exchanged(sent)
    sending, entering = local_call(
        functools.partial(turn_plan_kernel, parts, slot_cap),
        (map_v, pltpu.VMEM((span, width), jnp.bfloat16)),
        (sent[-1], received[-1]),
    )
    kept, passed = local_call(
        functools.partial(first_kernel, parts),
        (half, half),
        (received, relaying, *layer),
        (),
        [x_v],
    )
    passed = lax.ppermute(passed, "expert", sibling)
    (merged,) = local_call(merge_kernel, (numbered,), (kept, passed))
    relayed = tuple(
        lax.ppermute(x, ("pipe", "expert"), relay_pairs(chips - 1 - j, pipe, experts))
        for j, x in enumerate(merged)
    )
    (sent,) = local_call(
        functools.partial(turn_kernel, parts, slot_cap, pipe), (blocks,), (relayed, sending, entering)
    )
    (done,) = local_call(
        functools.partial(later_kernel, parts),
        (blocks,),
        (exchanged(sent), closing, *layer),
        (),
        [x_v],
    )
    result = jax.ShapeDtypeStruct((rows, features), jnp.bfloat16)
    up_done, down_done = local_call(unpack_kernel, (result, result), (exchanged(done), back))
    return (up_done[None], down_done[None])


def shards(*args):
    rows, features = args[0].shape[1:]
    experts = lax.axis_size("expert")
    slot_cap = rows * TOP // EXPERTS
    fits = experts == EXPERTS and rows % SUBLANES == 0 and SUBLANES % (2 * slot_cap) == 0
    fits = fits and TICKS == 2 and lax.axis_size("pipe") > 1
    fits = fits and features % (SUBLANES // (2 * slot_cap) * LANES) == 0
    return single_shards(*args) if fits else grouped_shards(*args)


def solution(mesh):
    return jax.shard_map(
        shards,
        mesh=mesh,
        in_specs=(
            P("pipe", "expert", None),
            P("pipe", "expert", None),
            P("expert", None),
            P("expert", None),
            P(None, "pipe", "expert", None),
            P(None, "pipe", "expert", None),
            P("pipe", None),
            P("pipe", None, None),
            P("pipe", None, "expert"),
            P("pipe", None, "expert"),
            P("pipe", "expert", None),
        ),
        out_specs=(P("pipe", "expert", None), P("pipe", "expert", None)),
        check_vma=False,
    )
```

```python
import functools

import jax
import jax.numpy as jnp
from jax import lax
from jax.experimental import pallas as pl
from jax.experimental.pallas import tpu as pltpu
from jax.sharding import PartitionSpec as P

TOP = 1
TICKS = 2
EXPERTS = 8
LANES = 128
SUBLANES = 16


norm_eps = 1e-06


def shifted(value, axis, by):
    length = lax.axis_size(axis)
    pairs = [(i, i + by) for i in range(length) if 0 <= i + by < length]
    return lax.ppermute(value, axis, pairs)


def normalize(token_rows, gain_row):
    widened = token_rows.astype(jnp.float32)
    inverse = lax.rsqrt(jnp.mean(widened * widened, axis=1, keepdims=True) + norm_eps)
    return (widened * inverse * gain_row).astype(jnp.bfloat16)


def routing_tables(normed, routing, router_cols, expert_count, slot_cap):
    logits = jnp.dot(normed, router_cols, preferred_element_type=jnp.float32)
    affinity = jax.nn.sigmoid(logits)
    weights = jnp.take_along_axis(affinity, routing, axis=1)
    flat_ids = routing.reshape(-1)
    onehot = (flat_ids[:, None] == jnp.arange(expert_count, dtype=jnp.int32)[None, :]).astype(
        jnp.int32
    )
    before = jnp.cumsum(onehot, axis=0) - onehot
    slot_ids = jnp.sum(before * onehot, axis=1).reshape(routing.shape)
    expert_hit = (
        routing[:, :, None] == jnp.arange(expert_count, dtype=jnp.int32)[None, None, :]
    ).astype(jnp.float32)
    slot_hit = (
        slot_ids[:, :, None] == jnp.arange(slot_cap, dtype=jnp.int32)[None, None, :]
    ).astype(jnp.float32)
    scatter_map = jnp.einsum("rke,rkc->ecr", expert_hit, slot_hit).astype(jnp.bfloat16)
    flat_slot = routing * slot_cap + slot_ids
    return (scatter_map, weights, flat_slot)


def run_experts(received, gate_cols, up_cols, down_rows):
    sources, slot_count, features = received.shape
    flat_rows = received.reshape(sources * slot_count, features)
    gate_pre = jnp.dot(flat_rows, gate_cols, preferred_element_type=jnp.float32)
    up_pre = jnp.dot(flat_rows, up_cols, preferred_element_type=jnp.float32)
    hidden = (jax.nn.silu(gate_pre) * up_pre).astype(jnp.bfloat16)
    partial_value = jnp.dot(hidden, down_rows, preferred_element_type=jnp.float32).astype(
        jnp.bfloat16
    )
    partial_value = partial_value.reshape(sources, slot_count, features)
    return lax.all_to_all(partial_value, "expert", split_axis=0, concat_axis=0, tiled=True)


def mix_rows(token_rows, weights, flat_slot, outputs):
    picked = outputs[flat_slot]
    return token_rows.astype(jnp.float32) + jnp.sum(weights[:, :, None] * picked, axis=1)


def grouped_shards(
    up_state,
    down_state,
    entering_up,
    entering_down,
    up_route,
    down_route,
    norm_gain,
    router,
    w_gate,
    w_up,
    w_down,
):
    gate_cols = w_gate[0]
    up_cols = w_up[0]
    down_rows = w_down[0]
    gain_row = norm_gain[0]
    router_cols = router[0]
    group_size = max(1, lax.axis_size("expert") // EXPERTS)
    expert_count = lax.axis_size("expert") // group_size
    segment_id = lax.axis_index("pipe")
    last_segment = lax.axis_size("pipe") - 1
    up_now = up_state[0]
    down_now = down_state[0]
    features = up_now.shape[1]
    slot_cap = up_now.shape[0] * TOP // expert_count
    up_done = up_now
    down_done = down_now
    for tick_id in range(TICKS):
        up_normed = normalize(up_now, gain_row)
        down_normed = normalize(down_now, gain_row)
        up_scatter, up_weights, up_slot = routing_tables(
            up_normed, up_route[tick_id, 0], router_cols, expert_count, slot_cap
        )
        down_scatter, down_weights, down_slot = routing_tables(
            down_normed, down_route[tick_id, 0], router_cols, expert_count, slot_cap
        )
        up_send = jnp.einsum(
            "ecr,rd->ecd", up_scatter, up_normed, preferred_element_type=jnp.float32
        ).astype(jnp.bfloat16)
        down_send = jnp.einsum(
            "ecr,rd->ecd", down_scatter, down_normed, preferred_element_type=jnp.float32
        ).astype(jnp.bfloat16)
        outbound = jnp.concatenate([up_send, down_send], axis=1)
        outgoing = jnp.broadcast_to(
            outbound[:, None], (expert_count, group_size, 2 * slot_cap, features)
        ).reshape(expert_count * group_size, 2 * slot_cap, features)
        returned = run_experts(
            lax.all_to_all(outgoing, "expert", split_axis=0, concat_axis=0, tiled=True),
            gate_cols,
            up_cols,
            down_rows,
        )
        summed = jnp.sum(
            returned.reshape(expert_count, group_size, 2 * slot_cap, features).astype(jnp.float32),
            axis=1,
        )
        up_outputs = summed[:, :slot_cap].reshape(expert_count * slot_cap, features)
        down_outputs = summed[:, slot_cap:].reshape(expert_count * slot_cap, features)
        up_done = mix_rows(up_now, up_weights, up_slot, up_outputs).astype(jnp.bfloat16)
        down_done = mix_rows(down_now, down_weights, down_slot, down_outputs).astype(jnp.bfloat16)
        if tick_id + 1 < TICKS:
            up_moved = shifted(up_done, "pipe", 1)
            down_moved = shifted(down_done, "pipe", -1)
            up_now = jnp.where(segment_id == 0, entering_up, up_moved)
            down_now = jnp.where(segment_id == last_segment, entering_down, down_moved)
    return (up_done[None], down_done[None])


def iota(shape, axis):
    return lax.broadcasted_iota(jnp.int32, shape, axis)


def chip_and_core():
    index = lax.axis_index("expert")
    return index // 2, index % 2


def one_hot(rows, target):
    return jnp.where(iota((rows, target.shape[1]), 0) == target, 1.0, 0.0)


def upright(ids):
    rows = ids.shape[1]
    diagonal = iota((rows, rows), 0) == iota((rows, rows), 1)
    return jnp.sum(jnp.where(diagonal, ids, 0), axis=1, keepdims=True)


def slots(first_ids, second_ids, parts):
    rows = first_ids.shape[1]
    width = 2 * rows * parts
    lane = iota((rows, width), 1)
    row = iota((rows, width), 0)
    own = lane % rows
    ids = jnp.where(lane // rows % 2 == 0, upright(first_ids), upright(second_ids))
    chosen = jnp.sum(jnp.where(row == own, ids, 0), axis=0, keepdims=True)
    rank = jnp.sum(jnp.where((ids == chosen) & (row < own), 1, 0), axis=0, keepdims=True)
    lane = iota((1, width), 1)
    return chosen, rank, lane // (2 * rows), lane // rows % 2


def sending_map(first_ids, second_ids, parts, slot_cap, span):
    chosen, rank, piece, group = slots(first_ids, second_ids, parts)
    chip, _ = chip_and_core()
    array = (chosen // 2) ^ chip ^ (span // (2 * SUBLANES) - 1)
    within = piece * (2 * slot_cap) + group * slot_cap + rank
    return one_hot(span, (array * 2 + chosen % 2) * SUBLANES + within)


def returning_map(up_ids, down_ids, parts, slot_cap, span):
    chosen, rank, piece, group = slots(up_ids, down_ids, parts)
    chip, core = chip_and_core()
    chips = span // (2 * SUBLANES)
    array = (chosen // 2) ^ chip ^ (chips - 1)
    array = array + jnp.where(chosen % 2 == core, 0, chips)
    sender = (lax.axis_index("pipe") + group) % 2
    within = piece * (2 * slot_cap) + sender * slot_cap + rank
    return one_hot(2 * span, (array * 2 + core) * SUBLANES + within)


def arriving_map(parts, slot_cap, span):
    wide = 2 * slot_cap
    _, core = chip_and_core()
    lane = iota((1, 2 * span), 1)
    array, to_core, within = lane // (2 * SUBLANES), lane // SUBLANES % 2, lane % SUBLANES
    row = within // wide * (span // parts) + array * wide + within % wide
    return one_hot(span, jnp.where(to_core == core, row, -1))


def relaying_map(parts, slot_cap, span):
    wide = 2 * slot_cap
    chips = span // (2 * SUBLANES)
    _, core = chip_and_core()
    lane = iota((1, span), 1)
    half = lane // (span // 2)
    array, within = lane % (span // 2) // SUBLANES, lane % SUBLANES
    piece, row = within // wide, within % wide
    array = array + jnp.where(row // slot_cap == core, 0, chips)
    way = (half + core + lax.axis_index("pipe")) % 2
    row = way * slot_cap + row % slot_cap
    return one_hot(span, piece * (span // parts) + array * wide + row)


def closing_map(parts, slot_cap, span):
    wide = 2 * slot_cap
    chips = span // (2 * SUBLANES)
    _, core = chip_and_core()
    lane = iota((1, span), 1)
    array, to_core, within = lane // (2 * SUBLANES), lane // SUBLANES % 2, lane % SUBLANES
    piece, row = within // wide, within % wide
    array = array + jnp.where(row // slot_cap == core, 0, chips)
    row = to_core * slot_cap + row % slot_cap
    return one_hot(span, piece * (span // parts) + array * wide + row)


def moved(onehot, rows):
    return jnp.dot(
        onehot.astype(jnp.bfloat16), rows, preferred_element_type=jnp.float32
    ).astype(jnp.bfloat16)


def stacked(refs):
    return jnp.concatenate([ref[...] for ref in refs], axis=0)


def put(value, refs):
    rows = refs[0].shape[0]
    for i, ref in enumerate(refs):
        ref[...] = value[i * rows : (i + 1) * rows]


def pack_rows(onehot, up_rows, down_rows, parts):
    width = up_rows.shape[1] // parts
    pieces = []
    for q in range(parts):
        pieces += [up_rows[:, q * width : (q + 1) * width], down_rows[:, q * width : (q + 1) * width]]
    return moved(onehot, jnp.concatenate(pieces, axis=0))


def started(sources, targets, sems, first=0):
    copies = [
        pltpu.make_async_copy(source, target, sems.at[first + i])
        for i, (source, target) in enumerate(zip(sources, targets))
    ]
    for copy in copies:
        copy.start()
    return copies


def send_kernel(
    parts,
    slot_cap,
    up,
    down,
    up_ids,
    down_ids,
    enter_up,
    enter_down,
    w_gate,
    w_up,
    w_down,
    out_refs,
    aside_ref,
    up_v,
    down_v,
    up_i,
    down_i,
    enter_up_v,
    enter_down_v,
    sems,
):
    del w_gate, w_up, w_down
    sources = (up_ids, down_ids, up.at[0], down.at[0], enter_up, enter_down)
    copies = started(sources, (up_i, down_i, up_v, down_v, enter_up_v, enter_down_v), sems)
    copies[0].wait()
    copies[1].wait()
    span = sum(ref.shape[0] for ref in out_refs)
    rows, features = up_v.shape
    width = features // parts
    sending = sending_map(up_i[0, 0], down_i[0, 0], parts, slot_cap, span)
    last = up_i.shape[0] - 1
    square = jnp.where(iota((rows, LANES), 0) == iota((rows, LANES), 1), 1, 0)
    up_line = jnp.sum(square * upright(up_i[last, 0]), axis=0, keepdims=True)
    down_line = jnp.sum(square * upright(down_i[last, 0]), axis=0, keepdims=True)
    row = iota((rows, LANES), 0)
    lines = jnp.where(row == 0, up_line, jnp.where(row == 1, down_line, 0))
    aside_ref[parts * rows :, :LANES] = lines.astype(jnp.float32).astype(jnp.bfloat16)
    numbers = (iota((span, LANES), 0) % rows).astype(jnp.float32).astype(jnp.bfloat16)
    put(moved(sending, numbers), [ref.at[:, width:] for ref in out_refs])
    copies[2].wait()
    copies[3].wait()
    packed = pack_rows(sending, up_v[...], down_v[...], parts)
    put(packed, [ref.at[:, :width] for ref in out_refs])
    copies[4].wait()
    copies[5].wait()
    for q in range(parts):
        cols = slice(q * width, (q + 1) * width)
        entering = jnp.where(lax.axis_index("pipe") == 0, enter_up_v[:, cols], enter_down_v[:, cols])
        aside_ref[q * rows : (q + 1) * rows, :width] = entering


def plan_kernel(
    parts,
    slot_cap,
    after_ref,
    up_ids,
    down_ids,
    gain,
    router,
    back_ref,
    arriving_ref,
    relaying_ref,
    closing_ref,
    gain_v,
    router_v,
    up_i,
    down_i,
    cols_v,
    sems,
):
    del after_ref
    last = up_ids.shape[0] - 1
    sources = (up_ids.at[last, 0], down_ids.at[last, 0], router.at[0], gain)
    copies = started(sources, (up_i, down_i, cols_v, gain_v), sems)
    span = back_ref.shape[0]
    arriving_ref[...] = arriving_map(parts, slot_cap, span).astype(jnp.bfloat16)
    relaying_ref[...] = relaying_map(parts, slot_cap, span).T.astype(jnp.bfloat16)
    closing_ref[...] = closing_map(parts, slot_cap, span).T.astype(jnp.bfloat16)
    copies[0].wait()
    copies[1].wait()
    back_ref[...] = returning_map(up_i[...], down_i[...], parts, slot_cap, span).T.astype(jnp.bfloat16)
    copies[2].wait()
    cols = cols_v[...].astype(jnp.float32)
    mine = iota(cols.shape, 0) == lax.axis_index("expert")
    router_v[...] = jnp.sum(jnp.where(mine, cols, 0.0), axis=0, keepdims=True)
    copies[3].wait()


def merge_kernel(kept_ref, passed_ref, out_refs):
    for j, ref in enumerate(out_refs):
        ref[:SUBLANES] = kept_ref[j * SUBLANES : (j + 1) * SUBLANES]
        ref[SUBLANES:] = passed_ref[j * SUBLANES : (j + 1) * SUBLANES]


def turn_plan_kernel(parts, slot_cap, after_ref, own_ref, other_ref, sending_ref, entering_ref):
    del after_ref
    section = lax.axis_index("pipe")
    _, core = chip_and_core()
    span, width = entering_ref.shape
    rows = span // (2 * parts)
    own, other = own_ref[...], other_ref[...]
    first = jnp.where(core == 0, own, other)
    second = jnp.where(core == 0, other, own)
    picked = iota((rows, LANES), 0) == (section + core) % 2

    def ids(aside):
        lines = jnp.where(picked, aside[parts * rows :, :LANES].astype(jnp.float32), 0.0)
        return jnp.sum(lines, axis=0, keepdims=True)[:, :rows].astype(jnp.int32)

    sending = sending_map(ids(first), ids(second), parts, slot_cap, span)
    sending_ref[...] = sending.astype(jnp.bfloat16)
    pieces = []
    for q in range(parts):
        pieces += [x[q * rows : (q + 1) * rows, :width] for x in (first, second)]
    entering_ref[...] = moved(sending, jnp.concatenate(pieces, axis=0))


def turn_kernel(parts, slot_cap, pipe, in_refs, sending_ref, entering_ref, out_refs):
    section = lax.axis_index("pipe")
    _, core = chip_and_core()
    wide = 2 * slot_cap
    span, width = entering_ref.shape
    rows = span // (2 * parts)
    received = stacked(in_refs)
    numbers = received[:, width:].astype(jnp.float32).astype(jnp.int32)[:, :span]
    sublane = iota((span, span), 0)
    within = sublane % SUBLANES
    place = within // wide * (2 * rows) + within % wide // slot_cap * rows
    sorting = jnp.where(iota((span, span), 1) == place + numbers, 1.0, 0.0).astype(jnp.bfloat16)
    across = (((1,), (1,)), ((), ()))
    sending = lax.dot_general(sending_ref[...], sorting, across, preferred_element_type=jnp.float32)
    partner = ((section + 1 - core) ^ 1) - (1 - core)
    enters = (partner < 0) | (partner >= pipe)
    put(jnp.where(enters, entering_ref[...], moved(sending, received[:, :width])), out_refs)


def unpack_kernel(in_refs, back_ref, up_ref, down_ref):
    rows = up_ref.shape[0]
    width = in_refs[0].shape[1]
    back = moved(back_ref[...], stacked(in_refs))
    for q in range(up_ref.shape[1] // width):
        up_ref[:, q * width : (q + 1) * width] = back[2 * q * rows : (2 * q + 1) * rows]
        down_ref[:, q * width : (q + 1) * width] = back[(2 * q + 1) * rows : (2 * q + 2) * rows]


MXU_ROWS = 128


def product(left, weight):
    rows = left.shape[0]
    spare = jnp.zeros((max(0, MXU_ROWS - rows), left.shape[1]), left.dtype)
    left = jnp.concatenate([left, spare], axis=0)
    return jnp.dot(left, weight, preferred_element_type=jnp.float32)[:rows]


def expert_rows(parts, in_refs, arriving_ref, gain_ref, router_ref, gate_ref, up_ref, down_ref, x_ref):
    rows = x_ref.shape[0]
    width = x_ref.shape[1] // parts
    spread = moved(arriving_ref[...], stacked(in_refs))
    for q in range(parts):
        x_ref[:, q * width : (q + 1) * width] = spread[q * rows : (q + 1) * rows, :width]
    widened = x_ref[...].astype(jnp.float32)
    inverse = lax.rsqrt(jnp.mean(widened * widened, axis=1, keepdims=True) + norm_eps)
    normed = (widened * inverse * gain_ref[...]).astype(jnp.bfloat16)
    logit = jnp.sum(normed.astype(jnp.float32) * router_ref[...], axis=1, keepdims=True)
    weight = jax.nn.sigmoid(logit)
    gate_pre = product(normed, gate_ref[...])
    hidden = (jax.nn.silu(gate_pre) * product(normed, up_ref[...])).astype(jnp.bfloat16)
    part = product(hidden, down_ref[...]).astype(jnp.bfloat16).astype(jnp.float32)
    done = (x_ref[...].astype(jnp.float32) + weight * part).astype(jnp.bfloat16)
    done = jnp.concatenate([done[:, q * width : (q + 1) * width] for q in range(parts)], axis=0)
    return done, spread[:, width:]


def first_kernel(parts, in_refs, leaving_ref, *refs):
    *ins, kept_ref, passed_ref, x_ref = refs
    done, numbers = expert_rows(parts, in_refs, *ins, x_ref)
    put(moved(leaving_ref[...], jnp.concatenate([done, numbers], axis=1)), (kept_ref, passed_ref))


def later_kernel(parts, in_refs, leaving_ref, *refs):
    *ins, out_refs, x_ref = refs
    done, _ = expert_rows(parts, in_refs, *ins, x_ref)
    put(moved(leaving_ref[...], done), out_refs)


VMEM_SPEC = pl.BlockSpec(memory_space=pltpu.VMEM)
HBM_SPEC = pl.BlockSpec(memory_space=pltpu.HBM)


def local_call(kernel, out_shapes, near, far=(), scratch=()):
    far = [pltpu.with_memory_space_constraint(x, pltpu.HBM) for x in far]
    close, near_tree = jax.tree.flatten(tuple(near))
    outs, out_tree = jax.tree.flatten(out_shapes)

    def body(*refs):
        refs = iter(refs)
        take = lambda count: [next(refs) for _ in range(count)]
        args = [*near_tree.unflatten(take(len(close))), *take(len(far))]
        results = out_tree.unflatten(take(len(outs)))
        kernel(*args, *(results if isinstance(results, tuple) else (results,)), *refs)

    results = pl.pallas_call(
        body,
        out_shape=outs,
        in_specs=[VMEM_SPEC] * len(close) + [HBM_SPEC] * len(far),
        out_specs=[VMEM_SPEC] * len(outs),
        scratch_shapes=list(scratch),
        compiler_params=pltpu.CompilerParams(vmem_limit_bytes=8 << 20),
    )(*close, *far)
    return out_tree.unflatten(results)


def exchanged(arrays):
    last = len(arrays) - 1
    devices = range(2 * len(arrays))
    sibling = [(i, i ^ 1) for i in devices]
    arrived = [
        lax.ppermute(arrays[j], "expert", [(i, i ^ (2 * (last - j)) ^ 1) for i in devices])
        for j in range(last)
    ]
    passed = [lax.ppermute(x, "expert", sibling) for x in arrived + [arrays[last]]]
    return tuple(passed[:last] + [arrays[last]] + arrived + passed[last:])


def relay_pairs(k, pipe, experts):
    pairs = []
    for section in range(pipe):
        for i in range(experts):
            other = ((section + i % 2) ^ 1) - i % 2
            other = other if 0 <= other < pipe else section
            pairs.append((section * experts + i, other * experts + (i ^ (2 * k) ^ 1)))
    return pairs


def single_shards(
    up_state,
    down_state,
    entering_up,
    entering_down,
    up_route,
    down_route,
    norm_gain,
    router,
    w_gate,
    w_up,
    w_down,
):
    pipe = lax.axis_size("pipe")
    experts = lax.axis_size("expert")
    rows, features = up_state.shape[1:]
    slot_cap = rows * TOP // experts
    parts = SUBLANES // (2 * slot_cap)
    span = experts * SUBLANES
    chips = experts // 2
    width = features // parts
    numbered = (pltpu.VMEM((2 * SUBLANES, width + LANES), jnp.bfloat16),) * chips
    blocks = (pltpu.VMEM((2 * SUBLANES, width), jnp.bfloat16),) * chips
    half = pltpu.VMEM((span // 2, width + LANES), jnp.bfloat16)
    batch = pltpu.VMEM((rows, features), jnp.bfloat16)
    ids_v = pltpu.VMEM((1, rows), jnp.int32)
    all_ids_v = pltpu.VMEM((TICKS, 1, 1, rows), jnp.int32)
    row_v = pltpu.VMEM((1, features), jnp.float32)
    x_v = pltpu.VMEM((span // parts, features), jnp.bfloat16)
    map_v = pltpu.VMEM((span, span), jnp.bfloat16)
    wide_map_v = pltpu.VMEM((span, 2 * span), jnp.bfloat16)
    sibling = [(i, i ^ 1) for i in range(experts)]
    ids = (up_route.transpose(0, 1, 3, 2), down_route.transpose(0, 1, 3, 2))
    aside_v = pltpu.VMEM(((parts + 1) * rows, width), jnp.bfloat16)
    sent, aside = local_call(
        functools.partial(send_kernel, parts, slot_cap),
        (numbered, aside_v),
        (),
        (up_state, down_state, *ids, entering_up, entering_down, w_gate, w_up, w_down),
        [batch, batch, all_ids_v, all_ids_v, batch, batch, pltpu.SemaphoreType.DMA((6,))],
    )
    back, arriving, relaying, closing, gain, column = local_call(
        functools.partial(plan_kernel, parts, slot_cap),
        (wide_map_v, wide_map_v, map_v, map_v, row_v, row_v),
        (sent[-1],),
        (*ids, norm_gain, router.transpose(0, 2, 1)),
        [ids_v, ids_v, pltpu.VMEM(router.shape[:0:-1], router.dtype), pltpu.SemaphoreType.DMA((4,))],
    )
    layer = (arriving, gain, column, w_gate[0], w_up[0], w_down[0])
    received = exchanged(sent)
    kept, passed = local_call(
        functools.partial(first_kernel, parts),
        (half, half),
        (received, relaying, *layer),
        (),
        [x_v],
    )
    sending, entering = local_call(
        functools.partial(turn_plan_kernel, parts, slot_cap),
        (map_v, pltpu.VMEM((span, width), jnp.bfloat16)),
        (kept, aside, lax.ppermute(aside, "expert", sibling)),
    )
    passed = lax.ppermute(passed, "expert", sibling)
    (merged,) = local_call(merge_kernel, (numbered,), (kept, passed))
    relayed = tuple(
        lax.ppermute(x, ("pipe", "expert"), relay_pairs(chips - 1 - j, pipe, experts))
        for j, x in enumerate(merged)
    )
    relayed = relayed[chips // 2 :] + relayed[: chips // 2]
    (sent,) = local_call(
        functools.partial(turn_kernel, parts, slot_cap, pipe), (blocks,), (relayed, sending, entering)
    )
    (done,) = local_call(
        functools.partial(later_kernel, parts),
        (blocks,),
        (exchanged(sent), closing, *layer),
        (),
        [x_v],
    )
    result = jax.ShapeDtypeStruct((rows, features), jnp.bfloat16)
    up_done, down_done = local_call(unpack_kernel, (result, result), (exchanged(done), back))
    return (up_done[None], down_done[None])


def shards(*args):
    rows, features = args[0].shape[1:]
    experts = lax.axis_size("expert")
    slot_cap = rows * TOP // EXPERTS
    fits = experts == EXPERTS and rows % SUBLANES == 0 and SUBLANES % (2 * slot_cap) == 0
    fits = fits and TICKS == 2 and lax.axis_size("pipe") > 1
    fits = fits and features % (SUBLANES // (2 * slot_cap) * LANES) == 0
    return single_shards(*args) if fits else grouped_shards(*args)


def solution(mesh):
    return jax.shard_map(
        shards,
        mesh=mesh,
        in_specs=(
            P("pipe", "expert", None),
            P("pipe", "expert", None),
            P("expert", None),
            P("expert", None),
            P(None, "pipe", "expert", None),
            P(None, "pipe", "expert", None),
            P("pipe", None),
            P("pipe", None, None),
            P("pipe", None, "expert"),
            P("pipe", None, "expert"),
            P("pipe", "expert", None),
        ),
        out_specs=(P("pipe", "expert", None), P("pipe", "expert", None)),
        check_vma=False,
    )
```

```python
import functools

import jax
import jax.numpy as jnp
from jax import lax
from jax.experimental import pallas as pl
from jax.experimental.pallas import tpu as pltpu
from jax.sharding import PartitionSpec as P

TOP = 1
TICKS = 2
EXPERTS = 8
LANES = 128
SUBLANES = 16


norm_eps = 1e-06


def shifted(value, axis, by):
    length = lax.axis_size(axis)
    pairs = [(i, i + by) for i in range(length) if 0 <= i + by < length]
    return lax.ppermute(value, axis, pairs)


def normalize(token_rows, gain_row):
    widened = token_rows.astype(jnp.float32)
    inverse = lax.rsqrt(jnp.mean(widened * widened, axis=1, keepdims=True) + norm_eps)
    return (widened * inverse * gain_row).astype(jnp.bfloat16)


def routing_tables(normed, routing, router_cols, expert_count, slot_cap):
    logits = jnp.dot(normed, router_cols, preferred_element_type=jnp.float32)
    affinity = jax.nn.sigmoid(logits)
    weights = jnp.take_along_axis(affinity, routing, axis=1)
    flat_ids = routing.reshape(-1)
    onehot = (flat_ids[:, None] == jnp.arange(expert_count, dtype=jnp.int32)[None, :]).astype(
        jnp.int32
    )
    before = jnp.cumsum(onehot, axis=0) - onehot
    slot_ids = jnp.sum(before * onehot, axis=1).reshape(routing.shape)
    expert_hit = (
        routing[:, :, None] == jnp.arange(expert_count, dtype=jnp.int32)[None, None, :]
    ).astype(jnp.float32)
    slot_hit = (
        slot_ids[:, :, None] == jnp.arange(slot_cap, dtype=jnp.int32)[None, None, :]
    ).astype(jnp.float32)
    scatter_map = jnp.einsum("rke,rkc->ecr", expert_hit, slot_hit).astype(jnp.bfloat16)
    flat_slot = routing * slot_cap + slot_ids
    return (scatter_map, weights, flat_slot)


def run_experts(received, gate_cols, up_cols, down_rows):
    sources, slot_count, features = received.shape
    flat_rows = received.reshape(sources * slot_count, features)
    gate_pre = jnp.dot(flat_rows, gate_cols, preferred_element_type=jnp.float32)
    up_pre = jnp.dot(flat_rows, up_cols, preferred_element_type=jnp.float32)
    hidden = (jax.nn.silu(gate_pre) * up_pre).astype(jnp.bfloat16)
    partial_value = jnp.dot(hidden, down_rows, preferred_element_type=jnp.float32).astype(
        jnp.bfloat16
    )
    partial_value = partial_value.reshape(sources, slot_count, features)
    return lax.all_to_all(partial_value, "expert", split_axis=0, concat_axis=0, tiled=True)


def mix_rows(token_rows, weights, flat_slot, outputs):
    picked = outputs[flat_slot]
    return token_rows.astype(jnp.float32) + jnp.sum(weights[:, :, None] * picked, axis=1)


def grouped_shards(
    up_state,
    down_state,
    entering_up,
    entering_down,
    up_route,
    down_route,
    norm_gain,
    router,
    w_gate,
    w_up,
    w_down,
):
    gate_cols = w_gate[0]
    up_cols = w_up[0]
    down_rows = w_down[0]
    gain_row = norm_gain[0]
    router_cols = router[0]
    group_size = max(1, lax.axis_size("expert") // EXPERTS)
    expert_count = lax.axis_size("expert") // group_size
    segment_id = lax.axis_index("pipe")
    last_segment = lax.axis_size("pipe") - 1
    up_now = up_state[0]
    down_now = down_state[0]
    features = up_now.shape[1]
    slot_cap = up_now.shape[0] * TOP // expert_count
    up_done = up_now
    down_done = down_now
    for tick_id in range(TICKS):
        up_normed = normalize(up_now, gain_row)
        down_normed = normalize(down_now, gain_row)
        up_scatter, up_weights, up_slot = routing_tables(
            up_normed, up_route[tick_id, 0], router_cols, expert_count, slot_cap
        )
        down_scatter, down_weights, down_slot = routing_tables(
            down_normed, down_route[tick_id, 0], router_cols, expert_count, slot_cap
        )
        up_send = jnp.einsum(
            "ecr,rd->ecd", up_scatter, up_normed, preferred_element_type=jnp.float32
        ).astype(jnp.bfloat16)
        down_send = jnp.einsum(
            "ecr,rd->ecd", down_scatter, down_normed, preferred_element_type=jnp.float32
        ).astype(jnp.bfloat16)
        outbound = jnp.concatenate([up_send, down_send], axis=1)
        outgoing = jnp.broadcast_to(
            outbound[:, None], (expert_count, group_size, 2 * slot_cap, features)
        ).reshape(expert_count * group_size, 2 * slot_cap, features)
        returned = run_experts(
            lax.all_to_all(outgoing, "expert", split_axis=0, concat_axis=0, tiled=True),
            gate_cols,
            up_cols,
            down_rows,
        )
        summed = jnp.sum(
            returned.reshape(expert_count, group_size, 2 * slot_cap, features).astype(jnp.float32),
            axis=1,
        )
        up_outputs = summed[:, :slot_cap].reshape(expert_count * slot_cap, features)
        down_outputs = summed[:, slot_cap:].reshape(expert_count * slot_cap, features)
        up_done = mix_rows(up_now, up_weights, up_slot, up_outputs).astype(jnp.bfloat16)
        down_done = mix_rows(down_now, down_weights, down_slot, down_outputs).astype(jnp.bfloat16)
        if tick_id + 1 < TICKS:
            up_moved = shifted(up_done, "pipe", 1)
            down_moved = shifted(down_done, "pipe", -1)
            up_now = jnp.where(segment_id == 0, entering_up, up_moved)
            down_now = jnp.where(segment_id == last_segment, entering_down, down_moved)
    return (up_done[None], down_done[None])


def iota(shape, axis):
    return lax.broadcasted_iota(jnp.int32, shape, axis)


def chip_and_core():
    index = lax.axis_index("expert")
    return index // 2, index % 2


def one_hot(rows, target):
    return jnp.where(iota((rows, target.shape[1]), 0) == target, 1.0, 0.0)


def upright(ids):
    rows = ids.shape[1]
    diagonal = iota((rows, rows), 0) == iota((rows, rows), 1)
    return jnp.sum(jnp.where(diagonal, ids, 0), axis=1, keepdims=True)


def slots(first_ids, second_ids, parts):
    rows = first_ids.shape[1]
    width = 2 * rows * parts
    lane = iota((rows, width), 1)
    row = iota((rows, width), 0)
    own = lane % rows
    ids = jnp.where(lane // rows % 2 == 0, upright(first_ids), upright(second_ids))
    chosen = jnp.sum(jnp.where(row == own, ids, 0), axis=0, keepdims=True)
    rank = jnp.sum(jnp.where((ids == chosen) & (row < own), 1, 0), axis=0, keepdims=True)
    lane = iota((1, width), 1)
    return chosen, rank, lane // (2 * rows), lane // rows % 2


def sending_map(first_ids, second_ids, parts, slot_cap, span):
    chosen, rank, piece, group = slots(first_ids, second_ids, parts)
    chip, _ = chip_and_core()
    array = (chosen // 2) ^ chip ^ (span // (2 * SUBLANES) - 1)
    within = piece * (2 * slot_cap) + group * slot_cap + rank
    return one_hot(span, (array * 2 + chosen % 2) * SUBLANES + within)


def returning_map(up_ids, down_ids, parts, slot_cap, span):
    chosen, rank, piece, group = slots(up_ids, down_ids, parts)
    chip, core = chip_and_core()
    chips = span // (2 * SUBLANES)
    array = (chosen // 2) ^ chip ^ (chips - 1)
    array = array + jnp.where(chosen % 2 == core, 0, chips)
    within = piece * (2 * slot_cap) + (1 - group) * slot_cap + rank
    return one_hot(2 * span, (array * 2 + core) * SUBLANES + within)


def arriving_map(parts, slot_cap, span):
    wide = 2 * slot_cap
    _, core = chip_and_core()
    lane = iota((1, 2 * span), 1)
    array, to_core, within = lane // (2 * SUBLANES), lane // SUBLANES % 2, lane % SUBLANES
    row = within // wide * (span // parts) + array * wide + within % wide
    return one_hot(span, jnp.where(to_core == core, row, -1))


def relaying_map(parts, slot_cap, span):
    wide = 2 * slot_cap
    chips = span // (2 * SUBLANES)
    _, core = chip_and_core()
    lane = iota((1, span), 1)
    half = lane // (span // 2)
    array, within = lane % (span // 2) // SUBLANES, lane % SUBLANES
    piece, row = within // wide, within % wide
    array = array + jnp.where(row // slot_cap == core, 0, chips)
    way = (half + core) % 2
    row = way * slot_cap + row % slot_cap
    return one_hot(span, piece * (span // parts) + array * wide + row)


def closing_map(parts, slot_cap, span):
    wide = 2 * slot_cap
    chips = span // (2 * SUBLANES)
    _, core = chip_and_core()
    lane = iota((1, span), 1)
    array, to_core, within = lane // (2 * SUBLANES), lane // SUBLANES % 2, lane % SUBLANES
    piece, row = within // wide, within % wide
    array = array + jnp.where(row // slot_cap == core, 0, chips)
    row = to_core * slot_cap + row % slot_cap
    return one_hot(span, piece * (span // parts) + array * wide + row)


def moved(onehot, rows):
    return jnp.dot(
        onehot.astype(jnp.bfloat16), rows, preferred_element_type=jnp.float32
    ).astype(jnp.bfloat16)


def stacked(refs):
    return jnp.concatenate([ref[...] for ref in refs], axis=0)


def put(value, refs):
    rows = refs[0].shape[0]
    for i, ref in enumerate(refs):
        ref[...] = value[i * rows : (i + 1) * rows]


def pack_rows(onehot, up_rows, down_rows, parts):
    width = up_rows.shape[1] // parts
    pieces = []
    for q in range(parts):
        pieces += [up_rows[:, q * width : (q + 1) * width], down_rows[:, q * width : (q + 1) * width]]
    return moved(onehot, jnp.concatenate(pieces, axis=0))


def started(sources, targets, sems, first=0):
    copies = [
        pltpu.make_async_copy(source, target, sems.at[first + i])
        for i, (source, target) in enumerate(zip(sources, targets))
    ]
    for copy in copies:
        copy.start()
    return copies


def send_kernel(
    parts,
    slot_cap,
    up,
    down,
    up_ids,
    down_ids,
    enter_up,
    enter_down,
    w_gate,
    w_up,
    w_down,
    out_refs,
    aside_ref,
    up_v,
    down_v,
    up_i,
    down_i,
    enter_up_v,
    enter_down_v,
    sems,
):
    del w_gate, w_up, w_down
    sources = (up_ids, down_ids, up.at[0], down.at[0], enter_up, enter_down)
    copies = started(sources, (up_i, down_i, up_v, down_v, enter_up_v, enter_down_v), sems)
    copies[0].wait()
    copies[1].wait()
    span = sum(ref.shape[0] for ref in out_refs)
    rows, features = up_v.shape
    width = features // parts
    sending = sending_map(up_i[0, 0], down_i[0, 0], parts, slot_cap, span)
    last = up_i.shape[0] - 1
    square = jnp.where(iota((rows, LANES), 0) == iota((rows, LANES), 1), 1, 0)
    up_line = jnp.sum(square * upright(up_i[last, 0]), axis=0, keepdims=True)
    down_line = jnp.sum(square * upright(down_i[last, 0]), axis=0, keepdims=True)
    row = iota((rows, LANES), 0)
    lines = jnp.where(row == 0, up_line, jnp.where(row == 1, down_line, 0))
    aside_ref[parts * rows :, :LANES] = lines.astype(jnp.float32).astype(jnp.bfloat16)
    numbers = (iota((span, LANES), 0) % rows).astype(jnp.float32).astype(jnp.bfloat16)
    put(moved(sending, numbers), [ref.at[:, width:] for ref in out_refs])
    copies[2].wait()
    copies[3].wait()
    packed = pack_rows(sending, up_v[...], down_v[...], parts)
    put(packed, [ref.at[:, :width] for ref in out_refs])
    copies[4].wait()
    copies[5].wait()
    for q in range(parts):
        cols = slice(q * width, (q + 1) * width)
        entering = jnp.where(lax.axis_index("pipe") == 0, enter_up_v[:, cols], enter_down_v[:, cols])
        aside_ref[q * rows : (q + 1) * rows, :width] = entering


def plan_kernel(
    parts,
    slot_cap,
    after_ref,
    up_ids,
    down_ids,
    gain,
    router,
    back_ref,
    arriving_ref,
    relaying_ref,
    closing_ref,
    gain_v,
    router_v,
    up_i,
    down_i,
    cols_v,
    sems,
):
    del after_ref
    last = up_ids.shape[0] - 1
    sources = (up_ids.at[last, 0], down_ids.at[last, 0], router.at[0], gain)
    copies = started(sources, (up_i, down_i, cols_v, gain_v), sems)
    span = back_ref.shape[0]
    arriving_ref[...] = arriving_map(parts, slot_cap, span).astype(jnp.bfloat16)
    relaying_ref[...] = relaying_map(parts, slot_cap, span).T.astype(jnp.bfloat16)
    closing_ref[...] = closing_map(parts, slot_cap, span).T.astype(jnp.bfloat16)
    copies[0].wait()
    copies[1].wait()
    back_ref[...] = returning_map(up_i[...], down_i[...], parts, slot_cap, span).T.astype(jnp.bfloat16)
    copies[2].wait()
    cols = cols_v[...].astype(jnp.float32)
    mine = iota(cols.shape, 0) == lax.axis_index("expert")
    router_v[...] = jnp.sum(jnp.where(mine, cols, 0.0), axis=0, keepdims=True)
    copies[3].wait()


def merge_kernel(kept_ref, passed_ref, out_refs):
    for j, ref in enumerate(out_refs):
        ref[:SUBLANES] = kept_ref[j * SUBLANES : (j + 1) * SUBLANES]
        ref[SUBLANES:] = passed_ref[j * SUBLANES : (j + 1) * SUBLANES]


def turn_plan_kernel(parts, slot_cap, after_ref, own_ref, other_ref, sending_ref, entering_ref):
    del after_ref
    _, core = chip_and_core()
    span, width = entering_ref.shape
    rows = span // (2 * parts)
    own, other = own_ref[...], other_ref[...]
    first = jnp.where(core == 0, own, other)
    second = jnp.where(core == 0, other, own)
    picked = iota((rows, LANES), 0) == 1 - core

    def ids(aside):
        lines = jnp.where(picked, aside[parts * rows :, :LANES].astype(jnp.float32), 0.0)
        return jnp.sum(lines, axis=0, keepdims=True)[:, :rows].astype(jnp.int32)

    sending = sending_map(ids(first), ids(second), parts, slot_cap, span)
    sending_ref[...] = sending.astype(jnp.bfloat16)
    pieces = []
    for q in range(parts):
        pieces += [x[q * rows : (q + 1) * rows, :width] for x in (first, second)]
    entering_ref[...] = moved(sending, jnp.concatenate(pieces, axis=0))


def turn_kernel(parts, slot_cap, pipe, in_refs, sending_ref, entering_ref, out_refs):
    section = lax.axis_index("pipe")
    _, core = chip_and_core()
    wide = 2 * slot_cap
    span, width = entering_ref.shape
    rows = span // (2 * parts)
    received = stacked(in_refs)
    numbers = received[:, width:].astype(jnp.float32).astype(jnp.int32)[:, :span]
    sublane = iota((span, span), 0)
    within = sublane % SUBLANES
    place = within // wide * (2 * rows) + within % wide // slot_cap * rows
    sorting = jnp.where(iota((span, span), 1) == place + numbers, 1.0, 0.0).astype(jnp.bfloat16)
    across = (((1,), (1,)), ((), ()))
    sending = lax.dot_general(sending_ref[...], sorting, across, preferred_element_type=jnp.float32)
    enters = section == jnp.where(core == 0, pipe - 1, 0)
    put(jnp.where(enters, entering_ref[...], moved(sending, received[:, :width])), out_refs)


def unpack_kernel(in_refs, back_ref, up_ref, down_ref):
    rows = up_ref.shape[0]
    width = in_refs[0].shape[1]
    back = moved(back_ref[...], stacked(in_refs))
    for q in range(up_ref.shape[1] // width):
        up_ref[:, q * width : (q + 1) * width] = back[2 * q * rows : (2 * q + 1) * rows]
        down_ref[:, q * width : (q + 1) * width] = back[(2 * q + 1) * rows : (2 * q + 2) * rows]


MXU_ROWS = 128


def product(left, weight):
    rows = left.shape[0]
    spare = jnp.zeros((max(0, MXU_ROWS - rows), left.shape[1]), left.dtype)
    left = jnp.concatenate([left, spare], axis=0)
    return jnp.dot(left, weight, preferred_element_type=jnp.float32)[:rows]


def expert_rows(parts, in_refs, arriving_ref, gain_ref, router_ref, gate_ref, up_ref, down_ref, x_ref):
    rows = x_ref.shape[0]
    width = x_ref.shape[1] // parts
    spread = moved(arriving_ref[...], stacked(in_refs))
    for q in range(parts):
        x_ref[:, q * width : (q + 1) * width] = spread[q * rows : (q + 1) * rows, :width]
    widened = x_ref[...].astype(jnp.float32)
    inverse = lax.rsqrt(jnp.mean(widened * widened, axis=1, keepdims=True) + norm_eps)
    normed = (widened * inverse * gain_ref[...]).astype(jnp.bfloat16)
    logit = jnp.sum(normed.astype(jnp.float32) * router_ref[...], axis=1, keepdims=True)
    weight = jax.nn.sigmoid(logit)
    gate_pre = product(normed, gate_ref[...])
    hidden = (jax.nn.silu(gate_pre) * product(normed, up_ref[...])).astype(jnp.bfloat16)
    part = product(hidden, down_ref[...]).astype(jnp.bfloat16).astype(jnp.float32)
    done = (x_ref[...].astype(jnp.float32) + weight * part).astype(jnp.bfloat16)
    done = jnp.concatenate([done[:, q * width : (q + 1) * width] for q in range(parts)], axis=0)
    return done, spread[:, width:]


def first_kernel(parts, in_refs, leaving_ref, *refs):
    *ins, kept_ref, passed_ref, x_ref = refs
    done, numbers = expert_rows(parts, in_refs, *ins, x_ref)
    put(moved(leaving_ref[...], jnp.concatenate([done, numbers], axis=1)), (kept_ref, passed_ref))


def later_kernel(parts, in_refs, leaving_ref, *refs):
    *ins, out_refs, x_ref = refs
    done, _ = expert_rows(parts, in_refs, *ins, x_ref)
    put(moved(leaving_ref[...], done), out_refs)


VMEM_SPEC = pl.BlockSpec(memory_space=pltpu.VMEM)
HBM_SPEC = pl.BlockSpec(memory_space=pltpu.HBM)


def local_call(kernel, out_shapes, near, far=(), scratch=()):
    far = [pltpu.with_memory_space_constraint(x, pltpu.HBM) for x in far]
    close, near_tree = jax.tree.flatten(tuple(near))
    outs, out_tree = jax.tree.flatten(out_shapes)

    def body(*refs):
        refs = iter(refs)
        take = lambda count: [next(refs) for _ in range(count)]
        args = [*near_tree.unflatten(take(len(close))), *take(len(far))]
        results = out_tree.unflatten(take(len(outs)))
        kernel(*args, *(results if isinstance(results, tuple) else (results,)), *refs)

    results = pl.pallas_call(
        body,
        out_shape=outs,
        in_specs=[VMEM_SPEC] * len(close) + [HBM_SPEC] * len(far),
        out_specs=[VMEM_SPEC] * len(outs),
        scratch_shapes=list(scratch),
        compiler_params=pltpu.CompilerParams(vmem_limit_bytes=8 << 20),
    )(*close, *far)
    return out_tree.unflatten(results)


def exchanged(arrays):
    last = len(arrays) - 1
    devices = range(2 * len(arrays))
    sibling = [(i, i ^ 1) for i in devices]
    arrived = [
        lax.ppermute(arrays[j], "expert", [(i, i ^ (2 * (last - j)) ^ 1) for i in devices])
        for j in range(last)
    ]
    passed = [lax.ppermute(x, "expert", sibling) for x in arrived + [arrays[last]]]
    return tuple(passed[:last] + [arrays[last]] + arrived + passed[last:])


def relay_pairs(k, pipe, experts):
    pairs = []
    for section in range(pipe):
        for i in range(experts):
            other = section + 1 - 2 * (i % 2)
            target = (other, i ^ (2 * k) ^ 1) if 0 <= other < pipe else (section, i ^ (2 * (k or 1)))
            pairs.append((section * experts + i, target[0] * experts + target[1]))
    return pairs


def single_shards(
    up_state,
    down_state,
    entering_up,
    entering_down,
    up_route,
    down_route,
    norm_gain,
    router,
    w_gate,
    w_up,
    w_down,
):
    pipe = lax.axis_size("pipe")
    experts = lax.axis_size("expert")
    rows, features = up_state.shape[1:]
    slot_cap = rows * TOP // experts
    parts = SUBLANES // (2 * slot_cap)
    span = experts * SUBLANES
    chips = experts // 2
    width = features // parts
    numbered = (pltpu.VMEM((2 * SUBLANES, width + LANES), jnp.bfloat16),) * chips
    blocks = (pltpu.VMEM((2 * SUBLANES, width), jnp.bfloat16),) * chips
    half = pltpu.VMEM((span // 2, width + LANES), jnp.bfloat16)
    batch = pltpu.VMEM((rows, features), jnp.bfloat16)
    ids_v = pltpu.VMEM((1, rows), jnp.int32)
    all_ids_v = pltpu.VMEM((TICKS, 1, 1, rows), jnp.int32)
    row_v = pltpu.VMEM((1, features), jnp.float32)
    x_v = pltpu.VMEM((span // parts, features), jnp.bfloat16)
    map_v = pltpu.VMEM((span, span), jnp.bfloat16)
    wide_map_v = pltpu.VMEM((span, 2 * span), jnp.bfloat16)
    sibling = [(i, i ^ 1) for i in range(experts)]
    ids = (up_route.transpose(0, 1, 3, 2), down_route.transpose(0, 1, 3, 2))
    aside_v = pltpu.VMEM(((parts + 1) * rows, width), jnp.bfloat16)
    sent, aside = local_call(
        functools.partial(send_kernel, parts, slot_cap),
        (numbered, aside_v),
        (),
        (up_state, down_state, *ids, entering_up, entering_down, w_gate, w_up, w_down),
        [batch, batch, all_ids_v, all_ids_v, batch, batch, pltpu.SemaphoreType.DMA((6,))],
    )
    back, arriving, relaying, closing, gain, column = local_call(
        functools.partial(plan_kernel, parts, slot_cap),
        (wide_map_v, wide_map_v, map_v, map_v, row_v, row_v),
        (sent[-1],),
        (*ids, norm_gain, router.transpose(0, 2, 1)),
        [ids_v, ids_v, pltpu.VMEM(router.shape[:0:-1], router.dtype), pltpu.SemaphoreType.DMA((4,))],
    )
    layer = (arriving, gain, column, w_gate[0], w_up[0], w_down[0])
    received = exchanged(sent)
    kept, passed = local_call(
        functools.partial(first_kernel, parts),
        (half, half),
        (received, relaying, *layer),
        (),
        [x_v],
    )
    sending, entering = local_call(
        functools.partial(turn_plan_kernel, parts, slot_cap),
        (map_v, pltpu.VMEM((span, width), jnp.bfloat16)),
        (kept, aside, lax.ppermute(aside, "expert", sibling)),
    )
    passed = lax.ppermute(passed, "expert", sibling)
    (merged,) = local_call(merge_kernel, (numbered,), (kept, passed))
    relayed = tuple(
        lax.ppermute(x, ("pipe", "expert"), relay_pairs(chips - 1 - j, pipe, experts))
        for j, x in enumerate(merged)
    )
    relayed = relayed[chips // 2 :] + relayed[: chips // 2]
    (sent,) = local_call(
        functools.partial(turn_kernel, parts, slot_cap, pipe), (blocks,), (relayed, sending, entering)
    )
    (done,) = local_call(
        functools.partial(later_kernel, parts),
        (blocks,),
        (exchanged(sent), closing, *layer),
        (),
        [x_v],
    )
    result = jax.ShapeDtypeStruct((rows, features), jnp.bfloat16)
    up_done, down_done = local_call(unpack_kernel, (result, result), (exchanged(done), back))
    return (up_done[None], down_done[None])


def shards(*args):
    rows, features = args[0].shape[1:]
    experts = lax.axis_size("expert")
    slot_cap = rows * TOP // EXPERTS
    fits = experts == EXPERTS and rows % SUBLANES == 0 and SUBLANES % (2 * slot_cap) == 0
    fits = fits and TICKS == 2 and lax.axis_size("pipe") > 1
    fits = fits and features % (SUBLANES // (2 * slot_cap) * LANES) == 0
    return single_shards(*args) if fits else grouped_shards(*args)


def solution(mesh):
    return jax.shard_map(
        shards,
        mesh=mesh,
        in_specs=(
            P("pipe", "expert", None),
            P("pipe", "expert", None),
            P("expert", None),
            P("expert", None),
            P(None, "pipe", "expert", None),
            P(None, "pipe", "expert", None),
            P("pipe", None),
            P("pipe", None, None),
            P("pipe", None, "expert"),
            P("pipe", None, "expert"),
            P("pipe", "expert", None),
        ),
        out_specs=(P("pipe", "expert", None), P("pipe", "expert", None)),
        check_vma=False,
    )
```

```python
import functools

import jax
import jax.numpy as jnp
from jax import lax
from jax.experimental import pallas as pl
from jax.experimental.pallas import tpu as pltpu
from jax.sharding import PartitionSpec as P

TOP = 1
TICKS = 2
EXPERTS = 8
LANES = 128
SUBLANES = 16


norm_eps = 1e-06


def shifted(value, axis, by):
    length = lax.axis_size(axis)
    pairs = [(i, i + by) for i in range(length) if 0 <= i + by < length]
    return lax.ppermute(value, axis, pairs)


def normalize(token_rows, gain_row):
    widened = token_rows.astype(jnp.float32)
    inverse = lax.rsqrt(jnp.mean(widened * widened, axis=1, keepdims=True) + norm_eps)
    return (widened * inverse * gain_row).astype(jnp.bfloat16)


def routing_tables(normed, routing, router_cols, expert_count, slot_cap):
    logits = jnp.dot(normed, router_cols, preferred_element_type=jnp.float32)
    affinity = jax.nn.sigmoid(logits)
    weights = jnp.take_along_axis(affinity, routing, axis=1)
    flat_ids = routing.reshape(-1)
    onehot = (flat_ids[:, None] == jnp.arange(expert_count, dtype=jnp.int32)[None, :]).astype(
        jnp.int32
    )
    before = jnp.cumsum(onehot, axis=0) - onehot
    slot_ids = jnp.sum(before * onehot, axis=1).reshape(routing.shape)
    expert_hit = (
        routing[:, :, None] == jnp.arange(expert_count, dtype=jnp.int32)[None, None, :]
    ).astype(jnp.float32)
    slot_hit = (
        slot_ids[:, :, None] == jnp.arange(slot_cap, dtype=jnp.int32)[None, None, :]
    ).astype(jnp.float32)
    scatter_map = jnp.einsum("rke,rkc->ecr", expert_hit, slot_hit).astype(jnp.bfloat16)
    flat_slot = routing * slot_cap + slot_ids
    return (scatter_map, weights, flat_slot)


def run_experts(received, gate_cols, up_cols, down_rows):
    sources, slot_count, features = received.shape
    flat_rows = received.reshape(sources * slot_count, features)
    gate_pre = jnp.dot(flat_rows, gate_cols, preferred_element_type=jnp.float32)
    up_pre = jnp.dot(flat_rows, up_cols, preferred_element_type=jnp.float32)
    hidden = (jax.nn.silu(gate_pre) * up_pre).astype(jnp.bfloat16)
    partial_value = jnp.dot(hidden, down_rows, preferred_element_type=jnp.float32).astype(
        jnp.bfloat16
    )
    partial_value = partial_value.reshape(sources, slot_count, features)
    return lax.all_to_all(partial_value, "expert", split_axis=0, concat_axis=0, tiled=True)


def mix_rows(token_rows, weights, flat_slot, outputs):
    picked = outputs[flat_slot]
    return token_rows.astype(jnp.float32) + jnp.sum(weights[:, :, None] * picked, axis=1)


def grouped_shards(
    up_state,
    down_state,
    entering_up,
    entering_down,
    up_route,
    down_route,
    norm_gain,
    router,
    w_gate,
    w_up,
    w_down,
):
    gate_cols = w_gate[0]
    up_cols = w_up[0]
    down_rows = w_down[0]
    gain_row = norm_gain[0]
    router_cols = router[0]
    group_size = max(1, lax.axis_size("expert") // EXPERTS)
    expert_count = lax.axis_size("expert") // group_size
    segment_id = lax.axis_index("pipe")
    last_segment = lax.axis_size("pipe") - 1
    up_now = up_state[0]
    down_now = down_state[0]
    features = up_now.shape[1]
    slot_cap = up_now.shape[0] * TOP // expert_count
    up_done = up_now
    down_done = down_now
    for tick_id in range(TICKS):
        up_normed = normalize(up_now, gain_row)
        down_normed = normalize(down_now, gain_row)
        up_scatter, up_weights, up_slot = routing_tables(
            up_normed, up_route[tick_id, 0], router_cols, expert_count, slot_cap
        )
        down_scatter, down_weights, down_slot = routing_tables(
            down_normed, down_route[tick_id, 0], router_cols, expert_count, slot_cap
        )
        up_send = jnp.einsum(
            "ecr,rd->ecd", up_scatter, up_normed, preferred_element_type=jnp.float32
        ).astype(jnp.bfloat16)
        down_send = jnp.einsum(
            "ecr,rd->ecd", down_scatter, down_normed, preferred_element_type=jnp.float32
        ).astype(jnp.bfloat16)
        outbound = jnp.concatenate([up_send, down_send], axis=1)
        outgoing = jnp.broadcast_to(
            outbound[:, None], (expert_count, group_size, 2 * slot_cap, features)
        ).reshape(expert_count * group_size, 2 * slot_cap, features)
        returned = run_experts(
            lax.all_to_all(outgoing, "expert", split_axis=0, concat_axis=0, tiled=True),
            gate_cols,
            up_cols,
            down_rows,
        )
        summed = jnp.sum(
            returned.reshape(expert_count, group_size, 2 * slot_cap, features).astype(jnp.float32),
            axis=1,
        )
        up_outputs = summed[:, :slot_cap].reshape(expert_count * slot_cap, features)
        down_outputs = summed[:, slot_cap:].reshape(expert_count * slot_cap, features)
        up_done = mix_rows(up_now, up_weights, up_slot, up_outputs).astype(jnp.bfloat16)
        down_done = mix_rows(down_now, down_weights, down_slot, down_outputs).astype(jnp.bfloat16)
        if tick_id + 1 < TICKS:
            up_moved = shifted(up_done, "pipe", 1)
            down_moved = shifted(down_done, "pipe", -1)
            up_now = jnp.where(segment_id == 0, entering_up, up_moved)
            down_now = jnp.where(segment_id == last_segment, entering_down, down_moved)
    return (up_done[None], down_done[None])


def iota(shape, axis):
    return lax.broadcasted_iota(jnp.int32, shape, axis)


def chip_and_core():
    index = lax.axis_index("expert")
    return index // 2, index % 2


def one_hot(rows, target):
    return jnp.where(iota((rows, target.shape[1]), 0) == target, 1.0, 0.0)


def upright(ids):
    rows = ids.shape[1]
    diagonal = iota((rows, rows), 0) == iota((rows, rows), 1)
    return jnp.sum(jnp.where(diagonal, ids, 0), axis=1, keepdims=True)


def slots(first_ids, second_ids, parts):
    rows = first_ids.shape[1]
    width = 2 * rows * parts
    lane = iota((rows, width), 1)
    row = iota((rows, width), 0)
    own = lane % rows
    ids = jnp.where(lane // rows % 2 == 0, upright(first_ids), upright(second_ids))
    chosen = jnp.sum(jnp.where(row == own, ids, 0), axis=0, keepdims=True)
    rank = jnp.sum(jnp.where((ids == chosen) & (row < own), 1, 0), axis=0, keepdims=True)
    lane = iota((1, width), 1)
    return chosen, rank, lane // (2 * rows), lane // rows % 2


def sending_map(first_ids, second_ids, parts, slot_cap, span):
    chosen, rank, piece, group = slots(first_ids, second_ids, parts)
    chip, _ = chip_and_core()
    array = (chosen // 2) ^ chip ^ (span // (2 * SUBLANES) - 1)
    within = piece * (2 * slot_cap) + group * slot_cap + rank
    return one_hot(span, (array * 2 + chosen % 2) * SUBLANES + within)


def returning_map(up_ids, down_ids, parts, slot_cap, span):
    chosen, rank, piece, group = slots(up_ids, down_ids, parts)
    chip, core = chip_and_core()
    chips = span // (2 * SUBLANES)
    array = (chosen // 2) ^ chip ^ (chips - 1)
    array = array + jnp.where(chosen % 2 == core, 0, chips)
    within = piece * (2 * slot_cap) + (1 - group) * slot_cap + rank
    return one_hot(2 * span, (array * 2 + core) * SUBLANES + within)


def arriving_map(parts, slot_cap, span):
    wide = 2 * slot_cap
    _, core = chip_and_core()
    lane = iota((1, 2 * span), 1)
    array, to_core, within = lane // (2 * SUBLANES), lane // SUBLANES % 2, lane % SUBLANES
    row = within // wide * (span // parts) + array * wide + within % wide
    return one_hot(span, jnp.where(to_core == core, row, -1))


def relaying_map(parts, slot_cap, span):
    wide = 2 * slot_cap
    chips = span // (2 * SUBLANES)
    _, core = chip_and_core()
    lane = iota((1, span), 1)
    half = lane // (span // 2)
    array, within = lane % (span // 2) // SUBLANES, lane % SUBLANES
    piece, row = within // wide, within % wide
    array = array + jnp.where(row // slot_cap == core, 0, chips)
    way = (half + core) % 2
    row = way * slot_cap + row % slot_cap
    return one_hot(span, piece * (span // parts) + array * wide + row)


def closing_map(parts, slot_cap, span):
    wide = 2 * slot_cap
    chips = span // (2 * SUBLANES)
    _, core = chip_and_core()
    lane = iota((1, span), 1)
    array, to_core, within = lane // (2 * SUBLANES), lane // SUBLANES % 2, lane % SUBLANES
    piece, row = within // wide, within % wide
    array = array + jnp.where(row // slot_cap == core, 0, chips)
    row = to_core * slot_cap + row % slot_cap
    return one_hot(span, piece * (span // parts) + array * wide + row)


def moved(onehot, rows):
    return jnp.dot(
        onehot.astype(jnp.bfloat16), rows, preferred_element_type=jnp.float32
    ).astype(jnp.bfloat16)


def stacked(refs):
    return jnp.concatenate([ref[...] for ref in refs], axis=0)


def put(value, refs):
    rows = refs[0].shape[0]
    for i, ref in enumerate(refs):
        ref[...] = value[i * rows : (i + 1) * rows]


def pack_rows(onehot, up_rows, down_rows, parts):
    width = up_rows.shape[1] // parts
    pieces = []
    for q in range(parts):
        pieces += [up_rows[:, q * width : (q + 1) * width], down_rows[:, q * width : (q + 1) * width]]
    return moved(onehot, jnp.concatenate(pieces, axis=0))


def started(sources, targets, sems, first=0):
    copies = [
        pltpu.make_async_copy(source, target, sems.at[first + i])
        for i, (source, target) in enumerate(zip(sources, targets))
    ]
    for copy in copies:
        copy.start()
    return copies


def send_kernel(
    parts,
    slot_cap,
    up,
    down,
    up_ids,
    down_ids,
    enter_up,
    enter_down,
    w_gate,
    w_up,
    w_down,
    out_refs,
    aside_ref,
    up_v,
    down_v,
    up_i,
    down_i,
    enter_up_v,
    enter_down_v,
    sems,
):
    del w_gate, w_up, w_down
    sources = (up_ids, down_ids, up.at[0], down.at[0], enter_up, enter_down)
    copies = started(sources, (up_i, down_i, up_v, down_v, enter_up_v, enter_down_v), sems)
    copies[0].wait()
    copies[1].wait()
    span = sum(ref.shape[0] for ref in out_refs)
    rows, features = up_v.shape
    width = features // parts
    sending = sending_map(up_i[0, 0], down_i[0, 0], parts, slot_cap, span)
    last = up_i.shape[0] - 1
    square = jnp.where(iota((rows, LANES), 0) == iota((rows, LANES), 1), 1, 0)
    up_line = jnp.sum(square * upright(up_i[last, 0]), axis=0, keepdims=True)
    down_line = jnp.sum(square * upright(down_i[last, 0]), axis=0, keepdims=True)
    row = iota((rows, LANES), 0)
    lines = jnp.where(row == 0, up_line, jnp.where(row == 1, down_line, 0))
    aside_ref[parts * rows :, :LANES] = lines.astype(jnp.float32).astype(jnp.bfloat16)
    numbers = (iota((span, LANES), 0) % rows).astype(jnp.float32).astype(jnp.bfloat16)
    put(moved(sending, numbers), [ref.at[:, width:] for ref in out_refs])
    copies[2].wait()
    copies[3].wait()
    packed = pack_rows(sending, up_v[...], down_v[...], parts)
    put(packed, [ref.at[:, :width] for ref in out_refs])
    copies[4].wait()
    copies[5].wait()
    for q in range(parts):
        cols = slice(q * width, (q + 1) * width)
        entering = jnp.where(lax.axis_index("pipe") == 0, enter_up_v[:, cols], enter_down_v[:, cols])
        aside_ref[q * rows : (q + 1) * rows, :width] = entering


def plan_kernel(
    parts,
    slot_cap,
    after_ref,
    up_ids,
    down_ids,
    gain,
    router,
    back_ref,
    arriving_ref,
    relaying_ref,
    closing_ref,
    gain_v,
    router_v,
    up_i,
    down_i,
    cols_v,
    sems,
):
    del after_ref
    last = up_ids.shape[0] - 1
    sources = (up_ids.at[last, 0], down_ids.at[last, 0], router.at[0], gain)
    copies = started(sources, (up_i, down_i, cols_v, gain_v), sems)
    span = back_ref.shape[0]
    arriving_ref[...] = arriving_map(parts, slot_cap, span).astype(jnp.bfloat16)
    relaying_ref[...] = relaying_map(parts, slot_cap, span).T.astype(jnp.bfloat16)
    closing_ref[...] = closing_map(parts, slot_cap, span).T.astype(jnp.bfloat16)
    copies[0].wait()
    copies[1].wait()
    back_ref[...] = returning_map(up_i[...], down_i[...], parts, slot_cap, span).T.astype(jnp.bfloat16)
    copies[2].wait()
    cols = cols_v[...].astype(jnp.float32)
    mine = iota(cols.shape, 0) == lax.axis_index("expert")
    router_v[...] = jnp.sum(jnp.where(mine, cols, 0.0), axis=0, keepdims=True)
    copies[3].wait()


def merge_kernel(kept_ref, passed_ref, out_refs):
    for j, ref in enumerate(out_refs):
        ref[:SUBLANES] = kept_ref[j * SUBLANES : (j + 1) * SUBLANES]
        ref[SUBLANES:] = passed_ref[j * SUBLANES : (j + 1) * SUBLANES]


def turn_plan_kernel(parts, slot_cap, after_ref, own_ref, other_ref, sending_ref, entering_ref):
    del after_ref
    _, core = chip_and_core()
    span, width = entering_ref.shape
    rows = span // (2 * parts)
    own, other = own_ref[...], other_ref[...]
    first = jnp.where(core == 0, own, other)
    second = jnp.where(core == 0, other, own)
    picked = iota((rows, LANES), 0) == 1 - core

    def ids(aside):
        lines = jnp.where(picked, aside[parts * rows :, :LANES].astype(jnp.float32), 0.0)
        return jnp.sum(lines, axis=0, keepdims=True)[:, :rows].astype(jnp.int32)

    sending = sending_map(ids(first), ids(second), parts, slot_cap, span)
    sending_ref[...] = sending.astype(jnp.bfloat16)
    pieces = []
    for q in range(parts):
        pieces += [x[q * rows : (q + 1) * rows, :width] for x in (first, second)]
    entering_ref[...] = moved(sending, jnp.concatenate(pieces, axis=0))


def turn_kernel(parts, slot_cap, pipe, in_refs, sending_ref, entering_ref, out_refs):
    section = lax.axis_index("pipe")
    _, core = chip_and_core()
    wide = 2 * slot_cap
    span, width = entering_ref.shape
    rows = span // (2 * parts)
    received = stacked(in_refs)
    numbers = received[:, width:].astype(jnp.float32).astype(jnp.int32)[:, :span]
    sublane = iota((span, span), 0)
    within = sublane % SUBLANES
    place = within // wide * (2 * rows) + within % wide // slot_cap * rows
    sorting = jnp.where(iota((span, span), 1) == place + numbers, 1.0, 0.0).astype(jnp.bfloat16)
    across = (((1,), (1,)), ((), ()))
    sending = lax.dot_general(sending_ref[...], sorting, across, preferred_element_type=jnp.float32)
    enters = section == jnp.where(core == 0, pipe - 1, 0)
    put(jnp.where(enters, entering_ref[...], moved(sending, received[:, :width])), out_refs)


def unpack_kernel(in_refs, back_ref, up_ref, down_ref):
    rows = up_ref.shape[0]
    width = in_refs[0].shape[1]
    back = moved(back_ref[...], stacked(in_refs))
    for q in range(up_ref.shape[1] // width):
        up_ref[:, q * width : (q + 1) * width] = back[2 * q * rows : (2 * q + 1) * rows]
        down_ref[:, q * width : (q + 1) * width] = back[(2 * q + 1) * rows : (2 * q + 2) * rows]


MXU_ROWS = 128


def product(left, weight):
    rows = left.shape[0]
    spare = jnp.zeros((max(0, MXU_ROWS - rows), left.shape[1]), left.dtype)
    left = jnp.concatenate([left, spare], axis=0)
    return jnp.dot(left, weight, preferred_element_type=jnp.float32)[:rows]


def expert_rows(parts, in_refs, arriving_ref, gain_ref, router_ref, gate_ref, up_ref, down_ref, x_ref):
    rows = x_ref.shape[0]
    width = x_ref.shape[1] // parts
    spread = moved(arriving_ref[...], stacked(in_refs))
    for q in range(parts):
        x_ref[:, q * width : (q + 1) * width] = spread[q * rows : (q + 1) * rows, :width]
    widened = x_ref[...].astype(jnp.float32)
    inverse = lax.rsqrt(jnp.mean(widened * widened, axis=1, keepdims=True) + norm_eps)
    normed = (widened * inverse * gain_ref[...]).astype(jnp.bfloat16)
    logit = jnp.sum(normed.astype(jnp.float32) * router_ref[...], axis=1, keepdims=True)
    weight = jax.nn.sigmoid(logit)
    gate_pre = product(normed, gate_ref[...])
    hidden = (jax.nn.silu(gate_pre) * product(normed, up_ref[...])).astype(jnp.bfloat16)
    part = product(hidden, down_ref[...]).astype(jnp.bfloat16).astype(jnp.float32)
    done = (x_ref[...].astype(jnp.float32) + weight * part).astype(jnp.bfloat16)
    done = jnp.concatenate([done[:, q * width : (q + 1) * width] for q in range(parts)], axis=0)
    return done, spread[:, width:]


def first_kernel(parts, in_refs, leaving_ref, *refs):
    *ins, kept_ref, passed_ref, x_ref = refs
    done, numbers = expert_rows(parts, in_refs, *ins, x_ref)
    put(moved(leaving_ref[...], jnp.concatenate([done, numbers], axis=1)), (kept_ref, passed_ref))


def later_kernel(parts, in_refs, leaving_ref, *refs):
    *ins, out_refs, x_ref = refs
    done, _ = expert_rows(parts, in_refs, *ins, x_ref)
    put(moved(leaving_ref[...], done), out_refs)


VMEM_SPEC = pl.BlockSpec(memory_space=pltpu.VMEM)
HBM_SPEC = pl.BlockSpec(memory_space=pltpu.HBM)


def local_call(kernel, out_shapes, near, far=(), scratch=()):
    far = [pltpu.with_memory_space_constraint(x, pltpu.HBM) for x in far]
    close, near_tree = jax.tree.flatten(tuple(near))
    outs, out_tree = jax.tree.flatten(out_shapes)

    def body(*refs):
        refs = iter(refs)
        take = lambda count: [next(refs) for _ in range(count)]
        args = [*near_tree.unflatten(take(len(close))), *take(len(far))]
        results = out_tree.unflatten(take(len(outs)))
        kernel(*args, *(results if isinstance(results, tuple) else (results,)), *refs)

    results = pl.pallas_call(
        body,
        out_shape=outs,
        in_specs=[VMEM_SPEC] * len(close) + [HBM_SPEC] * len(far),
        out_specs=[VMEM_SPEC] * len(outs),
        scratch_shapes=list(scratch),
        compiler_params=pltpu.CompilerParams(vmem_limit_bytes=8 << 20),
    )(*close, *far)
    return out_tree.unflatten(results)


def exchanged(arrays):
    last = len(arrays) - 1
    devices = range(2 * len(arrays))

    def sent(value, flip):
        return lax.ppermute(value, "expert", [(i, i ^ flip) for i in devices])

    arrived = [sent(x, 2 * (last - j) + 1) for j, x in enumerate(arrays[:last])]
    passed = [sent(x, 1) for x in arrived[:-1]] + [sent(arrays[last - 1], 2)]
    return (*passed, arrays[last], *arrived, sent(arrays[last], 1))


def relay_pairs(k, pipe, experts):
    pairs = []
    for section in range(pipe):
        for i in range(experts):
            other = section + 1 - 2 * (i % 2)
            target = (other, i ^ (2 * k) ^ 1) if 0 <= other < pipe else (section, i ^ (2 * (k or 1)))
            pairs.append((section * experts + i, target[0] * experts + target[1]))
    return pairs


def single_shards(
    up_state,
    down_state,
    entering_up,
    entering_down,
    up_route,
    down_route,
    norm_gain,
    router,
    w_gate,
    w_up,
    w_down,
):
    pipe = lax.axis_size("pipe")
    experts = lax.axis_size("expert")
    rows, features = up_state.shape[1:]
    slot_cap = rows * TOP // experts
    parts = SUBLANES // (2 * slot_cap)
    span = experts * SUBLANES
    chips = experts // 2
    width = features // parts
    numbered = (pltpu.VMEM((2 * SUBLANES, width + LANES), jnp.bfloat16),) * chips
    blocks = (pltpu.VMEM((2 * SUBLANES, width), jnp.bfloat16),) * chips
    half = pltpu.VMEM((span // 2, width + LANES), jnp.bfloat16)
    batch = pltpu.VMEM((rows, features), jnp.bfloat16)
    ids_v = pltpu.VMEM((1, rows), jnp.int32)
    all_ids_v = pltpu.VMEM((TICKS, 1, 1, rows), jnp.int32)
    row_v = pltpu.VMEM((1, features), jnp.float32)
    x_v = pltpu.VMEM((span // parts, features), jnp.bfloat16)
    map_v = pltpu.VMEM((span, span), jnp.bfloat16)
    wide_map_v = pltpu.VMEM((span, 2 * span), jnp.bfloat16)
    sibling = [(i, i ^ 1) for i in range(experts)]
    ids = (up_route.transpose(0, 1, 3, 2), down_route.transpose(0, 1, 3, 2))
    aside_v = pltpu.VMEM(((parts + 1) * rows, width), jnp.bfloat16)
    sent, aside = local_call(
        functools.partial(send_kernel, parts, slot_cap),
        (numbered, aside_v),
        (),
        (up_state, down_state, *ids, entering_up, entering_down, w_gate, w_up, w_down),
        [batch, batch, all_ids_v, all_ids_v, batch, batch, pltpu.SemaphoreType.DMA((6,))],
    )
    back, arriving, relaying, closing, gain, column = local_call(
        functools.partial(plan_kernel, parts, slot_cap),
        (wide_map_v, wide_map_v, map_v, map_v, row_v, row_v),
        (sent[-1],),
        (*ids, norm_gain, router.transpose(0, 2, 1)),
        [ids_v, ids_v, pltpu.VMEM(router.shape[:0:-1], router.dtype), pltpu.SemaphoreType.DMA((4,))],
    )
    layer = (arriving, gain, column, w_gate[0], w_up[0], w_down[0])
    received = exchanged(sent)
    kept, passed = local_call(
        functools.partial(first_kernel, parts),
        (half, half),
        (received, relaying, *layer),
        (),
        [x_v],
    )
    sending, entering = local_call(
        functools.partial(turn_plan_kernel, parts, slot_cap),
        (map_v, pltpu.VMEM((span, width), jnp.bfloat16)),
        (kept, aside, lax.ppermute(aside, "expert", sibling)),
    )
    passed = lax.ppermute(passed, "expert", sibling)
    (merged,) = local_call(merge_kernel, (numbered,), (kept, passed))
    relayed = tuple(
        lax.ppermute(x, ("pipe", "expert"), relay_pairs(chips - 1 - j, pipe, experts))
        for j, x in enumerate(merged)
    )
    relayed = relayed[chips // 2 :] + relayed[: chips // 2]
    (sent,) = local_call(
        functools.partial(turn_kernel, parts, slot_cap, pipe), (blocks,), (relayed, sending, entering)
    )
    (done,) = local_call(
        functools.partial(later_kernel, parts),
        (blocks,),
        (exchanged(sent), closing, *layer),
        (),
        [x_v],
    )
    result = jax.ShapeDtypeStruct((rows, features), jnp.bfloat16)
    up_done, down_done = local_call(unpack_kernel, (result, result), (exchanged(done), back))
    return (up_done[None], down_done[None])


def shards(*args):
    rows, features = args[0].shape[1:]
    experts = lax.axis_size("expert")
    slot_cap = rows * TOP // EXPERTS
    fits = experts == EXPERTS and rows % SUBLANES == 0 and SUBLANES % (2 * slot_cap) == 0
    fits = fits and TICKS == 2 and lax.axis_size("pipe") > 1
    fits = fits and features % (SUBLANES // (2 * slot_cap) * LANES) == 0
    return single_shards(*args) if fits else grouped_shards(*args)


def solution(mesh):
    return jax.shard_map(
        shards,
        mesh=mesh,
        in_specs=(
            P("pipe", "expert", None),
            P("pipe", "expert", None),
            P("expert", None),
            P("expert", None),
            P(None, "pipe", "expert", None),
            P(None, "pipe", "expert", None),
            P("pipe", None),
            P("pipe", None, None),
            P("pipe", None, "expert"),
            P("pipe", None, "expert"),
            P("pipe", "expert", None),
        ),
        out_specs=(P("pipe", "expert", None), P("pipe", "expert", None)),
        check_vma=False,
    )
```

```python
import functools

import jax
import jax.numpy as jnp
from jax import lax
from jax.experimental import pallas as pl
from jax.experimental.pallas import tpu as pltpu
from jax.sharding import PartitionSpec as P

TOP = 1
TICKS = 2
EXPERTS = 8
LANES = 128
SUBLANES = 16


norm_eps = 1e-06


def shifted(value, axis, by):
    length = lax.axis_size(axis)
    pairs = [(i, i + by) for i in range(length) if 0 <= i + by < length]
    return lax.ppermute(value, axis, pairs)


def normalize(token_rows, gain_row):
    widened = token_rows.astype(jnp.float32)
    inverse = lax.rsqrt(jnp.mean(widened * widened, axis=1, keepdims=True) + norm_eps)
    return (widened * inverse * gain_row).astype(jnp.bfloat16)


def routing_tables(normed, routing, router_cols, expert_count, slot_cap):
    logits = jnp.dot(normed, router_cols, preferred_element_type=jnp.float32)
    affinity = jax.nn.sigmoid(logits)
    weights = jnp.take_along_axis(affinity, routing, axis=1)
    flat_ids = routing.reshape(-1)
    onehot = (flat_ids[:, None] == jnp.arange(expert_count, dtype=jnp.int32)[None, :]).astype(
        jnp.int32
    )
    before = jnp.cumsum(onehot, axis=0) - onehot
    slot_ids = jnp.sum(before * onehot, axis=1).reshape(routing.shape)
    expert_hit = (
        routing[:, :, None] == jnp.arange(expert_count, dtype=jnp.int32)[None, None, :]
    ).astype(jnp.float32)
    slot_hit = (
        slot_ids[:, :, None] == jnp.arange(slot_cap, dtype=jnp.int32)[None, None, :]
    ).astype(jnp.float32)
    scatter_map = jnp.einsum("rke,rkc->ecr", expert_hit, slot_hit).astype(jnp.bfloat16)
    flat_slot = routing * slot_cap + slot_ids
    return (scatter_map, weights, flat_slot)


def run_experts(received, gate_cols, up_cols, down_rows):
    sources, slot_count, features = received.shape
    flat_rows = received.reshape(sources * slot_count, features)
    gate_pre = jnp.dot(flat_rows, gate_cols, preferred_element_type=jnp.float32)
    up_pre = jnp.dot(flat_rows, up_cols, preferred_element_type=jnp.float32)
    hidden = (jax.nn.silu(gate_pre) * up_pre).astype(jnp.bfloat16)
    partial_value = jnp.dot(hidden, down_rows, preferred_element_type=jnp.float32).astype(
        jnp.bfloat16
    )
    partial_value = partial_value.reshape(sources, slot_count, features)
    return lax.all_to_all(partial_value, "expert", split_axis=0, concat_axis=0, tiled=True)


def mix_rows(token_rows, weights, flat_slot, outputs):
    picked = outputs[flat_slot]
    return token_rows.astype(jnp.float32) + jnp.sum(weights[:, :, None] * picked, axis=1)


def grouped_shards(
    up_state,
    down_state,
    entering_up,
    entering_down,
    up_route,
    down_route,
    norm_gain,
    router,
    w_gate,
    w_up,
    w_down,
):
    gate_cols = w_gate[0]
    up_cols = w_up[0]
    down_rows = w_down[0]
    gain_row = norm_gain[0]
    router_cols = router[0]
    group_size = max(1, lax.axis_size("expert") // EXPERTS)
    expert_count = lax.axis_size("expert") // group_size
    segment_id = lax.axis_index("pipe")
    last_segment = lax.axis_size("pipe") - 1
    up_now = up_state[0]
    down_now = down_state[0]
    features = up_now.shape[1]
    slot_cap = up_now.shape[0] * TOP // expert_count
    up_done = up_now
    down_done = down_now
    for tick_id in range(TICKS):
        up_normed = normalize(up_now, gain_row)
        down_normed = normalize(down_now, gain_row)
        up_scatter, up_weights, up_slot = routing_tables(
            up_normed, up_route[tick_id, 0], router_cols, expert_count, slot_cap
        )
        down_scatter, down_weights, down_slot = routing_tables(
            down_normed, down_route[tick_id, 0], router_cols, expert_count, slot_cap
        )
        up_send = jnp.einsum(
            "ecr,rd->ecd", up_scatter, up_normed, preferred_element_type=jnp.float32
        ).astype(jnp.bfloat16)
        down_send = jnp.einsum(
            "ecr,rd->ecd", down_scatter, down_normed, preferred_element_type=jnp.float32
        ).astype(jnp.bfloat16)
        outbound = jnp.concatenate([up_send, down_send], axis=1)
        outgoing = jnp.broadcast_to(
            outbound[:, None], (expert_count, group_size, 2 * slot_cap, features)
        ).reshape(expert_count * group_size, 2 * slot_cap, features)
        returned = run_experts(
            lax.all_to_all(outgoing, "expert", split_axis=0, concat_axis=0, tiled=True),
            gate_cols,
            up_cols,
            down_rows,
        )
        summed = jnp.sum(
            returned.reshape(expert_count, group_size, 2 * slot_cap, features).astype(jnp.float32),
            axis=1,
        )
        up_outputs = summed[:, :slot_cap].reshape(expert_count * slot_cap, features)
        down_outputs = summed[:, slot_cap:].reshape(expert_count * slot_cap, features)
        up_done = mix_rows(up_now, up_weights, up_slot, up_outputs).astype(jnp.bfloat16)
        down_done = mix_rows(down_now, down_weights, down_slot, down_outputs).astype(jnp.bfloat16)
        if tick_id + 1 < TICKS:
            up_moved = shifted(up_done, "pipe", 1)
            down_moved = shifted(down_done, "pipe", -1)
            up_now = jnp.where(segment_id == 0, entering_up, up_moved)
            down_now = jnp.where(segment_id == last_segment, entering_down, down_moved)
    return (up_done[None], down_done[None])


def iota(shape, axis):
    return lax.broadcasted_iota(jnp.int32, shape, axis)


def chip_and_core():
    index = lax.axis_index("expert")
    return index // 2, index % 2


def one_hot(rows, target):
    return jnp.where(iota((rows, target.shape[1]), 0) == target, 1.0, 0.0)


def upright(ids):
    rows = ids.shape[1]
    diagonal = iota((rows, rows), 0) == iota((rows, rows), 1)
    return jnp.sum(jnp.where(diagonal, ids, 0), axis=1, keepdims=True)


def slots(first_ids, second_ids, parts):
    rows = first_ids.shape[1]
    width = 2 * rows * parts
    lane = iota((rows, width), 1)
    row = iota((rows, width), 0)
    own = lane % rows
    ids = jnp.where(lane // rows % 2 == 0, upright(first_ids), upright(second_ids))
    chosen = jnp.sum(jnp.where(row == own, ids, 0), axis=0, keepdims=True)
    rank = jnp.sum(jnp.where((ids == chosen) & (row < own), 1, 0), axis=0, keepdims=True)
    lane = iota((1, width), 1)
    return chosen, rank, lane // (2 * rows), lane // rows % 2


def sending_map(first_ids, second_ids, parts, slot_cap, span):
    chosen, rank, piece, group = slots(first_ids, second_ids, parts)
    chip, _ = chip_and_core()
    array = (chosen // 2) ^ chip ^ (span // (2 * SUBLANES) - 1)
    within = piece * (2 * slot_cap) + group * slot_cap + rank
    return one_hot(span, (array * 2 + chosen % 2) * SUBLANES + within)


def returning_map(up_ids, down_ids, parts, slot_cap, span):
    chosen, rank, piece, group = slots(up_ids, down_ids, parts)
    chip, core = chip_and_core()
    chips = span // (2 * SUBLANES)
    array = (chosen // 2) ^ chip ^ (chips - 1)
    array = array + jnp.where(chosen % 2 == core, 0, chips)
    within = piece * (2 * slot_cap) + (1 - group) * slot_cap + rank
    return one_hot(2 * span, (array * 2 + core) * SUBLANES + within)


def arriving_map(parts, slot_cap, span):
    wide = 2 * slot_cap
    _, core = chip_and_core()
    lane = iota((1, 2 * span), 1)
    array, to_core, within = lane // (2 * SUBLANES), lane // SUBLANES % 2, lane % SUBLANES
    row = within // wide * (span // parts) + array * wide + within % wide
    return one_hot(span, jnp.where(to_core == core, row, -1))


def relaying_map(parts, slot_cap, span):
    wide = 2 * slot_cap
    chips = span // (2 * SUBLANES)
    _, core = chip_and_core()
    lane = iota((1, span), 1)
    half = lane // (span // 2)
    array, within = lane % (span // 2) // SUBLANES, lane % SUBLANES
    piece, row = within // wide, within % wide
    array = array + jnp.where(row // slot_cap == core, 0, chips)
    way = (half + core) % 2
    row = way * slot_cap + row % slot_cap
    return one_hot(span, piece * (span // parts) + array * wide + row)


def closing_map(parts, slot_cap, span):
    wide = 2 * slot_cap
    chips = span // (2 * SUBLANES)
    _, core = chip_and_core()
    lane = iota((1, span), 1)
    array, to_core, within = lane // (2 * SUBLANES), lane // SUBLANES % 2, lane % SUBLANES
    piece, row = within // wide, within % wide
    array = array + jnp.where(row // slot_cap == core, 0, chips)
    row = to_core * slot_cap + row % slot_cap
    return one_hot(span, piece * (span // parts) + array * wide + row)


def moved(onehot, rows):
    return jnp.dot(
        onehot.astype(jnp.bfloat16), rows, preferred_element_type=jnp.float32
    ).astype(jnp.bfloat16)


def stacked(refs):
    return jnp.concatenate([ref[...] for ref in refs], axis=0)


def put(value, refs):
    rows = refs[0].shape[0]
    for i, ref in enumerate(refs):
        ref[...] = value[i * rows : (i + 1) * rows]


def pack_rows(onehot, up_rows, down_rows, parts):
    width = up_rows.shape[1] // parts
    pieces = []
    for q in range(parts):
        pieces += [up_rows[:, q * width : (q + 1) * width], down_rows[:, q * width : (q + 1) * width]]
    return moved(onehot, jnp.concatenate(pieces, axis=0))


def started(sources, targets, sems, first=0):
    copies = [
        pltpu.make_async_copy(source, target, sems.at[first + i])
        for i, (source, target) in enumerate(zip(sources, targets))
    ]
    for copy in copies:
        copy.start()
    return copies


def send_kernel(
    parts,
    slot_cap,
    up,
    down,
    up_ids,
    down_ids,
    enter_up,
    enter_down,
    w_gate,
    w_up,
    w_down,
    out_refs,
    aside_ref,
    up_v,
    down_v,
    up_i,
    down_i,
    enter_up_v,
    enter_down_v,
    sems,
):
    del w_gate, w_up, w_down
    sources = (up_ids, down_ids, up.at[0], down.at[0], enter_up, enter_down)
    copies = started(sources, (up_i, down_i, up_v, down_v, enter_up_v, enter_down_v), sems)
    copies[0].wait()
    copies[1].wait()
    span = sum(ref.shape[0] for ref in out_refs)
    rows, features = up_v.shape
    width = features // parts
    sending = sending_map(up_i[0, 0], down_i[0, 0], parts, slot_cap, span)
    last = up_i.shape[0] - 1
    square = jnp.where(iota((rows, LANES), 0) == iota((rows, LANES), 1), 1, 0)
    up_line = jnp.sum(square * upright(up_i[last, 0]), axis=0, keepdims=True)
    down_line = jnp.sum(square * upright(down_i[last, 0]), axis=0, keepdims=True)
    row = iota((rows, LANES), 0)
    lines = jnp.where(row == 0, up_line, jnp.where(row == 1, down_line, 0))
    aside_ref[parts * rows :, :LANES] = lines.astype(jnp.float32).astype(jnp.bfloat16)
    numbers = (iota((span, LANES), 0) % rows).astype(jnp.float32).astype(jnp.bfloat16)
    put(moved(sending, numbers), [ref.at[:, width:] for ref in out_refs])
    copies[2].wait()
    copies[3].wait()
    packed = pack_rows(sending, up_v[...], down_v[...], parts)
    put(packed, [ref.at[:, :width] for ref in out_refs])
    copies[4].wait()
    copies[5].wait()
    for q in range(parts):
        cols = slice(q * width, (q + 1) * width)
        entering = jnp.where(lax.axis_index("pipe") == 0, enter_up_v[:, cols], enter_down_v[:, cols])
        aside_ref[q * rows : (q + 1) * rows, :width] = entering


def plan_kernel(
    parts,
    slot_cap,
    after_ref,
    up_ids,
    down_ids,
    gain,
    router,
    back_ref,
    arriving_ref,
    relaying_ref,
    closing_ref,
    gain_v,
    router_v,
    up_i,
    down_i,
    cols_v,
    sems,
):
    del after_ref
    last = up_ids.shape[0] - 1
    sources = (up_ids.at[last, 0], down_ids.at[last, 0], router.at[0], gain)
    copies = started(sources, (up_i, down_i, cols_v, gain_v), sems)
    span = back_ref.shape[0]
    arriving_ref[...] = arriving_map(parts, slot_cap, span).astype(jnp.bfloat16)
    relaying_ref[...] = relaying_map(parts, slot_cap, span).T.astype(jnp.bfloat16)
    closing_ref[...] = closing_map(parts, slot_cap, span).T.astype(jnp.bfloat16)
    copies[0].wait()
    copies[1].wait()
    back_ref[...] = returning_map(up_i[...], down_i[...], parts, slot_cap, span).T.astype(jnp.bfloat16)
    copies[2].wait()
    cols = cols_v[...].astype(jnp.float32)
    mine = iota(cols.shape, 0) == lax.axis_index("expert")
    router_v[...] = jnp.sum(jnp.where(mine, cols, 0.0), axis=0, keepdims=True)
    copies[3].wait()


def merge_kernel(kept_ref, passed_ref, out_refs):
    for j, ref in enumerate(out_refs):
        ref[:SUBLANES] = kept_ref[j * SUBLANES : (j + 1) * SUBLANES]
        ref[SUBLANES:] = passed_ref[j * SUBLANES : (j + 1) * SUBLANES]


def turn_plan_kernel(parts, slot_cap, after_ref, own_ref, other_ref, sending_ref, entering_ref):
    del after_ref
    _, core = chip_and_core()
    span, width = entering_ref.shape
    rows = span // (2 * parts)
    own, other = own_ref[...], other_ref[...]
    first = jnp.where(core == 0, own, other)
    second = jnp.where(core == 0, other, own)
    picked = iota((rows, LANES), 0) == 1 - core

    def ids(aside):
        lines = jnp.where(picked, aside[parts * rows :, :LANES].astype(jnp.float32), 0.0)
        return jnp.sum(lines, axis=0, keepdims=True)[:, :rows].astype(jnp.int32)

    sending = sending_map(ids(first), ids(second), parts, slot_cap, span)
    sending_ref[...] = sending.astype(jnp.bfloat16)
    pieces = []
    for q in range(parts):
        pieces += [x[q * rows : (q + 1) * rows, :width] for x in (first, second)]
    entering_ref[...] = moved(sending, jnp.concatenate(pieces, axis=0))


def turn_kernel(parts, slot_cap, pipe, in_refs, sending_ref, entering_ref, out_refs):
    section = lax.axis_index("pipe")
    _, core = chip_and_core()
    wide = 2 * slot_cap
    span, width = entering_ref.shape
    rows = span // (2 * parts)
    received = stacked(in_refs)
    numbers = received[:, width:].astype(jnp.float32).astype(jnp.int32)[:, :span]
    sublane = iota((span, span), 0)
    within = sublane % SUBLANES
    place = within // wide * (2 * rows) + within % wide // slot_cap * rows
    sorting = jnp.where(iota((span, span), 1) == place + numbers, 1.0, 0.0).astype(jnp.bfloat16)
    across = (((1,), (1,)), ((), ()))
    sending = lax.dot_general(sending_ref[...], sorting, across, preferred_element_type=jnp.float32)
    enters = section == jnp.where(core == 0, pipe - 1, 0)
    put(jnp.where(enters, entering_ref[...], moved(sending, received[:, :width])), out_refs)


def unpack_kernel(in_refs, back_ref, up_ref, down_ref):
    rows = up_ref.shape[0]
    width = in_refs[0].shape[1]
    back = moved(back_ref[...], stacked(in_refs))
    for q in range(up_ref.shape[1] // width):
        up_ref[:, q * width : (q + 1) * width] = back[2 * q * rows : (2 * q + 1) * rows]
        down_ref[:, q * width : (q + 1) * width] = back[(2 * q + 1) * rows : (2 * q + 2) * rows]


MXU_ROWS = 128


def product(left, weight):
    rows = left.shape[0]
    spare = jnp.zeros((max(0, MXU_ROWS - rows), left.shape[1]), left.dtype)
    left = jnp.concatenate([left, spare], axis=0)
    return jnp.dot(left, weight, preferred_element_type=jnp.float32)[:rows]


def expert_rows(parts, in_refs, arriving_ref, gain_ref, router_ref, gate_ref, up_ref, down_ref, x_ref):
    rows = x_ref.shape[0]
    width = x_ref.shape[1] // parts
    spread = moved(arriving_ref[...], stacked(in_refs))
    for q in range(parts):
        x_ref[:, q * width : (q + 1) * width] = spread[q * rows : (q + 1) * rows, :width]
    widened = x_ref[...].astype(jnp.float32)
    inverse = lax.rsqrt(jnp.mean(widened * widened, axis=1, keepdims=True) + norm_eps)
    normed = (widened * inverse * gain_ref[...]).astype(jnp.bfloat16)
    logit = jnp.sum(normed.astype(jnp.float32) * router_ref[...], axis=1, keepdims=True)
    weight = jax.nn.sigmoid(logit)
    gate_pre = product(normed, gate_ref[...])
    hidden = (jax.nn.silu(gate_pre) * product(normed, up_ref[...])).astype(jnp.bfloat16)
    part = product(hidden, down_ref[...]).astype(jnp.bfloat16).astype(jnp.float32)
    done = (x_ref[...].astype(jnp.float32) + weight * part).astype(jnp.bfloat16)
    done = jnp.concatenate([done[:, q * width : (q + 1) * width] for q in range(parts)], axis=0)
    return done, spread[:, width:]


def first_kernel(parts, in_refs, leaving_ref, *refs):
    *ins, kept_ref, passed_ref, x_ref = refs
    done, numbers = expert_rows(parts, in_refs, *ins, x_ref)
    put(moved(leaving_ref[...], jnp.concatenate([done, numbers], axis=1)), (kept_ref, passed_ref))


def later_kernel(parts, in_refs, leaving_ref, *refs):
    *ins, out_refs, x_ref = refs
    done, _ = expert_rows(parts, in_refs, *ins, x_ref)
    put(moved(leaving_ref[...], done), out_refs)


VMEM_SPEC = pl.BlockSpec(memory_space=pltpu.VMEM)
HBM_SPEC = pl.BlockSpec(memory_space=pltpu.HBM)


def local_call(kernel, out_shapes, near, far=(), scratch=(), order=()):
    far = [pltpu.with_memory_space_constraint(x, pltpu.HBM) for x in far]
    close, near_tree = jax.tree.flatten(tuple(near))
    order = list(order) + list(range(len(order), len(close)))
    outs, out_tree = jax.tree.flatten(out_shapes)

    def body(*refs):
        refs = iter(refs)
        take = lambda count: [next(refs) for _ in range(count)]
        fed = dict(zip(order, take(len(close))))
        args = [*near_tree.unflatten([fed[i] for i in range(len(close))]), *take(len(far))]
        results = out_tree.unflatten(take(len(outs)))
        kernel(*args, *(results if isinstance(results, tuple) else (results,)), *refs)

    results = pl.pallas_call(
        body,
        out_shape=outs,
        in_specs=[VMEM_SPEC] * len(close) + [HBM_SPEC] * len(far),
        out_specs=[VMEM_SPEC] * len(outs),
        scratch_shapes=list(scratch),
        compiler_params=pltpu.CompilerParams(vmem_limit_bytes=8 << 20),
    )(*[close[i] for i in order], *far)
    return out_tree.unflatten(results)


def exchanged(arrays):
    last = len(arrays) - 1
    devices = range(2 * len(arrays))

    def sent(value, flip):
        return lax.ppermute(value, "expert", [(i, i ^ flip) for i in devices])

    arrived = [sent(x, 2 * (last - j) + 1) for j, x in enumerate(arrays[:last])]
    passed = [sent(x, 1) for x in arrived[:-1]] + [sent(arrays[last - 1], 2)]
    return (*passed, arrays[last], *arrived, sent(arrays[last], 1))


def start_order(chips):
    last = chips - 1
    return [*range(chips, chips + last - 1), last - 1, chips + last - 1, *range(last - 1), last, chips + last]


def relay_pairs(k, pipe, experts):
    pairs = []
    for section in range(pipe):
        for i in range(experts):
            other = section + 1 - 2 * (i % 2)
            target = (other, i ^ (2 * k) ^ 1) if 0 <= other < pipe else (section, i ^ 2)
            pairs.append((section * experts + i, target[0] * experts + target[1]))
    return pairs


def single_shards(
    up_state,
    down_state,
    entering_up,
    entering_down,
    up_route,
    down_route,
    norm_gain,
    router,
    w_gate,
    w_up,
    w_down,
):
    pipe = lax.axis_size("pipe")
    experts = lax.axis_size("expert")
    rows, features = up_state.shape[1:]
    slot_cap = rows * TOP // experts
    parts = SUBLANES // (2 * slot_cap)
    span = experts * SUBLANES
    chips = experts // 2
    width = features // parts
    numbered = (pltpu.VMEM((2 * SUBLANES, width + LANES), jnp.bfloat16),) * chips
    blocks = (pltpu.VMEM((2 * SUBLANES, width), jnp.bfloat16),) * chips
    half = pltpu.VMEM((span // 2, width + LANES), jnp.bfloat16)
    batch = pltpu.VMEM((rows, features), jnp.bfloat16)
    ids_v = pltpu.VMEM((1, rows), jnp.int32)
    all_ids_v = pltpu.VMEM((TICKS, 1, 1, rows), jnp.int32)
    row_v = pltpu.VMEM((1, features), jnp.float32)
    x_v = pltpu.VMEM((span // parts, features), jnp.bfloat16)
    map_v = pltpu.VMEM((span, span), jnp.bfloat16)
    wide_map_v = pltpu.VMEM((span, 2 * span), jnp.bfloat16)
    sibling = [(i, i ^ 1) for i in range(experts)]
    ids = (up_route.transpose(0, 1, 3, 2), down_route.transpose(0, 1, 3, 2))
    aside_v = pltpu.VMEM(((parts + 1) * rows, width), jnp.bfloat16)
    sent, aside = local_call(
        functools.partial(send_kernel, parts, slot_cap),
        (numbered, aside_v),
        (),
        (up_state, down_state, *ids, entering_up, entering_down, w_gate, w_up, w_down),
        [batch, batch, all_ids_v, all_ids_v, batch, batch, pltpu.SemaphoreType.DMA((6,))],
    )
    back, arriving, relaying, closing, gain, column = local_call(
        functools.partial(plan_kernel, parts, slot_cap),
        (wide_map_v, wide_map_v, map_v, map_v, row_v, row_v),
        (sent[-1],),
        (*ids, norm_gain, router.transpose(0, 2, 1)),
        [ids_v, ids_v, pltpu.VMEM(router.shape[:0:-1], router.dtype), pltpu.SemaphoreType.DMA((4,))],
    )
    layer = (arriving, gain, column, w_gate[0], w_up[0], w_down[0])
    received = exchanged(sent)
    kept, passed = local_call(
        functools.partial(first_kernel, parts),
        (half, half),
        (received, relaying, *layer),
        (),
        [x_v],
        order=start_order(chips),
    )
    sending, entering = local_call(
        functools.partial(turn_plan_kernel, parts, slot_cap),
        (map_v, pltpu.VMEM((span, width), jnp.bfloat16)),
        (kept, aside, lax.ppermute(aside, "expert", sibling)),
    )
    passed = lax.ppermute(passed, "expert", sibling)
    (merged,) = local_call(merge_kernel, (numbered,), (kept, passed))
    relayed = tuple(
        lax.ppermute(x, ("pipe", "expert"), relay_pairs(chips - 1 - j, pipe, experts))
        for j, x in enumerate(merged)
    )
    relayed = relayed[chips // 2 :] + relayed[: chips // 2]
    (sent,) = local_call(
        functools.partial(turn_kernel, parts, slot_cap, pipe), (blocks,), (relayed, sending, entering)
    )
    (done,) = local_call(
        functools.partial(later_kernel, parts),
        (blocks,),
        (exchanged(sent), closing, *layer),
        (),
        [x_v],
        order=start_order(chips),
    )
    result = jax.ShapeDtypeStruct((rows, features), jnp.bfloat16)
    up_done, down_done = local_call(unpack_kernel, (result, result), (exchanged(done), back), order=start_order(chips))
    return (up_done[None], down_done[None])


def shards(*args):
    rows, features = args[0].shape[1:]
    experts = lax.axis_size("expert")
    slot_cap = rows * TOP // EXPERTS
    fits = experts == EXPERTS and rows % SUBLANES == 0 and SUBLANES % (2 * slot_cap) == 0
    fits = fits and TICKS == 2 and lax.axis_size("pipe") > 1
    fits = fits and features % (SUBLANES // (2 * slot_cap) * LANES) == 0
    return single_shards(*args) if fits else grouped_shards(*args)


def solution(mesh):
    return jax.shard_map(
        shards,
        mesh=mesh,
        in_specs=(
            P("pipe", "expert", None),
            P("pipe", "expert", None),
            P("expert", None),
            P("expert", None),
            P(None, "pipe", "expert", None),
            P(None, "pipe", "expert", None),
            P("pipe", None),
            P("pipe", None, None),
            P("pipe", None, "expert"),
            P("pipe", None, "expert"),
            P("pipe", "expert", None),
        ),
        out_specs=(P("pipe", "expert", None), P("pipe", "expert", None)),
        check_vma=False,
    )
```
